128 devices in a mesh: tok: 32 (over z, x, core), blk: 4 (over y).
Axes of the slice: x: 4, y: 4, z: 4, core: 2. Of those that a mesh axis runs over, the one named last changes fastest.
Arguments:
- resid: bfloat16 [16384, 8192], P('tok', 'blk'), may hold values from -2500 to 2500
- norm_gain: float32 [8192], P('blk'), may hold values from 0.25 to 1.75
- keep_index: int32 [8192], P('tok'), may hold values from 0 to 511, as said below
- counts: int32 [64], P('tok'), may hold values from 0 to 128, as said below
Outputs:
- feature_mean: float32 [8192], P('blk')
- gram_factor: float32 [8192, 8192], P('tok', 'blk')
The draws below stay inside these ranges and needn't reach their ends.
Inputs may be any that keep to these rules, and one draw needn't show every extreme that they name: `keep_index`: the 256 entries of one index of tok are distinct row numbers among that index's 512 tokens. `counts`: the live slots of a block are its first ones, and within one index of tok each block is full before the next block has a live slot; exactly half of the 8192 slots are live; some index of tok has all its 256 slots live.
All inputs are finite; a program needn't handle non-finite values.
Results may differ from the reference program's by a relative error of at most 0.007.
Values may be sent and summed in bfloat16 or wider, within the bound.
No kernel may reach another device: no remote copies, remote signals or barrier semaphores. Data moves between devices by JAX's collectives and lax.ppermute only.
A program may use at most 192 MiB of HBM per device.

```python
import math
import jax
import jax.numpy as jnp
from jax import lax

D = 8192
TOK_DEV = 512
BLOCK = 128
KBLK = 2
KEEP_DEV = 256
KEPT = 8192
TOKENS = 16384


def draw_resid(key, part):
    key = jax.random.fold_in(key, 11)
    key_list = jax.random.split(key, 5)
    position = jnp.arange(D, dtype=jnp.float32)[None, :] / float(D - 1)
    offset = jax.random.uniform(key_list[1], (1, D), jnp.float32, -1.5, 1.5)
    rising = jnp.exp(position * (0.5 * math.log(10.0)))
    col_scale = rising * jnp.exp(jax.random.uniform(key_list[0], (1, D), jnp.float32, 0.0, math.log(4.0)))
    noise_part = jnp.clip(jax.random.normal(key_list[2], (TOKENS, D), jnp.float32), -5.0, 5.0)
    row_scale = jnp.exp(jax.random.uniform(key_list[4], (TOKENS, 1), jnp.float32, 0.0, math.log(10.0)))
    values = row_scale * col_scale * (offset + noise_part)
    return values.astype(jnp.bfloat16)


def draw_keep_index(key, part):
    key = jax.random.fold_in(key, 23)
    devices = KEPT // KEEP_DEV
    key_list = jax.random.split(key, devices)
    index_lists = jax.vmap(lambda subkey: jax.random.permutation(subkey, TOK_DEV)[:KEEP_DEV])(key_list)
    return index_lists.reshape(-1).astype(jnp.int32)


def draw_counts(key, part):
    key = jax.random.fold_in(key, 37)
    devices = KEPT // KEEP_DEV
    key_list = jax.random.split(key, 3)
    pair_count = (devices - 4) // 2
    paired_low = jax.random.randint(key_list[0], (pair_count,), KEEP_DEV // 8, KEEP_DEV - KEEP_DEV // 8 + 1, dtype=jnp.int32)
    small_loads = jax.random.randint(key_list[1], (2,), KEEP_DEV // 4, 3 * KEEP_DEV // 8 + 1, dtype=jnp.int32)
    third_load = (KEEP_DEV - jnp.sum(small_loads)).astype(jnp.int32)
    device_loads = jnp.concatenate([jnp.full((1,), KEEP_DEV, jnp.int32), small_loads, third_load[None], paired_low, (KEEP_DEV - paired_low).astype(jnp.int32)]).astype(jnp.int32)
    order = jax.random.permutation(key_list[2], devices)
    device_loads = device_loads[order]
    block_first = jnp.arange(KBLK, dtype=jnp.int32) * BLOCK
    block_counts = jnp.clip(device_loads[:, None] - block_first[None, :], 0, BLOCK)
    return block_counts.reshape(-1).astype(jnp.int32)


def setup_inputs(seed: int = 0) -> dict:
    splits = jax.random.split(jax.random.key(seed), 5)
    return {
        "resid": draw_resid(jax.random.fold_in(splits[4], 71), 0),
        "norm_gain": jnp.clip(1.0 + 0.15 * jax.random.normal(splits[1], (D,), jnp.float32), 0.25, 1.75),
        "keep_index": draw_keep_index(jax.random.fold_in(splits[4], 71), 0),
        "counts": draw_counts(jax.random.fold_in(splits[4], 71), 0),
    }


epsilon = 1e-05

def reference(resid, norm_gain, keep_index, counts):
    devices = KEPT // KEEP_DEV
    offsets = (jnp.arange(devices, dtype=jnp.int32) * TOK_DEV)[:, None]
    row_ids = (keep_index.reshape(devices, KEEP_DEV) + offsets).reshape(-1).astype(jnp.int32)
    picked = resid[row_ids].astype(jnp.float32)
    live_slot = jnp.arange(KEPT, dtype=jnp.int32) % BLOCK < jnp.repeat(counts, BLOCK, total_repeat_length=KEPT)
    squares = lax.optimization_barrier(jnp.mean(picked * picked, axis=1, keepdims=True))
    normed = jnp.where(live_slot[:, None], picked * lax.rsqrt(squares + epsilon) * norm_gain[None, :], 0.0).astype(jnp.bfloat16)
    kept_total = jnp.sum(counts).astype(jnp.float32)
    col_sum = jnp.dot(jnp.ones((1, KEPT), jnp.bfloat16), normed, preferred_element_type=jnp.float32)[0]
    feature_mean = col_sum / kept_total
    gram_sum = jnp.dot(normed.T, normed, preferred_element_type=jnp.float32)
    upper_part = jnp.arange(D, dtype=jnp.int32)[:, None] <= jnp.arange(D, dtype=jnp.int32)[None, :]
    gram_factor = jnp.where(upper_part, gram_sum / kept_total, 0.0)
    return (feature_mean, gram_factor)
```

```python
import jax
import jax.numpy as jnp
from jax import lax
from jax.experimental import pallas as pl
from jax.experimental.pallas import tpu as pltpu
from jax.sharding import Mesh, PartitionSpec as P

epsilon = 1e-05
TOK = ("z", "x", "c")
SLOTS = 256
LIVE = 4096
WIDTH = 2048
PIECE = 64
VMEM = 60 * 1024 * 1024
bf16 = jnp.bfloat16
f32 = jnp.float32


def params(**kw):
    return pltpu.CompilerParams(vmem_limit_bytes=VMEM, **kw)


def pick_kernel(index_ref, counts_ref, resid_ref, picked_ref, sums_ref):
    tokens = resid_ref.shape[0]
    token = lax.broadcasted_iota(jnp.int32, (tokens, SLOTS), 0)
    slot = lax.broadcasted_iota(jnp.int32, (1, SLOTS), 1)
    half = SLOTS // 2
    end = jnp.where(slot < half, counts_ref[0], half + counts_ref[1])
    kept = jnp.where(slot < end, index_ref[...], -1)
    one_hot = jnp.where(token == kept, 1.0, 0.0).astype(bf16)
    total = jnp.zeros((1, SLOTS), f32)
    step = 512
    for k in range(WIDTH // step):
        part = lax.dot_general(
            resid_ref[:, k * step : (k + 1) * step],
            one_hot,
            (((0,), (0,)), ((), ())),
            preferred_element_type=f32,
        )
        picked_ref[k * step : (k + 1) * step, :] = part.astype(bf16)
        total += jnp.sum(part * part, axis=0, keepdims=True)
    sums_ref[...] = jnp.broadcast_to(total, sums_ref.shape)


def pick(resid, keep_index, counts):
    return pl.pallas_call(
        pick_kernel,
        out_shape=(
            jax.ShapeDtypeStruct((WIDTH, SLOTS), bf16),
            jax.ShapeDtypeStruct((8, SLOTS), f32),
        ),
        in_specs=[
            pl.BlockSpec(memory_space=pltpu.VMEM),
            pl.BlockSpec(memory_space=pltpu.SMEM),
            pl.BlockSpec(memory_space=pltpu.VMEM),
        ],
        out_specs=(pl.BlockSpec(memory_space=pltpu.VMEM),) * 2,
        compiler_params=params(),
        name="pick",
    )(keep_index[None, :], counts, resid)


def norm_kernel(picked_ref, scale_ref, gain_ref, out_ref):
    scale = scale_ref[0:1, :]
    for x in range(4):
        for c in range(2):
            for z in range(4):
                first = ((x * 2 + c) * 4 + z) * PIECE
                rows = picked_ref[first : first + PIECE, :].astype(f32)
                gain = gain_ref[first : first + PIECE, :]
                out_ref[z * 8 + x * 2 + c] = (rows * scale * gain).astype(bf16)


def norm(picked, scale, gain):
    return pl.pallas_call(
        norm_kernel,
        out_shape=jax.ShapeDtypeStruct((32, PIECE, SLOTS), bf16),
        compiler_params=params(),
        name="norm",
    )(picked, scale, gain)


def pack_kernel(first_ref, in_ref, out_ref, acc_ref):
    acc_ref[...] = jnp.zeros_like(acc_ref)

    def body(t, _):
        first = first_ref[t]
        base = pl.multiple_of((first // 128) * 128, 128)
        wide = jnp.concatenate([in_ref[t].astype(f32), jnp.zeros((PIECE, 128), f32)], axis=1)
        moved = pltpu.roll(wide, first - base, 1)
        acc_ref[:, pl.ds(base, SLOTS + 128)] += moved
        return 0

    lax.fori_loop(0, 32, body, 0)
    out_ref[...] = acc_ref[:, :LIVE].astype(bf16)


def pack(first, pieces):
    return pl.pallas_call(
        pack_kernel,
        out_shape=jax.ShapeDtypeStruct((PIECE, LIVE), bf16),
        in_specs=[pl.BlockSpec(memory_space=pltpu.SMEM), pl.BlockSpec(memory_space=pltpu.VMEM)],
        out_specs=pl.BlockSpec(memory_space=pltpu.VMEM),
        scratch_shapes=[pltpu.VMEM((PIECE, LIVE + SLOTS + 128), f32)],
        compiler_params=params(),
        name="pack",
    )(first, pieces)


def gram_kernel(place, n_arrays, *refs):
    where_ref = refs[0]
    arrays = refs[1 : 1 + n_arrays]
    out_ref, sum_ref, rows, cols, sem = refs[1 + n_arrays :]
    copies = []
    for k, (kind, index, start, height) in enumerate(place):
        target = rows if kind == "r" else cols
        first = pl.multiple_of(where_ref[k], 32)
        source = arrays[index].at[pl.ds(start, height)]
        copies.append(pltpu.make_async_copy(source, target.at[pl.ds(first, height)], sem.at[k]))
    for copy in copies:
        copy.start()
    for copy in copies:
        copy.wait()
    step = 256

    def body(n, _):
        at = pl.multiple_of(n * step, step)
        block = cols[pl.ds(at, step), :]
        out_ref[:, pl.ds(at, step)] = lax.dot_general(
            rows[...], block, (((1,), (1,)), ((), ())), preferred_element_type=f32
        )
        sum_ref[:, pl.ds(at, step)] = lax.dot_general(
            jnp.ones((8, LIVE), bf16), block, (((1,), (1,)), ((), ())), preferred_element_type=f32
        )
        return 0

    lax.fori_loop(0, cols.shape[0] // step, body, 0)


def gram(where, arrays, place):
    n_rows, n_cols = 512, 1024
    return pl.pallas_call(
        lambda *refs: gram_kernel(place, len(arrays), *refs),
        out_shape=(
            jax.ShapeDtypeStruct((n_rows, n_cols), f32),
            jax.ShapeDtypeStruct((8, n_cols), f32),
        ),
        in_specs=[pl.BlockSpec(memory_space=pltpu.SMEM)]
        + [pl.BlockSpec(memory_space=pl.ANY)] * len(arrays),
        out_specs=(pl.BlockSpec(memory_space=pltpu.VMEM),) * 2,
        scratch_shapes=[
            pltpu.VMEM((n_rows, LIVE), bf16),
            pltpu.VMEM((n_cols, LIVE), bf16),
            pltpu.SemaphoreType.DMA((len(place),)),
        ],
        compiler_params=params(),
        cost_estimate=pl.CostEstimate(
            flops=2 * n_rows * n_cols * LIVE, bytes_accessed=14 * 1024 * 1024, transcendentals=0
        ),
        name="gram",
    )(where, *arrays)


def shift(value, axis, by):
    return lax.ppermute(value, axis, [((i + by) % 4, i) for i in range(4)])


def swap(value):
    return lax.ppermute(value, "c", [(0, 1), (1, 0)])


def per_device(resid, norm_gain, keep_index, counts):
    z, x, c, y = (lax.axis_index(a) for a in ("z", "x", "c", "y"))
    all_counts = lax.all_gather(counts, TOK, axis=0, tiled=True)
    loads = jnp.sum(all_counts.reshape(32, 2), axis=1)
    first = jnp.cumsum(loads) - loads
    kept_total = jnp.sum(loads).astype(f32)

    picked, sums = pick(resid, keep_index, counts)
    scale = lax.rsqrt(lax.psum(sums, "y") / 8192 + epsilon)
    normed = norm(picked, scale, norm_gain[:, None])
    pieces = lax.all_to_all(normed, TOK, 0, 0, tiled=True)
    mine = pack(first, pieces)

    half = PIECE // 2
    turned = lax.ppermute(mine, ("z", "y"), [(i * 4 + j, j * 4 + i) for i in range(4) for j in range(4)])
    a0, b0 = mine[:half], mine[half:]
    a = {d: shift(a0, "x", d) for d in (1, 3, 2)}
    b = {d: shift(b0, "z", d) for d in (1, 3, 2)}
    r = {d: shift(turned, "y", d) for d in (1, 3, 2)}
    a4 = jnp.concatenate([a0, a[1], a[3], a[2]], axis=0)
    b4 = jnp.concatenate([b0, b[1], b[3], b[2]], axis=0)
    a_up, a_down = shift(a4, "z", 1), shift(a4, "z", 3)
    b_up, b_down = shift(b4, "x", 1), shift(b4, "x", 3)
    a_far0, a_far1 = shift(a_up[: 2 * half], "z", 1), shift(a_down[2 * half :], "z", 3)
    b_far0, b_far1 = shift(b_up[: 2 * half], "x", 1), shift(b_down[2 * half :], "x", 3)

    place, arrays, where = [], [], []

    def add(kind, value, height, places):
        for k, at in enumerate(places):
            place.append((kind, len(arrays), k * height, height))
            where.append(at)
        arrays.append(value)

    order = (0, 1, 3, 2)
    rows = jnp.concatenate([turned, r[1], r[3], r[2]], axis=0)
    other = swap(rows)
    add("r", rows, PIECE, [((y + d) % 4) * PIECE for d in order])
    add("r", other, PIECE, [256 + ((y + d) % 4) * PIECE for d in order])
    for value, dz, dxs in (
        (a4, 0, order),
        (a_up, 1, order),
        (a_down, 3, order),
        (a_far0, 2, order[:2]),
        (a_far1, 2, order[2:]),
    ):
        add("c", value, half, [((x + dx) % 4) * 256 + ((z + dz) % 4) * PIECE for dx in dxs])
    for value, dx, dzs in (
        (b4, 0, order),
        (b_up, 1, order),
        (b_down, 3, order),
        (b_far0, 2, order[:2]),
        (b_far1, 2, order[2:]),
    ):
        add("c", value, half, [((x + dx) % 4) * 256 + ((z + dz) % 4) * PIECE + half for dz in dzs])
    product, col_sum = gram(jnp.stack(where).astype(jnp.int32), arrays, tuple(place))

    own = jnp.concatenate([product[:256], col_sum], axis=0)
    given = jnp.concatenate([product[256:], col_sum], axis=0)
    got = swap(given)
    low = jnp.where(c == 0, own, got)
    high = jnp.where(c == 0, got, own)
    n = own.shape[0]
    whole = jnp.stack([low.reshape(n, 4, 256), high.reshape(n, 4, 256)], axis=2).reshape(n, WIDTH)
    whole = whole / kept_total
    row_index = (z * 8 + x * 2 + c) * 256 + jnp.arange(256, dtype=jnp.int32)[:, None]
    col_index = y * WIDTH + jnp.arange(WIDTH, dtype=jnp.int32)[None, :]
    gram_factor = jnp.where(row_index <= col_index, whole[:256], 0.0)
    return (whole[256], gram_factor)


def solution(mesh):
    fine = Mesh(mesh.devices.reshape(4, 4, 2, 4), ("z", "x", "c", "y"))
    return jax.shard_map(
        per_device,
        mesh=fine,
        in_specs=(P(TOK, "y"), P("y"), P(TOK), P(TOK)),
        out_specs=(P("y"), P(TOK, "y")),
        check_vma=False,
    )
```

```python
import jax
import jax.numpy as jnp
from jax import lax
from jax.experimental import pallas as pl
from jax.experimental.pallas import tpu as pltpu
from jax.sharding import Mesh, PartitionSpec as P

epsilon = 1e-05
TOK = ("z", "x", "c")
SLOTS = 256
LIVE = 4096
WIDTH = 2048
PIECE = 64
EXTRA = 16
VMEM = 60 * 1024 * 1024
bf16 = jnp.bfloat16
f32 = jnp.float32


def params(**kw):
    return pltpu.CompilerParams(vmem_limit_bytes=VMEM, **kw)


def pick_kernel(index_ref, counts_ref, resid_ref, out_ref):
    tokens = resid_ref.shape[0]
    token = lax.broadcasted_iota(jnp.int32, (tokens, SLOTS), 0)
    slot = lax.broadcasted_iota(jnp.int32, (1, SLOTS), 1)
    half = SLOTS // 2
    end = jnp.where(slot < half, counts_ref[0], half + counts_ref[1])
    kept = jnp.where(slot < end, index_ref[...], -1)
    one_hot = jnp.where(token == kept, 1.0, 0.0).astype(bf16)
    total = jnp.zeros((1, SLOTS), f32)
    step = 512
    for x in range(4):
        part = lax.dot_general(
            resid_ref[:, x * step : (x + 1) * step],
            one_hot,
            (((0,), (0,)), ((), ())),
            preferred_element_type=f32,
        )
        total += jnp.sum(part * part, axis=0, keepdims=True)
        short = part.astype(bf16)
        for c in range(2):
            for z in range(4):
                first = (c * 4 + z) * PIECE
                out_ref[z * 8 + x * 2 + c, :PIECE, :] = short[first : first + PIECE, :]
    live = (counts_ref[0] + counts_ref[1]).astype(f32)
    high = total.astype(bf16).astype(f32)
    middle = (total - high).astype(bf16).astype(f32)
    low = total - high - middle
    row = lax.broadcasted_iota(jnp.int32, (EXTRA, SLOTS), 0)
    extra = jnp.where(row == 0, live, 0.0)
    for k, term in enumerate((high, middle, low)):
        extra = jnp.where(row == k + 1, term, extra)
    extra = extra.astype(bf16)
    for t in range(32):
        out_ref[t, PIECE:, :] = extra


def pick(resid, keep_index, counts):
    return pl.pallas_call(
        pick_kernel,
        out_shape=jax.ShapeDtypeStruct((32, PIECE + EXTRA, SLOTS), bf16),
        in_specs=[
            pl.BlockSpec(memory_space=pltpu.VMEM),
            pl.BlockSpec(memory_space=pltpu.SMEM),
            pl.BlockSpec(memory_space=pltpu.VMEM),
        ],
        out_specs=pl.BlockSpec(memory_space=pltpu.VMEM),
        compiler_params=params(),
        name="pick",
    )(keep_index[None, :], counts, resid)


def pack_kernel(first_ref, in_ref, scale_ref, gain_ref, out_ref, acc_ref):
    acc_ref[...] = jnp.zeros_like(acc_ref)
    gain = gain_ref[...]
    group = 4

    def body(g, _):
        moved = []
        for k in range(group):
            t = g * group + k
            rows = in_ref[t, :PIECE, :].astype(f32) * scale_ref[pl.ds(t, 1), :] * gain
            first = first_ref[t]
            base = pl.multiple_of((first // 128) * 128, 128)
            wide = jnp.concatenate([rows, jnp.zeros((PIECE, 128), f32)], axis=1)
            moved.append((base, pltpu.roll(wide, first - base, 1)))
        for base, rows in moved:
            acc_ref[:, pl.ds(base, SLOTS + 128)] += rows
        return 0

    lax.fori_loop(0, 32 // group, body, 0)
    out_ref[...] = acc_ref[:, :LIVE].astype(bf16)


def pack(first, pieces, scale, gain):
    return pl.pallas_call(
        pack_kernel,
        out_shape=jax.ShapeDtypeStruct((PIECE, LIVE), bf16),
        in_specs=[pl.BlockSpec(memory_space=pltpu.SMEM)] + [pl.BlockSpec(memory_space=pltpu.VMEM)] * 3,
        out_specs=pl.BlockSpec(memory_space=pltpu.VMEM),
        scratch_shapes=[pltpu.VMEM((PIECE, LIVE + SLOTS + 128), f32)],
        compiler_params=params(),
        name="pack",
    )(first, pieces, scale, gain)


def gram_kernel(place, n_arrays, *refs):
    where_ref, block_ref, rows_in = refs[:3]
    arrays = refs[3 : 3 + n_arrays]
    out_ref, rows, cols, row_sem, sem = refs[3 + n_arrays :]
    row_copy = pltpu.make_async_copy(rows_in, rows.at[pl.ds(0, 256)], row_sem)
    row_copy.start()
    copies = []
    for k, (index, start, height, block) in enumerate(place):
        first = pl.multiple_of(where_ref[k], 16)
        source = arrays[index].at[pl.ds(start, height)]
        copies.append(
            (block, pltpu.make_async_copy(source, cols.at[pl.ds(first, height)], sem.at[k]))
        )
    for block in range(4):
        for at, copy in copies:
            if at == block:
                copy.start()
    rows[256:, :] = jnp.ones((16, LIVE), bf16)
    row_copy.wait()
    for block in range(4):
        for at, copy in copies:
            if at == block:
                copy.wait()
        at = pl.multiple_of(block_ref[block], 256)
        out_ref[:, pl.ds(at, 256)] = lax.dot_general(
            rows[...], cols[pl.ds(at, 256), :], (((1,), (1,)), ((), ())), preferred_element_type=f32
        )


def gram(where, blocks, rows, arrays, place):
    n_rows, n_cols = 272, 1024
    return pl.pallas_call(
        lambda *refs: gram_kernel(place, len(arrays), *refs),
        out_shape=jax.ShapeDtypeStruct((n_rows, n_cols), f32),
        in_specs=[pl.BlockSpec(memory_space=pltpu.SMEM)] * 2
        + [pl.BlockSpec(memory_space=pl.ANY)] * (1 + len(arrays)),
        out_specs=pl.BlockSpec(memory_space=pltpu.VMEM),
        scratch_shapes=[
            pltpu.VMEM((n_rows, LIVE), bf16),
            pltpu.VMEM((n_cols, LIVE), bf16),
            pltpu.SemaphoreType.DMA,
            pltpu.SemaphoreType.DMA((len(place),)),
        ],
        compiler_params=params(),
        cost_estimate=pl.CostEstimate(
            flops=2 * n_rows * n_cols * LIVE, bytes_accessed=12 * 1024 * 1024, transcendentals=0
        ),
        name="gram",
    )(where, blocks, rows, *arrays)


def finish_kernel(info_ref, total_ref, own_ref, got_ref, mean_ref, out_ref):
    core, row_first, col_first = info_ref[0], info_ref[1], info_ref[2]
    total = total_ref[0]
    row = row_first + lax.broadcasted_iota(jnp.int32, (256, 256), 0)
    col = col_first + lax.broadcasted_iota(jnp.int32, (256, 256), 1)
    for k in range(8):
        x = k // 2

        def put(ref):
            values = ref[:256, x * 256 : (x + 1) * 256] / total
            out_ref[:, k * 256 : (k + 1) * 256] = jnp.where(row <= col + k * 256, values, 0.0)
            mean_ref[:, k * 256 : (k + 1) * 256] = ref[256:264, x * 256 : (x + 1) * 256] / total

        @pl.when(core == k % 2)
        def _():
            put(own_ref)

        @pl.when(core != k % 2)
        def _():
            put(got_ref)


def finish(info, total, own, got):
    return pl.pallas_call(
        finish_kernel,
        out_shape=(
            jax.ShapeDtypeStruct((8, WIDTH), f32),
            jax.ShapeDtypeStruct((256, WIDTH), f32),
        ),
        in_specs=[pl.BlockSpec(memory_space=pltpu.SMEM)] * 2 + [pl.BlockSpec(memory_space=pltpu.VMEM)] * 2,
        out_specs=(pl.BlockSpec(memory_space=pltpu.VMEM),) * 2,
        compiler_params=params(),
        name="finish",
    )(info, total, own, got)


def shift(value, axis, by):
    return lax.ppermute(value, axis, [((i + by) % 4, i) for i in range(4)])


def swap(value):
    return lax.ppermute(value, "c", [(0, 1), (1, 0)])


def per_device(resid, norm_gain, keep_index, counts):
    z, x, c, y = (lax.axis_index(a) for a in ("z", "x", "c", "y"))
    pieces = lax.all_to_all(pick(resid, keep_index, counts), TOK, 0, 0, tiled=True)

    extra = pieces[:, PIECE : PIECE + 4, :].astype(f32)
    loads = extra[:, 0, 0].astype(jnp.int32)
    first = jnp.cumsum(loads) - loads
    kept_total = jnp.sum(loads).astype(f32)
    sums = extra[:, 1, :] + extra[:, 2, :] + extra[:, 3, :]
    squares = (sums + shift(sums, "y", 2)) + (shift(sums, "y", 1) + shift(sums, "y", 3))
    scale = lax.rsqrt(squares / 8192 + epsilon)
    gain = lax.dynamic_slice_in_dim(norm_gain, ((x * 2 + c) * 4 + z) * PIECE, PIECE)[:, None]
    mine = pack(first, pieces, scale, gain)

    half = PIECE // 2
    order = (1, 3, 2)
    turned = lax.ppermute(mine, ("z", "y"), [(i * 4 + j, j * 4 + i) for i in range(4) for j in range(4)])
    from_x = {d: shift(mine, "x", d) for d in order}
    from_z = {d: shift(mine, "z", d) for d in order}
    a3 = jnp.concatenate([from_x[d][:half] for d in order], axis=0)
    b3 = jnp.concatenate([from_z[d][half:] for d in order], axis=0)
    a3, b3, turned = lax.optimization_barrier((a3, b3, turned))
    rows = lax.all_gather(turned, "y", axis=0, tiled=True)
    a_up, b_up = shift(a3, "z", 1), shift(b3, "x", 1)
    a_down, b_down = shift(a3, "z", 3), shift(b3, "x", 3)
    a_far0, a_far1 = shift(a_up[:48], "z", 1), shift(a_down[48:], "z", 3)
    b_far0, b_far1 = shift(b_up[:48], "x", 1), shift(b_down[48:], "x", 3)

    held = [(mine, [(0, 0, 0, PIECE)])]
    for d in order:
        held.append((from_x[d], [(d, 0, 0, PIECE)]))
        held.append((from_z[d], [(0, d, 0, PIECE)]))
    for d, value in ((1, a_up), (3, a_down)):
        held.append((value, [(e, d, 0, half) for e in order]))
    held.append((a_far0, [(1, 2, 0, half), (3, 2, 0, 16)]))
    held.append((a_far1, [(3, 2, 16, 16), (2, 2, 0, half)]))
    for d, value in ((1, b_up), (3, b_down)):
        held.append((value, [(d, e, half, half) for e in order]))
    held.append((b_far0, [(2, 1, half, half), (2, 3, half, 16)]))
    held.append((b_far1, [(2, 3, half + 16, 16), (2, 2, half, half)]))

    place, where = [], []
    for index, (_, parts) in enumerate(held):
        start = 0
        for dx, dz, row, height in parts:
            place.append((index, start, height, dx))
            where.append(((x + dx) % 4) * 256 + ((z + dz) % 4) * PIECE + row)
            start += height
    where = jnp.stack(where).astype(jnp.int32)
    blocks = jnp.stack([((x + d) % 4) * 256 for d in range(4)]).astype(jnp.int32)
    arrays = [value for value, _ in held]
    given = gram(where, blocks, swap(rows), arrays, tuple(place))
    got = swap(given)
    own = gram(where, blocks, rows, arrays, tuple(place))
    info = jnp.stack([c, (z * 8 + x * 2 + c) * 256, y * WIDTH]).astype(jnp.int32)
    mean, gram_factor = finish(info, kept_total[None], own, got)
    return (mean[0], gram_factor)


def solution(mesh):
    fine = Mesh(mesh.devices.reshape(4, 4, 2, 4), ("z", "x", "c", "y"))
    return jax.shard_map(
        per_device,
        mesh=fine,
        in_specs=(P(TOK, "y"), P("y"), P(TOK), P(TOK)),
        out_specs=(P("y"), P(TOK, "y")),
        check_vma=False,
    )
```

```python
import jax
import jax.numpy as jnp
from jax import lax
from jax.experimental import pallas as pl
from jax.experimental.pallas import tpu as pltpu
from jax.sharding import Mesh, PartitionSpec as P

epsilon = 1e-05
TOK = ("z", "x", "c")
SLOTS = 256
LIVE = 4096
WIDTH = 2048
PIECE = 64
EXTRA = 16
LONG = LIVE + 128
VMEM = 60 * 1024 * 1024
bf16 = jnp.bfloat16
f32 = jnp.float32


def params(**kw):
    return pltpu.CompilerParams(vmem_limit_bytes=VMEM, **kw)


def spread(value, place):
    high = value.astype(bf16).astype(f32)
    middle = (value - high).astype(bf16).astype(f32)
    low = value - high - middle
    rest = jnp.where(place == 2, low, 0.0)
    return jnp.where(place == 0, high, jnp.where(place == 1, middle, rest))


def pick_kernel(index_ref, counts_ref, resid_ref, out_ref):
    tokens = resid_ref.shape[0]
    token = lax.broadcasted_iota(jnp.int32, (tokens, SLOTS), 0)
    slot = lax.broadcasted_iota(jnp.int32, (1, SLOTS), 1)
    half = SLOTS // 2
    end = jnp.where(slot < half, counts_ref[0], half + counts_ref[1])
    kept = jnp.where(slot < end, index_ref[...], -1)
    one_hot = jnp.where(token == kept, 1.0, 0.0).astype(bf16)
    total = jnp.zeros((1, SLOTS), f32)
    step = 512
    for x in range(4):
        part = lax.dot_general(
            resid_ref[:, x * step : (x + 1) * step],
            one_hot,
            (((0,), (0,)), ((), ())),
            preferred_element_type=f32,
        )
        total += jnp.sum(part * part, axis=0, keepdims=True)
        short = part.astype(bf16)
        for c in range(2):
            for z in range(4):
                first = (c * 4 + z) * PIECE
                out_ref[z * 8 + x * 2 + c, :PIECE, :] = short[first : first + PIECE, :]
    live = (counts_ref[0] + counts_ref[1]).astype(f32)
    row = lax.broadcasted_iota(jnp.int32, (EXTRA, SLOTS), 0)
    extra = jnp.where(row == 3, live, spread(total, row)).astype(bf16)
    for t in range(32):
        out_ref[t, PIECE:, :] = extra


def pick(resid, keep_index, counts):
    return pl.pallas_call(
        pick_kernel,
        out_shape=jax.ShapeDtypeStruct((32, PIECE + EXTRA, SLOTS), bf16),
        in_specs=[
            pl.BlockSpec(memory_space=pltpu.VMEM),
            pl.BlockSpec(memory_space=pltpu.SMEM),
            pl.BlockSpec(memory_space=pltpu.VMEM),
        ],
        out_specs=pl.BlockSpec(memory_space=pltpu.VMEM),
        compiler_params=params(),
        name="pick",
    )(keep_index[None, :], counts, resid)


def pack_kernel(first_ref, in_ref, scale_ref, gain_ref, out_ref, acc_ref):
    acc_ref[...] = jnp.zeros_like(acc_ref)
    gain = gain_ref[...]
    group = 4

    def body(g, _):
        moved = []
        for k in range(group):
            t = g * group + k
            rows = in_ref[t, :PIECE, :].astype(f32) * scale_ref[pl.ds(t, 1), :] * gain
            first = first_ref[t]
            base = pl.multiple_of((first // 128) * 128, 128)
            wide = jnp.concatenate([rows, jnp.zeros((PIECE, 128), f32)], axis=1)
            moved.append((base, pltpu.roll(wide, first - base, 1)))
        for base, rows in moved:
            acc_ref[:, pl.ds(base, SLOTS + 128)] += rows
        return 0

    lax.fori_loop(0, 32 // group, body, 0)
    short = acc_ref[:, :LIVE].astype(bf16)
    out_ref[:, :LIVE] = short
    total = jnp.sum(short.astype(f32), axis=1, keepdims=True)
    lane = lax.broadcasted_iota(jnp.int32, (PIECE, 128), 1)
    out_ref[:, LIVE:] = spread(total, lane).astype(bf16)


def pack(first, pieces, scale, gain):
    return pl.pallas_call(
        pack_kernel,
        out_shape=jax.ShapeDtypeStruct((PIECE, LONG), bf16),
        in_specs=[pl.BlockSpec(memory_space=pltpu.SMEM)] + [pl.BlockSpec(memory_space=pltpu.VMEM)] * 3,
        out_specs=pl.BlockSpec(memory_space=pltpu.VMEM),
        scratch_shapes=[pltpu.VMEM((PIECE, LIVE + SLOTS + 128), f32)],
        compiler_params=params(),
        name="pack",
    )(first, pieces, scale, gain)


def gram_kernel(row_place, col_place, row_where, col_where, *refs):
    arrays = refs[: 2 + 8]
    own_ref, given_ref, rows, cols, row_sem, sem = refs[2 + 8 :]
    row_copies = []
    for k, (index, start, height) in enumerate(row_place):
        first = pl.multiple_of(row_where[k], 32)
        source = arrays[index].at[pl.ds(start, height), pl.ds(0, LIVE)]
        row_copies.append(pltpu.make_async_copy(source, rows.at[pl.ds(first, height)], row_sem.at[k]))
    copies = []
    for k, (index, start, height, block) in enumerate(col_place):
        first = pl.multiple_of(col_where[k], 16)
        source = arrays[2 + index].at[pl.ds(start, height)]
        copies.append((block, pltpu.make_async_copy(source, cols.at[pl.ds(first, height)], sem.at[k])))
    copies.sort(key=lambda pair: pair[0])
    for copy in row_copies:
        copy.start()
    for _, copy in copies:
        copy.start()
    for copy in row_copies:
        copy.wait()
    lane = lax.broadcasted_iota(jnp.int32, (16, 128), 1)
    terms = jnp.where(lane < 3, 1.0, 0.0).astype(bf16)
    for block in range(2):
        for at, copy in copies:
            if at == block:
                copy.wait()
        inside = slice(block * 256, (block + 1) * 256)
        product = lax.dot_general(
            rows[...], cols[inside, :LIVE], (((1,), (1,)), ((), ())), preferred_element_type=f32
        )
        own_ref[:256, inside] = product[:256]
        given_ref[:256, inside] = product[256:]
        sums = lax.dot_general(
            terms, cols[inside, LIVE:], (((1,), (1,)), ((), ())), preferred_element_type=f32
        )
        own_ref[256:, inside] = sums[:8]
        given_ref[256:, inside] = sums[:8]


def gram(row_where, col_where, arrays, row_place, col_place):
    n_cols = 512
    return pl.pallas_call(
        lambda *refs: gram_kernel(row_place, col_place, *refs),
        out_shape=(jax.ShapeDtypeStruct((264, n_cols), f32),) * 2,
        in_specs=[pl.BlockSpec(memory_space=pltpu.SMEM)] * 2
        + [pl.BlockSpec(memory_space=pl.ANY)] * len(arrays),
        out_specs=(pl.BlockSpec(memory_space=pltpu.VMEM),) * 2,
        scratch_shapes=[
            pltpu.VMEM((512, LIVE), bf16),
            pltpu.VMEM((n_cols, LONG), bf16),
            pltpu.SemaphoreType.DMA((len(row_place),)),
            pltpu.SemaphoreType.DMA((len(col_place),)),
        ],
        compiler_params=params(),
        cost_estimate=pl.CostEstimate(
            flops=2 * 512 * n_cols * LIVE, bytes_accessed=10 * 1024 * 1024, transcendentals=0
        ),
        name="gram",
    )(row_where, col_where, *arrays)


def finish_kernel(info_ref, total_ref, own0_ref, own1_ref, got0_ref, got1_ref, mean_ref, out_ref):
    core, row_first, col_first, place = info_ref[0], info_ref[1], info_ref[2], info_ref[3]
    total = total_ref[0]
    row = row_first + lax.broadcasted_iota(jnp.int32, (256, 256), 0)
    col = col_first + lax.broadcasted_iota(jnp.int32, (256, 256), 1)
    for k, flip in enumerate((0, 1, 3, 2)):
        x = place ^ flip
        inside = slice((k % 2) * 256, (k % 2 + 1) * 256)
        for ref, side in (
            ((own0_ref, own1_ref)[k // 2], core),
            ((got0_ref, got1_ref)[k // 2], 1 - core),
        ):
            at = pl.multiple_of(x * 512 + side * 256, 256)
            values = ref[:256, inside] / total
            out_ref[:, pl.ds(at, 256)] = jnp.where(row <= col + at, values, 0.0)
            mean_ref[:, pl.ds(at, 256)] = ref[256:264, inside][:1] / total


def finish(info, total, own, got):
    return pl.pallas_call(
        finish_kernel,
        out_shape=(
            jax.ShapeDtypeStruct((1, WIDTH), f32),
            jax.ShapeDtypeStruct((256, WIDTH), f32),
        ),
        in_specs=[pl.BlockSpec(memory_space=pltpu.SMEM)] * 2 + [pl.BlockSpec(memory_space=pltpu.VMEM)] * 4,
        out_specs=(pl.BlockSpec(memory_space=pltpu.VMEM),) * 2,
        compiler_params=params(),
        name="finish",
    )(info, total, *own, *got)


def shift(value, axis, by):
    return lax.ppermute(value, axis, [((i + by) % 4, i) for i in range(4)])


def swap(value):
    return lax.ppermute(value, "c", [(0, 1), (1, 0)])


def trade(value, axis, flip):
    return lax.ppermute(value, axis, [(i, i ^ flip) for i in range(4)])


def join(*values):
    return jnp.concatenate(values, axis=0)


def per_device(resid, norm_gain, keep_index, counts):
    z, x, c, y = (lax.axis_index(a) for a in ("z", "x", "c", "y"))
    pieces = lax.all_to_all(pick(resid, keep_index, counts), TOK, 0, 0, tiled=True)

    extra = pieces[:, PIECE : PIECE + 4, :].astype(f32)
    loads = extra[:, 3, 0].astype(jnp.int32)
    first = jnp.cumsum(loads) - loads
    kept_total = jnp.sum(loads).astype(f32)
    sums = extra[:, 0, :] + extra[:, 1, :] + extra[:, 2, :]
    squares = (sums + shift(sums, "y", 2)) + (shift(sums, "y", 1) + shift(sums, "y", 3))
    scale = lax.rsqrt(squares / 8192 + epsilon)
    gain = lax.dynamic_slice_in_dim(norm_gain, ((x * 2 + c) * 4 + z) * PIECE, PIECE)[:, None]
    mine = pack(first, pieces, scale, gain)

    turned = lax.ppermute(mine, ("z", "y"), [(i * 4 + j, j * 4 + i) for i in range(4) for j in range(4)])

    partners = (("x", 1), ("z", 1), ("x", 3), ("z", 3))
    streams = [mine[s * 16 : (s + 1) * 16] for s in range(4)]
    held = [[(0, 0)]] * 4
    arrays, place, where = [], [[], []], [[], []]
    for step in range(4):
        for s in range(4):
            axis, flip = partners[(s + step) % 4]
            dx, dz = (flip, 0) if axis == "x" else (0, flip)
            got = trade(streams[s], axis, flip)
            told = [(a ^ dx, b ^ dz) for a, b in held[s]]
            if step < 3:
                streams[s] = join(streams[s], got)
                held[s] = held[s] + told
                continue
            for value, tags in ((streams[s], held[s]), (got, told)):
                for k, (a, b) in enumerate(tags):
                    block = (0, 1, 3, 2).index(a)
                    place[block // 2].append((len(arrays), k * 16, 16, block % 2))
                    where[block // 2].append((block % 2) * 256 + (z ^ b) * PIECE + s * 16)
                arrays.append(value)

    low, high = turned[:32], turned[32:]
    low, high = join(low, trade(low, "y", 1)), join(high, trade(high, "y", 3))
    low, high = join(low, trade(low, "y", 3)), join(high, trade(high, "y", 1))
    rows = join(low, high)
    other = swap(rows)
    row_place, row_where = [], []
    for index in range(2):
        for k in range(8):
            flip = ((0, 1, 3, 2), (0, 3, 1, 2))[k // 4][k % 4]
            row_place.append((index, k * 32, 32))
            row_where.append(index * 256 + (y ^ flip) * PIECE + k // 4 * 32)
    row_where = jnp.stack(row_where).astype(jnp.int32)

    own, got = [], []
    for k in range(2):
        col_where = jnp.stack(where[k]).astype(jnp.int32)
        kept, given = gram(row_where, col_where, [rows, other, *arrays], tuple(row_place), tuple(place[k]))
        own.append(kept)
        got.append(swap(given))
    info = jnp.stack([c, (z * 8 + x * 2 + c) * 256, y * WIDTH, x]).astype(jnp.int32)
    mean, gram_factor = finish(info, kept_total[None], own, got)
    return (mean[0], gram_factor)


def solution(mesh):
    fine = Mesh(mesh.devices.reshape(4, 4, 2, 4), ("z", "x", "c", "y"))
    return jax.shard_map(
        per_device,
        mesh=fine,
        in_specs=(P(TOK, "y"), P("y"), P(TOK), P(TOK)),
        out_specs=(P("y"), P(TOK, "y")),
        check_vma=False,
    )
```

```python
import jax
import jax.numpy as jnp
from jax import lax
from jax.experimental import pallas as pl
from jax.experimental.pallas import tpu as pltpu
from jax.sharding import Mesh, PartitionSpec as P

epsilon = 1e-05
TOK = ("z", "x", "c")
SLOTS = 256
LIVE = 4096
WIDTH = 2048
PIECE = 64
EXTRA = 16
LONG = LIVE + 128
VMEM = 60 * 1024 * 1024
bf16 = jnp.bfloat16
f32 = jnp.float32


def params(**kw):
    return pltpu.CompilerParams(vmem_limit_bytes=VMEM, **kw)


def spread(value, place):
    high = value.astype(bf16).astype(f32)
    middle = (value - high).astype(bf16).astype(f32)
    low = value - high - middle
    rest = jnp.where(place == 2, low, 0.0)
    return jnp.where(place == 0, high, jnp.where(place == 1, middle, rest))


def pick_kernel(index_ref, counts_ref, resid_ref, picked_ref, sums_ref):
    tokens = resid_ref.shape[0]
    token = lax.broadcasted_iota(jnp.int32, (tokens, SLOTS), 0)
    slot = lax.broadcasted_iota(jnp.int32, (1, SLOTS), 1)
    half = SLOTS // 2
    end = jnp.where(slot < half, counts_ref[0], half + counts_ref[1])
    kept = jnp.where(slot < end, index_ref[...], -1)
    one_hot = jnp.where(token == kept, 1.0, 0.0).astype(bf16)
    total = jnp.zeros((1, SLOTS), f32)
    step = 512
    for k in range(WIDTH // step):
        part = lax.dot_general(
            resid_ref[:, k * step : (k + 1) * step],
            one_hot,
            (((0,), (0,)), ((), ())),
            preferred_element_type=f32,
        )
        total += jnp.sum(part * part, axis=0, keepdims=True)
        picked_ref[k * step : (k + 1) * step, :] = part.astype(bf16)
    sums_ref[...] = jnp.broadcast_to(total, sums_ref.shape)


def pick(resid, keep_index, counts):
    return pl.pallas_call(
        pick_kernel,
        out_shape=(
            jax.ShapeDtypeStruct((WIDTH, SLOTS), bf16),
            jax.ShapeDtypeStruct((8, SLOTS), f32),
        ),
        in_specs=[
            pl.BlockSpec(memory_space=pltpu.VMEM),
            pl.BlockSpec(memory_space=pltpu.SMEM),
            pl.BlockSpec(memory_space=pltpu.VMEM),
        ],
        out_specs=(pl.BlockSpec(memory_space=pltpu.VMEM),) * 2,
        compiler_params=params(),
        name="pick",
    )(keep_index[None, :], counts, resid)


def norm_kernel(place_ref, counts_ref, picked_ref, gain_ref, s0, s1, s2, s3, out_ref, *turn_refs):
    squares = (s0[:1, :] + s2[:1, :]) + (s1[:1, :] + s3[:1, :])
    scale = lax.rsqrt(squares / 8192 + epsilon)
    y = place_ref[0]
    live = (counts_ref[0] + counts_ref[1]).astype(f32)
    extra = jnp.full((EXTRA, SLOTS), live, f32).astype(bf16)

    for x in range(4):
        for c in range(2):
            first = (x * 2 + c) * 4 * PIECE
            rows = picked_ref[first : first + 4 * PIECE, :].astype(f32)
            short = (rows * scale * gain_ref[first : first + 4 * PIECE, :]).astype(bf16)
            for q in range(4):
                piece = short[q * PIECE : (q + 1) * PIECE, :]
                out_ref[q * 8 + x * 2 + c, :PIECE, :] = piece
                out_ref[q * 8 + x * 2 + c, PIECE:, :] = extra
            for k, ref in enumerate(turn_refs):
                ref[x * 2 + c] = out_ref[(y ^ (k + 1)) * 8 + x * 2 + c, :PIECE, :]


def norm(place, counts, picked, gain, sums):
    return pl.pallas_call(
        norm_kernel,
        out_shape=(jax.ShapeDtypeStruct((32, PIECE + EXTRA, SLOTS), bf16),)
        + (jax.ShapeDtypeStruct((8, PIECE, SLOTS), bf16),) * 3,
        in_specs=[pl.BlockSpec(memory_space=pltpu.SMEM)] * 2 + [pl.BlockSpec(memory_space=pltpu.VMEM)] * 6,
        out_specs=(pl.BlockSpec(memory_space=pltpu.VMEM),) * 4,
        compiler_params=params(),
        name="norm",
    )(place, counts, picked, gain, *sums)


def order_kernel(place_ref, own_ref, a_ref, b_ref, c_ref, out_ref, sem):
    y = place_ref[0]
    copies = [
        pltpu.make_async_copy(
            own_ref.at[pl.ds(y * 8, 8), pl.ds(0, PIECE)], out_ref.at[pl.ds(y * 8, 8)], sem.at[0]
        )
    ]
    for k, ref in enumerate((a_ref, b_ref, c_ref)):
        copies.append(
            pltpu.make_async_copy(ref, out_ref.at[pl.ds((y ^ (k + 1)) * 8, 8)], sem.at[k + 1])
        )
    for copy in copies:
        copy.start()
    for copy in copies:
        copy.wait()


def order(place, own, others):
    return pl.pallas_call(
        order_kernel,
        out_shape=jax.ShapeDtypeStruct((32, PIECE, SLOTS), bf16),
        in_specs=[pl.BlockSpec(memory_space=pltpu.SMEM)] + [pl.BlockSpec(memory_space=pl.ANY)] * 4,
        out_specs=pl.BlockSpec(memory_space=pl.ANY),
        scratch_shapes=[pltpu.SemaphoreType.DMA((4,))],
        compiler_params=params(),
        name="order",
    )(place, own, *others)


def pack_kernel(first_ref, in_ref, out_ref, acc_ref):
    acc_ref[...] = jnp.zeros_like(acc_ref)
    group = 4

    def body(g, _):
        moved = []
        for k in range(group):
            t = g * group + k
            rows = in_ref[t, :PIECE, :].astype(f32)
            first = first_ref[t]
            base = pl.multiple_of((first // 128) * 128, 128)
            wide = jnp.concatenate([rows, jnp.zeros((PIECE, 128), f32)], axis=1)
            moved.append((base, pltpu.roll(wide, first - base, 1)))
        for base, rows in moved:
            acc_ref[:, pl.ds(base, SLOTS + 128)] += rows
        return 0

    lax.fori_loop(0, 32 // group, body, 0)
    short = acc_ref[:, :LIVE].astype(bf16)
    out_ref[:, :LIVE] = short
    total = jnp.sum(short.astype(f32), axis=1, keepdims=True)
    lane = lax.broadcasted_iota(jnp.int32, (PIECE, 128), 1)
    out_ref[:, LIVE:] = spread(total, lane).astype(bf16)


def pack(first, pieces):
    return pl.pallas_call(
        pack_kernel,
        out_shape=jax.ShapeDtypeStruct((PIECE, LONG), bf16),
        in_specs=[pl.BlockSpec(memory_space=pltpu.SMEM)] + [pl.BlockSpec(memory_space=pltpu.VMEM)],
        out_specs=pl.BlockSpec(memory_space=pltpu.VMEM),
        scratch_shapes=[pltpu.VMEM((PIECE, LIVE + SLOTS + 128), f32)],
        compiler_params=params(),
        name="pack",
    )(first, pieces)


def gram_kernel(row_place, col_place, row_where, col_where, *refs):
    arrays = refs[: 2 + 8]
    own_ref, given_ref, rows, cols, row_sem, sem = refs[2 + 8 :]
    row_copies = []
    for k, (index, start, height) in enumerate(row_place):
        first = pl.multiple_of(row_where[k], 32)
        source = arrays[index].at[pl.ds(start, height), pl.ds(0, LIVE)]
        row_copies.append(pltpu.make_async_copy(source, rows.at[pl.ds(first, height)], row_sem.at[k]))
    copies = []
    for k, (index, start, height, block) in enumerate(col_place):
        first = pl.multiple_of(col_where[k], 16)
        source = arrays[2 + index].at[pl.ds(start, height)]
        copies.append((block, pltpu.make_async_copy(source, cols.at[pl.ds(first, height)], sem.at[k])))
    copies.sort(key=lambda pair: pair[0])
    for copy in row_copies:
        copy.start()
    for _, copy in copies:
        copy.start()
    for copy in row_copies:
        copy.wait()
    lane = lax.broadcasted_iota(jnp.int32, (16, 128), 1)
    terms = jnp.where(lane < 3, 1.0, 0.0).astype(bf16)
    for block in range(2):
        for at, copy in copies:
            if at == block:
                copy.wait()
        inside = slice(block * 256, (block + 1) * 256)
        product = lax.dot_general(
            rows[...], cols[inside, :LIVE], (((1,), (1,)), ((), ())), preferred_element_type=f32
        )
        own_ref[:256, inside] = product[:256]
        given_ref[:256, inside] = product[256:]
        sums = lax.dot_general(
            terms, cols[inside, LIVE:], (((1,), (1,)), ((), ())), preferred_element_type=f32
        )
        own_ref[256:, inside] = sums[:8]
        given_ref[256:, inside] = sums[:8]


def gram(row_where, col_where, arrays, row_place, col_place):
    n_cols = 512
    return pl.pallas_call(
        lambda *refs: gram_kernel(row_place, col_place, *refs),
        out_shape=(jax.ShapeDtypeStruct((264, n_cols), f32),) * 2,
        in_specs=[pl.BlockSpec(memory_space=pltpu.SMEM)] * 2
        + [pl.BlockSpec(memory_space=pl.ANY)] * len(arrays),
        out_specs=(pl.BlockSpec(memory_space=pltpu.VMEM),) * 2,
        scratch_shapes=[
            pltpu.VMEM((512, LIVE), bf16),
            pltpu.VMEM((n_cols, LONG), bf16),
            pltpu.SemaphoreType.DMA((len(row_place),)),
            pltpu.SemaphoreType.DMA((len(col_place),)),
        ],
        compiler_params=params(),
        cost_estimate=pl.CostEstimate(
            flops=2 * 512 * n_cols * LIVE, bytes_accessed=10 * 1024 * 1024, transcendentals=0
        ),
        name="gram",
    )(row_where, col_where, *arrays)


def finish_kernel(info_ref, total_ref, own0_ref, own1_ref, got0_ref, got1_ref, mean_ref, out_ref):
    core, row_first, col_first, place = info_ref[0], info_ref[1], info_ref[2], info_ref[3]
    total = total_ref[0]
    row = row_first + lax.broadcasted_iota(jnp.int32, (256, 256), 0)
    col = col_first + lax.broadcasted_iota(jnp.int32, (256, 256), 1)
    for k, flip in enumerate((0, 1, 3, 2)):
        x = place ^ flip
        inside = slice((k % 2) * 256, (k % 2 + 1) * 256)
        for ref, side in (
            ((own0_ref, own1_ref)[k // 2], core),
            ((got0_ref, got1_ref)[k // 2], 1 - core),
        ):
            at = pl.multiple_of(x * 512 + side * 256, 256)
            values = ref[:256, inside] / total
            out_ref[:, pl.ds(at, 256)] = jnp.where(row <= col + at, values, 0.0)
            mean_ref[:, pl.ds(at, 256)] = ref[256:264, inside][:1] / total


def finish(info, total, own, got):
    return pl.pallas_call(
        finish_kernel,
        out_shape=(
            jax.ShapeDtypeStruct((1, WIDTH), f32),
            jax.ShapeDtypeStruct((256, WIDTH), f32),
        ),
        in_specs=[pl.BlockSpec(memory_space=pltpu.SMEM)] * 2 + [pl.BlockSpec(memory_space=pltpu.VMEM)] * 4,
        out_specs=(pl.BlockSpec(memory_space=pltpu.VMEM),) * 2,
        compiler_params=params(),
        name="finish",
    )(info, total, *own, *got)


def swap(value):
    return lax.ppermute(value, "c", [(0, 1), (1, 0)])


def trade(value, axis, flip):
    return lax.ppermute(value, axis, [(i, i ^ flip) for i in range(4)])


def join(*values):
    return jnp.concatenate(values, axis=0)


def per_device(resid, norm_gain, keep_index, counts):
    z, x, c, y = (lax.axis_index(a) for a in ("z", "x", "c", "y"))
    place_y = y[None].astype(jnp.int32)
    picked, sums = pick(resid, keep_index, counts)
    all_sums = [sums] + [trade(sums, "y", flip) for flip in (1, 2, 3)]
    normed, *turns = norm(place_y, counts, picked, norm_gain[:, None], all_sums)
    pieces = lax.all_to_all(normed, TOK, 0, 0, tiled=True)
    panel = order(place_y, normed, [trade(turns[k], "y", k + 1) for k in range(3)])
    panel = lax.all_to_all(panel, TOK, 0, 0, tiled=True)

    loads = pieces[:, PIECE, 0].astype(jnp.int32)
    first = jnp.cumsum(loads) - loads
    kept_total = jnp.sum(loads).astype(f32)
    mine = pack(first, pieces)
    turned = pack(first, panel)

    partners = (("x", 1), ("z", 1), ("x", 3), ("z", 3))
    streams = [mine[s * 16 : (s + 1) * 16] for s in range(4)]
    held = [[(0, 0)]] * 4
    arrays, place, where = [], [[], []], [[], []]
    for step in range(4):
        for s in range(4):
            axis, flip = partners[(s + step) % 4]
            dx, dz = (flip, 0) if axis == "x" else (0, flip)
            got = trade(streams[s], axis, flip)
            told = [(a ^ dx, b ^ dz) for a, b in held[s]]
            if step < 3:
                streams[s] = join(streams[s], got)
                held[s] = held[s] + told
                continue
            for value, tags in ((streams[s], held[s]), (got, told)):
                for k, (a, b) in enumerate(tags):
                    block = (0, 1, 3, 2).index(a)
                    place[block // 2].append((len(arrays), k * 16, 16, block % 2))
                    where[block // 2].append((block % 2) * 256 + (z ^ b) * PIECE + s * 16)
                arrays.append(value)

    low, high = turned[:32], turned[32:]
    low, high = join(low, trade(low, "y", 1)), join(high, trade(high, "y", 3))
    low, high = join(low, trade(low, "y", 3)), join(high, trade(high, "y", 1))
    rows = join(low, high)
    other = swap(rows)
    row_place, row_where = [], []
    for index in range(2):
        for k in range(8):
            flip = ((0, 1, 3, 2), (0, 3, 1, 2))[k // 4][k % 4]
            row_place.append((index, k * 32, 32))
            row_where.append(index * 256 + (y ^ flip) * PIECE + k // 4 * 32)
    row_where = jnp.stack(row_where).astype(jnp.int32)

    own, got = [], []
    for k in range(2):
        col_where = jnp.stack(where[k]).astype(jnp.int32)
        kept, given = gram(row_where, col_where, [rows, other, *arrays], tuple(row_place), tuple(place[k]))
        own.append(kept)
        got.append(swap(given))
    info = jnp.stack([c, (z * 8 + x * 2 + c) * 256, y * WIDTH, x]).astype(jnp.int32)
    mean, gram_factor = finish(info, kept_total[None], own, got)
    return (mean[0], gram_factor)


def solution(mesh):
    fine = Mesh(mesh.devices.reshape(4, 4, 2, 4), ("z", "x", "c", "y"))
    return jax.shard_map(
        per_device,
        mesh=fine,
        in_specs=(P(TOK, "y"), P("y"), P(TOK), P(TOK)),
        out_specs=(P("y"), P(TOK, "y")),
        check_vma=False,
    )
```

```python
import jax
import jax.numpy as jnp
from jax import lax
from jax.experimental import pallas as pl
from jax.experimental.pallas import tpu as pltpu
from jax.sharding import Mesh, PartitionSpec as P

epsilon = 1e-05
TOK = ("z", "x", "c")
SLOTS = 256
LIVE = 4096
WIDTH = 2048
PIECE = 64
EXTRA = 16
LONG = LIVE + 128
MIB = 1024 * 1024
bf16 = jnp.bfloat16
f32 = jnp.float32


def params(mib):
    return pltpu.CompilerParams(vmem_limit_bytes=mib * MIB)


def spread(value, place):
    high = value.astype(bf16).astype(f32)
    middle = (value - high).astype(bf16).astype(f32)
    low = value - high - middle
    rest = jnp.where(place == 2, low, 0.0)
    return jnp.where(place == 0, high, jnp.where(place == 1, middle, rest))


def pick_kernel(index_ref, counts_ref, resid_ref, picked_ref, sums_ref):
    tokens = resid_ref.shape[0]
    token = lax.broadcasted_iota(jnp.int32, (tokens, SLOTS), 0)
    slot = lax.broadcasted_iota(jnp.int32, (1, SLOTS), 1)
    half = SLOTS // 2
    end = jnp.where(slot < half, counts_ref[0], half + counts_ref[1])
    kept = jnp.where(slot < end, index_ref[...], -1)
    one_hot = jnp.where(token == kept, 1.0, 0.0).astype(bf16)
    total = jnp.zeros((1, SLOTS), f32)
    step = 512
    for k in range(WIDTH // step):
        part = lax.dot_general(
            resid_ref[:, k * step : (k + 1) * step],
            one_hot,
            (((0,), (0,)), ((), ())),
            preferred_element_type=f32,
        )
        total += jnp.sum(part * part, axis=0, keepdims=True)
        picked_ref[k * step : (k + 1) * step, :] = part.astype(bf16)
    sums_ref[...] = jnp.broadcast_to(total, sums_ref.shape)


def pick(resid, keep_index, counts):
    return pl.pallas_call(
        pick_kernel,
        out_shape=(
            jax.ShapeDtypeStruct((WIDTH, SLOTS), bf16),
            jax.ShapeDtypeStruct((8, SLOTS), f32),
        ),
        in_specs=[
            pl.BlockSpec(memory_space=pltpu.VMEM),
            pl.BlockSpec(memory_space=pltpu.SMEM),
            pl.BlockSpec(memory_space=pltpu.VMEM),
        ],
        out_specs=(pl.BlockSpec(memory_space=pltpu.VMEM),) * 2,
        compiler_params=params(16),
        name="pick",
    )(keep_index[None, :], counts, resid)


PARTNERS = (("x", 1), ("z", 1), ("x", 3), ("z", 3))


def side(place, flip, first):
    if flip == 1 and not first:
        return (place ^ (place >> 1)) & 1
    return place & 1 if flip == 1 else place >> 1


def slot_of(s, x, z):
    at, seen = 0, []
    for step in range(4):
        axis, flip = PARTNERS[(s + step) % 4]
        at += side(x if axis == "x" else z, flip, axis not in seen) << step
        seen.append(axis)
    return at


def norm_kernel(place_ref, counts_ref, picked_ref, gain_ref, s0, s1, s2, s3, out_ref, *refs):
    turn_refs, all_ref = refs[:4], refs[4]
    squares = (s0[:1, :] + s2[:1, :]) + (s1[:1, :] + s3[:1, :])
    scale = lax.rsqrt(squares / 8192 + epsilon)
    y = place_ref[0]
    live = (counts_ref[0] + counts_ref[1]).astype(f32)
    extra = jnp.full((EXTRA, SLOTS), live, f32).astype(bf16)
    for s in range(4):
        for c in range(2):
            first = (s * 2 + c) * 256
            rows = picked_ref[first : first + 256, :].astype(f32)
            short = (rows * scale * gain_ref[first : first + 256, :]).astype(bf16)
            all_ref[first : first + 256, :] = short
            for z in range(4):
                for x in range(4):
                    at = slot_of(s, x, z) * 16
                    out_ref[z * 8 + x * 2 + c, s * 16 : (s + 1) * 16, :] = short[at : at + 16, :]
    for t in range(32):
        out_ref[t, PIECE:, :] = extra
    for flip, ref in enumerate(turn_refs):
        q = y ^ flip
        low = q * 32
        high = 128 + (((q ^ (q >> 1)) & 1) * 2 + (q >> 1)) * 32
        for k in range(8):
            ref[k, :32, :] = all_ref[pl.ds(pl.multiple_of(k * 256 + low, 32), 32), :]
            ref[k, 32:, :] = all_ref[pl.ds(pl.multiple_of(k * 256 + high, 32), 32), :]


def norm(place, counts, picked, gain, sums):
    return pl.pallas_call(
        norm_kernel,
        out_shape=(jax.ShapeDtypeStruct((32, PIECE + EXTRA, SLOTS), bf16),)
        + (jax.ShapeDtypeStruct((8, PIECE, SLOTS), bf16),) * 4,
        in_specs=[pl.BlockSpec(memory_space=pltpu.SMEM)] * 2 + [pl.BlockSpec(memory_space=pltpu.VMEM)] * 6,
        out_specs=(pl.BlockSpec(memory_space=pltpu.VMEM),) * 5,
        scratch_shapes=[pltpu.VMEM((WIDTH, SLOTS), bf16)],
        compiler_params=params(12),
        name="norm",
    )(place, counts, picked, gain, *sums)


def order_kernel(place_ref, own_ref, a_ref, b_ref, c_ref, out_ref):
    y = place_ref[0]
    for k in range(8):
        for flip, ref in enumerate((own_ref, a_ref, b_ref, c_ref)):
            out_ref[(y ^ flip) * 8 + k] = ref[k]


def order(place, blocks):
    return pl.pallas_call(
        order_kernel,
        out_shape=jax.ShapeDtypeStruct((32, PIECE, SLOTS), bf16),
        in_specs=[pl.BlockSpec(memory_space=pltpu.SMEM)] + [pl.BlockSpec(memory_space=pltpu.VMEM)] * 4,
        out_specs=pl.BlockSpec(memory_space=pltpu.VMEM),
        compiler_params=params(8),
        name="order",
    )(place, *blocks)


def pack_kernel(heights, first_ref, in_ref, *refs):
    out_refs, acc_ref = refs[:-1], refs[-1]
    acc_ref[...] = jnp.zeros_like(acc_ref)
    group = 4

    def body(g, _):
        moved = []
        for k in range(group):
            t = g * group + k
            rows = in_ref[t, :PIECE, :].astype(f32)
            first = first_ref[t]
            base = pl.multiple_of((first // 128) * 128, 128)
            wide = jnp.concatenate([rows, jnp.zeros((PIECE, 128), f32)], axis=1)
            moved.append((base, pltpu.roll(wide, first - base, 1)))
        for base, rows in moved:
            acc_ref[:, pl.ds(base, SLOTS + 128)] += rows
        return 0

    lax.fori_loop(0, 32 // group, body, 0)
    start = 0
    for ref, height in zip(out_refs, heights):
        rows = acc_ref[start : start + height, :LIVE]
        ref[:, :LIVE] = rows.astype(bf16)
        total = jnp.sum(rows, axis=1, keepdims=True)
        lane = lax.broadcasted_iota(jnp.int32, (height, 128), 1)
        ref[:, LIVE:] = spread(total, lane).astype(bf16)
        start += height


def pack(first, pieces, heights):
    return pl.pallas_call(
        lambda *refs: pack_kernel(heights, *refs),
        out_shape=tuple(jax.ShapeDtypeStruct((height, LONG), bf16) for height in heights),
        in_specs=[pl.BlockSpec(memory_space=pltpu.SMEM), pl.BlockSpec(memory_space=pltpu.VMEM)],
        out_specs=(pl.BlockSpec(memory_space=pltpu.VMEM),) * len(heights),
        scratch_shapes=[pltpu.VMEM((PIECE, LIVE + SLOTS + 128), f32)],
        compiler_params=params(10),
        name="pack",
    )(first, pieces)


def gram_kernel(rows_ref, cols_ref, own_ref, given_ref):
    product = lax.dot_general(
        rows_ref[:, :LIVE], cols_ref[:, :LIVE], (((1,), (1,)), ((), ())), preferred_element_type=f32
    )
    own_ref[:256, :] = product[:256]
    given_ref[:256, :] = product[256:]
    lane = lax.broadcasted_iota(jnp.int32, (16, 128), 1)
    terms = jnp.where(lane < 3, 1.0, 0.0).astype(bf16)
    sums = lax.dot_general(
        terms, cols_ref[:, LIVE:], (((1,), (1,)), ((), ())), preferred_element_type=f32
    )
    own_ref[256:, :] = sums[:8]
    given_ref[256:, :] = sums[:8]


def gram(rows, cols):
    return pl.pallas_call(
        gram_kernel,
        out_shape=(jax.ShapeDtypeStruct((264, 256), f32),) * 2,
        in_specs=[pl.BlockSpec(memory_space=pltpu.VMEM)] * 2,
        out_specs=(pl.BlockSpec(memory_space=pltpu.VMEM),) * 2,
        compiler_params=params(10),
        cost_estimate=pl.CostEstimate(
            flops=2 * 512 * 256 * LIVE, bytes_accessed=6 * 1024 * 1024, transcendentals=0
        ),
        name="gram",
    )(rows, cols)


def finish_kernel(info_ref, part_ref, *refs):
    own, got, (mean_ref, out_ref) = refs[:4], refs[4:8], refs[8:]
    core, row_first, col_first = info_ref[0], info_ref[1], info_ref[2]
    part = part_ref[0]
    row = row_first + lax.broadcasted_iota(jnp.int32, (256, 256), 0)
    col = col_first + lax.broadcasted_iota(jnp.int32, (256, 256), 1)
    for s in range(4):
        for ref, which in ((own[s], core), (got[s], 1 - core)):
            at = pl.multiple_of(s * 512 + which * 256, 256)
            out_ref[:, pl.ds(at, 256)] = jnp.where(row <= col + at, ref[:256, :] * part, 0.0)
            mean_ref[:, pl.ds(at, 256)] = ref[256:264, :][:1] * part


def finish(info, part, own, got):
    return pl.pallas_call(
        finish_kernel,
        out_shape=(
            jax.ShapeDtypeStruct((1, WIDTH), f32),
            jax.ShapeDtypeStruct((256, WIDTH), f32),
        ),
        in_specs=[pl.BlockSpec(memory_space=pltpu.SMEM)] * 2 + [pl.BlockSpec(memory_space=pltpu.VMEM)] * 8,
        out_specs=(pl.BlockSpec(memory_space=pltpu.VMEM),) * 2,
        compiler_params=params(10),
        name="finish",
    )(info, part, *own, *got)


def swap(value):
    return lax.ppermute(value, "c", [(0, 1), (1, 0)])


def trade(value, axis, flip):
    return lax.ppermute(value, axis, [(i, i ^ flip) for i in range(4)])


def join(*values):
    return jnp.concatenate(values, axis=0)


def meet(value, axis, flip, which):
    got = trade(value, axis, flip)
    return join(jnp.where(which == 0, value, got), jnp.where(which == 0, got, value))


def per_device(resid, norm_gain, keep_index, counts):
    z, x, c, y = (lax.axis_index(a) for a in ("z", "x", "c", "y"))
    place_y = y[None].astype(jnp.int32)
    picked, sums = pick(resid, keep_index, counts)
    all_sums = [sums] + [trade(sums, "y", flip) for flip in (1, 2, 3)]
    normed, *turns = norm(place_y, counts, picked, norm_gain[:, None], all_sums)
    pieces = lax.all_to_all(normed, TOK, 0, 0, tiled=True)
    panel = order(place_y, [turns[0]] + [trade(turns[flip], "y", flip) for flip in (1, 2, 3)])
    panel = lax.all_to_all(panel, TOK, 0, 0, tiled=True)

    loads = pieces[:, PIECE, 0].astype(jnp.int32)
    first = jnp.cumsum(loads) - loads
    part = 1.0 / jnp.sum(loads).astype(f32)

    streams = list(pack(first, pieces, (16, 16, 16, 16)))
    for step in range(4):
        for s in range(4):
            axis, flip = PARTNERS[(s + step) % 4]
            seen = [PARTNERS[(s + k) % 4][0] for k in range(step)]
            which = side(x if axis == "x" else z, flip, axis not in seen)
            streams[s] = meet(streams[s], axis, flip, which)

    low, high = pack(first, panel, (32, 32))
    low, high = meet(low, "y", 1, side(y, 1, True)), meet(high, "y", 3, side(y, 3, True))
    low, high = meet(low, "y", 3, side(y, 3, False)), meet(high, "y", 1, side(y, 1, False))
    rows = join(low, high)
    rows = join(rows, swap(rows))

    own, got = [], []
    for s in range(4):
        kept, given = gram(rows, streams[s])
        own.append(kept)
        got.append(swap(given))
    info = jnp.stack([c, (z * 8 + x * 2 + c) * 256, y * WIDTH]).astype(jnp.int32)
    mean, gram_factor = finish(info, part[None], own, got)
    return (mean[0], gram_factor)


def solution(mesh):
    fine = Mesh(mesh.devices.reshape(4, 4, 2, 4), ("z", "x", "c", "y"))
    return jax.shard_map(
        per_device,
        mesh=fine,
        in_specs=(P(TOK, "y"), P("y"), P(TOK), P(TOK)),
        out_specs=(P("y"), P(TOK, "y")),
        check_vma=False,
    )
```

```python
import jax
import jax.numpy as jnp
from jax import lax
from jax.experimental import pallas as pl
from jax.experimental.pallas import tpu as pltpu
from jax.sharding import Mesh, PartitionSpec as P

epsilon = 1e-05
TOK = ("z", "x", "c")
SLOTS = 256
LIVE = 4096
WIDTH = 2048
PIECE = 64
EXTRA = 16
LONG = LIVE + 128
MIB = 1024 * 1024
bf16 = jnp.bfloat16
f32 = jnp.float32


def params(mib):
    return pltpu.CompilerParams(vmem_limit_bytes=mib * MIB)


def spread(value, place):
    high = value.astype(bf16).astype(f32)
    middle = (value - high).astype(bf16).astype(f32)
    low = value - high - middle
    rest = jnp.where(place == 2, low, 0.0)
    return jnp.where(place == 0, high, jnp.where(place == 1, middle, rest))


def pick_kernel(place_ref, index_ref, counts_ref, resid_ref, gain_ref, picked_ref, sums_ref, *turn_refs):
    tokens = resid_ref.shape[0]
    token = lax.broadcasted_iota(jnp.int32, (tokens, SLOTS), 0)
    slot = lax.broadcasted_iota(jnp.int32, (1, SLOTS), 1)
    half = SLOTS // 2
    end = jnp.where(slot < half, counts_ref[0], half + counts_ref[1])
    kept = jnp.where(slot < end, index_ref[...], -1)
    one_hot = jnp.where(token == kept, 1.0, 0.0).astype(bf16)
    total = jnp.zeros((1, SLOTS), f32)
    step = 512
    for k in range(WIDTH // step):
        part = lax.dot_general(
            resid_ref[:, k * step : (k + 1) * step],
            one_hot,
            (((0,), (0,)), ((), ())),
            preferred_element_type=f32,
        )
        total += jnp.sum(part * part, axis=0, keepdims=True)
        picked_ref[k * step : (k + 1) * step, :] = part.astype(bf16)
    sums_ref[:8, :] = jnp.broadcast_to(total, (8, SLOTS))
    sums_ref[8:, :] = gain_ref[...]
    for flip, ref in zip((1, 2, 3), turn_refs):
        first = pl.multiple_of((place_ref[0] ^ flip) * PIECE, PIECE)
        for k in range(8):
            ref[k] = picked_ref[pl.ds(k * 256 + first, PIECE), :]


def pick(place, resid, gain, keep_index, counts):
    vmem = pl.BlockSpec(memory_space=pltpu.VMEM)
    smem = pl.BlockSpec(memory_space=pltpu.SMEM)
    return pl.pallas_call(
        pick_kernel,
        out_shape=(
            jax.ShapeDtypeStruct((WIDTH, SLOTS), bf16),
            jax.ShapeDtypeStruct((16, SLOTS), f32),
        )
        + (jax.ShapeDtypeStruct((8, PIECE, SLOTS), bf16),) * 3,
        in_specs=[smem, vmem, smem, vmem, vmem],
        out_specs=(vmem,) * 5,
        compiler_params=params(16),
        name="pick",
    )(place, keep_index[None, :], counts, resid, gain)


def scale_of(s0, s1, s2, s3):
    squares = (s0[:1, :] + s2[:1, :]) + (s1[:1, :] + s3[:1, :])
    return lax.rsqrt(squares / 8192 + epsilon)


PARTNERS = (("x", 1), ("z", 1), ("x", 3), ("z", 3))


def side(place, flip, first):
    if flip == 1 and not first:
        return (place ^ (place >> 1)) & 1
    return place & 1 if flip == 1 else place >> 1


def slot_of(s, x, z):
    at, seen = 0, []
    for step in range(4):
        axis, flip = PARTNERS[(s + step) % 4]
        at += side(x if axis == "x" else z, flip, axis not in seen) << step
        seen.append(axis)
    return at


def norm_kernel(counts_ref, picked_ref, gain_ref, s0, s1, s2, s3, out_ref):
    scale = scale_of(s0, s1, s2, s3)
    live = (counts_ref[0] + counts_ref[1]).astype(f32)
    extra = jnp.full((EXTRA, SLOTS), live, f32).astype(bf16)
    for s in range(4):
        for c in range(2):
            first = (s * 2 + c) * 256
            rows = picked_ref[first : first + 256, :].astype(f32)
            short = (rows * scale * gain_ref[first : first + 256, :]).astype(bf16)
            for z in range(4):
                for x in range(4):
                    at = slot_of(s, x, z) * 16
                    out_ref[z * 8 + x * 2 + c, s * 16 : (s + 1) * 16, :] = short[at : at + 16, :]
    for t in range(32):
        out_ref[t, PIECE:, :] = extra


def norm(counts, picked, gain, sums):
    return pl.pallas_call(
        norm_kernel,
        out_shape=jax.ShapeDtypeStruct((32, PIECE + EXTRA, SLOTS), bf16),
        in_specs=[pl.BlockSpec(memory_space=pltpu.SMEM)] + [pl.BlockSpec(memory_space=pltpu.VMEM)] * 6,
        out_specs=pl.BlockSpec(memory_space=pltpu.VMEM),
        compiler_params=params(10),
        name="norm",
    )(counts, picked, gain, *sums)


def panel_kernel(place_ref, picked_ref, t1, t2, t3, s0, s1, s2, s3, out_ref, gain_ref):
    scale = scale_of(s0, s1, s2, s3)
    y = place_ref[0]
    first = pl.multiple_of(y * PIECE, PIECE)
    for flip, (turn, sums) in enumerate(((None, s0), (t1, s1), (t2, s2), (t3, s3))):
        wide = jnp.concatenate([sums[8:, :], jnp.zeros((120, SLOTS), f32)], axis=0)
        gain_ref[...] = wide.T
        for k in range(8):
            at = (y ^ flip) * 8 + k
            rows = picked_ref[pl.ds(k * 256 + first, PIECE), :] if turn is None else turn[k]
            gain = gain_ref[pl.ds(first, PIECE), :][:, k : k + 1]
            out_ref[at] = (rows.astype(f32) * scale * gain).astype(bf16)


def panel_pieces(place, picked, turns, sums):
    return pl.pallas_call(
        panel_kernel,
        out_shape=jax.ShapeDtypeStruct((32, PIECE, SLOTS), bf16),
        in_specs=[pl.BlockSpec(memory_space=pltpu.SMEM)] + [pl.BlockSpec(memory_space=pltpu.VMEM)] * 8,
        out_specs=pl.BlockSpec(memory_space=pltpu.VMEM),
        scratch_shapes=[pltpu.VMEM((SLOTS, 128), f32)],
        compiler_params=params(10),
        name="panel",
    )(place, picked, *turns, *sums)


def pack_kernel(heights, first_ref, in_ref, *refs):
    out_refs, acc_ref = refs[:-1], refs[-1]
    acc_ref[...] = jnp.zeros_like(acc_ref)
    group = 4

    def body(g, _):
        moved = []
        for k in range(group):
            t = g * group + k
            rows = in_ref[t, :PIECE, :].astype(f32)
            first = first_ref[t]
            base = pl.multiple_of((first // 128) * 128, 128)
            wide = jnp.concatenate([rows, jnp.zeros((PIECE, 128), f32)], axis=1)
            moved.append((base, pltpu.roll(wide, first - base, 1)))
        for base, rows in moved:
            acc_ref[:, pl.ds(base, SLOTS + 128)] += rows
        return 0

    lax.fori_loop(0, 32 // group, body, 0)
    start = 0
    for ref, height in zip(out_refs, heights):
        rows = acc_ref[start : start + height, :LIVE]
        ref[:, :LIVE] = rows.astype(bf16)
        total = jnp.sum(rows, axis=1, keepdims=True)
        lane = lax.broadcasted_iota(jnp.int32, (height, 128), 1)
        ref[:, LIVE:] = spread(total, lane).astype(bf16)
        start += height


def pack(first, pieces, heights):
    return pl.pallas_call(
        lambda *refs: pack_kernel(heights, *refs),
        out_shape=tuple(jax.ShapeDtypeStruct((height, LONG), bf16) for height in heights),
        in_specs=[pl.BlockSpec(memory_space=pltpu.SMEM), pl.BlockSpec(memory_space=pltpu.VMEM)],
        out_specs=(pl.BlockSpec(memory_space=pltpu.VMEM),) * len(heights),
        scratch_shapes=[pltpu.VMEM((PIECE, LIVE + SLOTS + 128), f32)],
        compiler_params=params(10),
        name="pack",
    )(first, pieces)


def gram_kernel(rows_ref, cols_ref, own_ref, given_ref):
    product = lax.dot_general(
        rows_ref[:, :LIVE], cols_ref[:, :LIVE], (((1,), (1,)), ((), ())), preferred_element_type=f32
    )
    own_ref[:256, :] = product[:256]
    given_ref[:256, :] = product[256:]
    lane = lax.broadcasted_iota(jnp.int32, (16, 128), 1)
    terms = jnp.where(lane < 3, 1.0, 0.0).astype(bf16)
    sums = lax.dot_general(
        terms, cols_ref[:, LIVE:], (((1,), (1,)), ((), ())), preferred_element_type=f32
    )
    own_ref[256:, :] = sums[:8]
    given_ref[256:, :] = sums[:8]


def gram(rows, cols):
    return pl.pallas_call(
        gram_kernel,
        out_shape=(jax.ShapeDtypeStruct((264, 256), f32),) * 2,
        in_specs=[pl.BlockSpec(memory_space=pltpu.VMEM)] * 2,
        out_specs=(pl.BlockSpec(memory_space=pltpu.VMEM),) * 2,
        compiler_params=params(10),
        cost_estimate=pl.CostEstimate(
            flops=2 * 512 * 256 * LIVE, bytes_accessed=6 * 1024 * 1024, transcendentals=0
        ),
        name="gram",
    )(rows, cols)


def finish_kernel(info_ref, part_ref, *refs):
    own, got, (mean_ref, out_ref) = refs[:4], refs[4:8], refs[8:]
    core, row_first, col_first = info_ref[0], info_ref[1], info_ref[2]
    part = part_ref[0]
    row = row_first + lax.broadcasted_iota(jnp.int32, (256, 256), 0)
    col = col_first + lax.broadcasted_iota(jnp.int32, (256, 256), 1)
    for s in range(4):
        for ref, which in ((own[s], core), (got[s], 1 - core)):
            at = pl.multiple_of(s * 512 + which * 256, 256)
            out_ref[:, pl.ds(at, 256)] = jnp.where(row <= col + at, ref[:256, :] * part, 0.0)
            mean_ref[:, pl.ds(at, 256)] = ref[256:264, :][:1] * part


def finish(info, part, own, got):
    return pl.pallas_call(
        finish_kernel,
        out_shape=(
            jax.ShapeDtypeStruct((1, WIDTH), f32),
            jax.ShapeDtypeStruct((256, WIDTH), f32),
        ),
        in_specs=[pl.BlockSpec(memory_space=pltpu.SMEM)] * 2 + [pl.BlockSpec(memory_space=pltpu.VMEM)] * 8,
        out_specs=(pl.BlockSpec(memory_space=pltpu.VMEM),) * 2,
        compiler_params=params(10),
        name="finish",
    )(info, part, *own, *got)


def swap(value):
    return lax.ppermute(value, "c", [(0, 1), (1, 0)])


def trade(value, axis, flip):
    return lax.ppermute(value, axis, [(i, i ^ flip) for i in range(4)])


def join(*values):
    return jnp.concatenate(values, axis=0)


def meet(value, axis, flip, which):
    got = trade(value, axis, flip)
    return join(jnp.where(which == 0, value, got), jnp.where(which == 0, got, value))


def per_device(resid, norm_gain, keep_index, counts):
    z, x, c, y = (lax.axis_index(a) for a in ("z", "x", "c", "y"))
    place_y = y[None].astype(jnp.int32)
    picked, sums, *turns = pick(place_y, resid, norm_gain.reshape(8, SLOTS), keep_index, counts)
    all_sums = [sums] + [trade(sums, "y", flip) for flip in (1, 2, 3)]
    turns = [trade(turn, "y", flip) for turn, flip in zip(turns, (1, 2, 3))]
    normed = norm(counts, picked, norm_gain[:, None], all_sums)
    pieces = lax.all_to_all(normed, TOK, 0, 0, tiled=True)
    panel = panel_pieces(place_y, picked, turns, all_sums)
    panel = lax.all_to_all(panel, TOK, 0, 0, tiled=True)

    loads = pieces[:, PIECE, 0].astype(jnp.int32)
    first = jnp.cumsum(loads) - loads
    part = 1.0 / jnp.sum(loads).astype(f32)

    streams = list(pack(first, pieces, (16, 16, 16, 16)))
    for step in range(4):
        for s in range(4):
            axis, flip = PARTNERS[(s + step) % 4]
            seen = [PARTNERS[(s + k) % 4][0] for k in range(step)]
            which = side(x if axis == "x" else z, flip, axis not in seen)
            streams[s] = meet(streams[s], axis, flip, which)
        if step == 0:
            panel, _ = lax.optimization_barrier((panel, streams[3][:8, :128]))

    (rows,) = pack(first, panel, (PIECE,))
    rows = meet(rows, "y", 1, side(y, 1, True))
    rows = meet(rows, "y", 3, side(y, 3, False))
    rows = join(rows, swap(rows))

    own, got = [], []
    for s in range(4):
        kept, given = gram(rows, streams[s])
        own.append(kept)
        got.append(swap(given))
    info = jnp.stack([c, (z * 8 + x * 2 + c) * 256, y * WIDTH]).astype(jnp.int32)
    mean, gram_factor = finish(info, part[None], own, got)
    return (mean[0], gram_factor)


def solution(mesh):
    fine = Mesh(mesh.devices.reshape(4, 4, 2, 4), ("z", "x", "c", "y"))
    return jax.shard_map(
        per_device,
        mesh=fine,
        in_specs=(P(TOK, "y"), P("y"), P(TOK), P(TOK)),
        out_specs=(P("y"), P(TOK, "y")),
        check_vma=False,
    )
```

```python
import jax
import jax.numpy as jnp
from jax import lax
from jax.experimental import pallas as pl
from jax.experimental.pallas import tpu as pltpu
from jax.sharding import Mesh, PartitionSpec as P

epsilon = 1e-05
TOK = ("z", "x", "c")
SLOTS = 256
LIVE = 4096
WIDTH = 2048
PIECE = 64
EXTRA = 16
LONG = LIVE + 128
MIB = 1024 * 1024
bf16 = jnp.bfloat16
f32 = jnp.float32


def params(mib):
    return pltpu.CompilerParams(vmem_limit_bytes=mib * MIB)


def spread(value, place):
    high = value.astype(bf16).astype(f32)
    middle = (value - high).astype(bf16).astype(f32)
    low = value - high - middle
    rest = jnp.where(place == 2, low, 0.0)
    return jnp.where(place == 0, high, jnp.where(place == 1, middle, rest))


def pick_kernel(place_ref, index_hbm, counts_hbm, resid_hbm, gain_ref, picked_ref, sums_ref, t1, t2, t3, *scratch):
    index_ref, counts_ref, resid_ref, sem = scratch
    step = 512
    parts = [pl.ds(k * step, step) for k in range(WIDTH // step)]
    small = [
        pltpu.make_async_copy(index_hbm, index_ref, sem.at[0]),
        pltpu.make_async_copy(counts_hbm, counts_ref, sem.at[1]),
    ]
    large = [
        pltpu.make_async_copy(resid_hbm.at[:, part], resid_ref.at[:, part], sem.at[2 + k])
        for k, part in enumerate(parts)
    ]
    for copy in small + large:
        copy.start()
    for copy in small:
        copy.wait()
    tokens = resid_ref.shape[0]
    token = lax.broadcasted_iota(jnp.int32, (tokens, SLOTS), 0)
    slot = lax.broadcasted_iota(jnp.int32, (1, SLOTS), 1)
    half = SLOTS // 2
    end = jnp.where(slot < half, counts_ref[0], half + counts_ref[1])
    kept = jnp.where(slot < end, index_ref[...], -1)
    one_hot = jnp.where(token == kept, 1.0, 0.0).astype(bf16)
    total = jnp.zeros((1, SLOTS), f32)
    for part, copy in zip(parts, large):
        copy.wait()
        product = lax.dot_general(
            resid_ref[:, part], one_hot, (((0,), (0,)), ((), ())), preferred_element_type=f32
        )
        total += jnp.sum(product * product, axis=0, keepdims=True)
        picked_ref[part, :] = product.astype(bf16)
    sums_ref[...] = jnp.broadcast_to(total, (8, SLOTS))
    row = lax.broadcasted_iota(jnp.int32, (EXTRA, SLOTS), 0)
    sum_terms = spread(total, row)
    for flip, ref in ((1, t1), (2, t2), (3, t3)):
        first = pl.multiple_of((place_ref[0] ^ flip) * PIECE, PIECE)
        for k in range(8):
            ref[k, :PIECE, :] = picked_ref[pl.ds(k * 256 + first, PIECE), :]
            terms = jnp.where(row < 3, sum_terms, spread(gain_ref[k : k + 1, :], row - 3))
            ref[k, PIECE:, :] = terms.astype(bf16)


def pick(place, resid, gain, keep_index, counts):
    vmem = pl.BlockSpec(memory_space=pltpu.VMEM)
    smem = pl.BlockSpec(memory_space=pltpu.SMEM)
    hbm = pl.BlockSpec(memory_space=pl.ANY)
    return pl.pallas_call(
        pick_kernel,
        out_shape=(
            jax.ShapeDtypeStruct((WIDTH, SLOTS), bf16),
            jax.ShapeDtypeStruct((8, SLOTS), f32),
        )
        + (jax.ShapeDtypeStruct((8, PIECE + EXTRA, SLOTS), bf16),) * 3,
        in_specs=[smem, hbm, hbm, hbm, vmem],
        out_specs=(vmem,) * 5,
        scratch_shapes=[
            pltpu.VMEM((1, SLOTS), jnp.int32),
            pltpu.SMEM((2,), jnp.int32),
            pltpu.VMEM((512, WIDTH), bf16),
            pltpu.SemaphoreType.DMA((6,)),
        ],
        compiler_params=params(16),
        name="pick",
    )(place, keep_index[None, :], counts, resid, gain)


def whole_terms(ref, k, first):
    terms = ref[k, PIECE:, :].astype(f32)
    return terms[first : first + 1, :] + (terms[first + 1 : first + 2, :] + terms[first + 2 : first + 3, :])


def scale_of(sums, t1, t2, t3):
    squares = (sums[:1, :] + whole_terms(t2, 0, 0)) + (whole_terms(t1, 0, 0) + whole_terms(t3, 0, 0))
    return lax.rsqrt(squares / 8192 + epsilon)


PARTNERS = (("x", 1), ("z", 1), ("x", 3), ("z", 3))


def side(place, flip, first):
    if flip == 1 and not first:
        return (place ^ (place >> 1)) & 1
    return place & 1 if flip == 1 else place >> 1


def slot_of(s, x, z):
    at, seen = 0, []
    for step in range(4):
        axis, flip = PARTNERS[(s + step) % 4]
        at += side(x if axis == "x" else z, flip, axis not in seen) << step
        seen.append(axis)
    return at


def norm_kernel(counts_ref, picked_ref, gain_ref, sums, t1, t2, t3, out_ref):
    scale = scale_of(sums, t1, t2, t3)
    live = (counts_ref[0] + counts_ref[1]).astype(f32)
    extra = jnp.full((EXTRA, SLOTS), live, f32).astype(bf16)
    for s in range(4):
        for c in range(2):
            first = (s * 2 + c) * 256
            rows = picked_ref[first : first + 256, :].astype(f32)
            short = (rows * scale * gain_ref[first : first + 256, :]).astype(bf16)
            for z in range(4):
                for x in range(4):
                    at = slot_of(s, x, z) * 16
                    out_ref[z * 8 + x * 2 + c, s * 16 : (s + 1) * 16, :] = short[at : at + 16, :]
    for t in range(32):
        out_ref[t, PIECE:, :] = extra


def norm(counts, picked, gain, sums, turns):
    return pl.pallas_call(
        norm_kernel,
        out_shape=jax.ShapeDtypeStruct((32, PIECE + EXTRA, SLOTS), bf16),
        in_specs=[pl.BlockSpec(memory_space=pltpu.SMEM)] + [pl.BlockSpec(memory_space=pltpu.VMEM)] * 6,
        out_specs=pl.BlockSpec(memory_space=pltpu.VMEM),
        compiler_params=params(10),
        name="norm",
    )(counts, picked, gain, sums, *turns)


def panel_kernel(place_ref, picked_ref, own_gain_ref, sums, t1, t2, t3, out_ref, gain_ref):
    scale = scale_of(sums, t1, t2, t3)
    y = place_ref[0]
    first = pl.multiple_of(y * PIECE, PIECE)
    for flip, turn in enumerate((None, t1, t2, t3)):
        if turn is None:
            gains = own_gain_ref[...]
        else:
            gains = jnp.concatenate([whole_terms(turn, k, 3) for k in range(8)], axis=0)
        gain_ref[...] = jnp.concatenate([gains, jnp.zeros((120, SLOTS), f32)], axis=0).T
        for k in range(8):
            rows = picked_ref[pl.ds(k * 256 + first, PIECE), :] if turn is None else turn[k, :PIECE, :]
            gain = gain_ref[pl.ds(first, PIECE), :][:, k : k + 1]
            out_ref[(y ^ flip) * 8 + k] = (rows.astype(f32) * scale * gain).astype(bf16)


def panel_pieces(place, picked, gain, sums, turns):
    return pl.pallas_call(
        panel_kernel,
        out_shape=jax.ShapeDtypeStruct((32, PIECE, SLOTS), bf16),
        in_specs=[pl.BlockSpec(memory_space=pltpu.SMEM)] + [pl.BlockSpec(memory_space=pltpu.VMEM)] * 6,
        out_specs=pl.BlockSpec(memory_space=pltpu.VMEM),
        scratch_shapes=[pltpu.VMEM((SLOTS, 128), f32)],
        compiler_params=params(10),
        name="panel",
    )(place, picked, gain, sums, *turns)


def pack_kernel(heights, first_ref, in_ref, *refs):
    out_refs, acc_ref = refs[:-1], refs[-1]
    acc_ref[...] = jnp.zeros_like(acc_ref)
    group = 4

    def body(g, _):
        moved = []
        for k in range(group):
            t = g * group + k
            rows = in_ref[t, :PIECE, :].astype(f32)
            first = first_ref[t]
            base = pl.multiple_of((first // 128) * 128, 128)
            wide = jnp.concatenate([rows, jnp.zeros((PIECE, 128), f32)], axis=1)
            moved.append((base, pltpu.roll(wide, first - base, 1)))
        for base, rows in moved:
            acc_ref[:, pl.ds(base, SLOTS + 128)] += rows
        return 0

    lax.fori_loop(0, 32 // group, body, 0)
    start = 0
    for ref, height in zip(out_refs, heights):
        rows = acc_ref[start : start + height, :LIVE]
        ref[:, :LIVE] = rows.astype(bf16)
        total = jnp.sum(rows, axis=1, keepdims=True)
        lane = lax.broadcasted_iota(jnp.int32, (height, 128), 1)
        ref[:, LIVE:] = spread(total, lane).astype(bf16)
        start += height


def pack(first, pieces, heights):
    return pl.pallas_call(
        lambda *refs: pack_kernel(heights, *refs),
        out_shape=tuple(jax.ShapeDtypeStruct((height, LONG), bf16) for height in heights),
        in_specs=[pl.BlockSpec(memory_space=pltpu.SMEM), pl.BlockSpec(memory_space=pltpu.VMEM)],
        out_specs=(pl.BlockSpec(memory_space=pltpu.VMEM),) * len(heights),
        scratch_shapes=[pltpu.VMEM((PIECE, LIVE + SLOTS + 128), f32)],
        compiler_params=params(10),
        name="pack",
    )(first, pieces)


def gram_kernel(rows_ref, cols_ref, own_ref, given_ref):
    product = lax.dot_general(
        rows_ref[:, :LIVE], cols_ref[:, :LIVE], (((1,), (1,)), ((), ())), preferred_element_type=f32
    )
    own_ref[:256, :] = product[:256]
    given_ref[:256, :] = product[256:]
    lane = lax.broadcasted_iota(jnp.int32, (16, 128), 1)
    terms = jnp.where(lane < 3, 1.0, 0.0).astype(bf16)
    sums = lax.dot_general(
        terms, cols_ref[:, LIVE:], (((1,), (1,)), ((), ())), preferred_element_type=f32
    )
    own_ref[256:, :] = sums[:8]
    given_ref[256:, :] = sums[:8]


def gram(rows, cols):
    return pl.pallas_call(
        gram_kernel,
        out_shape=(jax.ShapeDtypeStruct((264, 256), f32),) * 2,
        in_specs=[pl.BlockSpec(memory_space=pltpu.VMEM)] * 2,
        out_specs=(pl.BlockSpec(memory_space=pltpu.VMEM),) * 2,
        compiler_params=params(10),
        cost_estimate=pl.CostEstimate(
            flops=2 * 512 * 256 * LIVE, bytes_accessed=6 * 1024 * 1024, transcendentals=0
        ),
        name="gram",
    )(rows, cols)


def finish_kernel(info_ref, part_ref, *refs):
    own, got, (mean_ref, out_ref) = refs[:4], refs[4:8], refs[8:]
    core, row_first, col_first = info_ref[0], info_ref[1], info_ref[2]
    part = part_ref[0]
    row = row_first + lax.broadcasted_iota(jnp.int32, (256, 256), 0)
    col = col_first + lax.broadcasted_iota(jnp.int32, (256, 256), 1)
    for s in range(4):

        @pl.when(pl.program_id(0) == s)
        def _():
            for ref, which in ((own[s], core), (got[s], 1 - core)):
                at = pl.multiple_of(which * 256, 256)
                values = jnp.where(row <= col + (s * 512 + at), ref[:256, :] * part, 0.0)
                out_ref[:, pl.ds(at, 256)] = values
                mean_ref[:, pl.ds(at, 256)] = ref[256:264, :][:1] * part


def finish(info, part, own, got):
    vmem = pl.BlockSpec(memory_space=pltpu.VMEM)
    return pl.pallas_call(
        finish_kernel,
        grid=(4,),
        out_shape=(
            jax.ShapeDtypeStruct((1, WIDTH), f32),
            jax.ShapeDtypeStruct((256, WIDTH), f32),
        ),
        in_specs=[pl.BlockSpec(memory_space=pltpu.SMEM)] * 2 + [vmem] * 8,
        out_specs=(pl.BlockSpec((1, 512), lambda s: (0, s)), pl.BlockSpec((256, 512), lambda s: (0, s))),
        compiler_params=params(10),
        name="finish",
    )(info, part, *own, *got)


def swap(value):
    return lax.ppermute(value, "c", [(0, 1), (1, 0)])


def trade(value, axis, flip):
    return lax.ppermute(value, axis, [(i, i ^ flip) for i in range(4)])


def join(*values):
    return jnp.concatenate(values, axis=0)


def meet(value, axis, flip, which):
    got = trade(value, axis, flip)
    return join(jnp.where(which == 0, value, got), jnp.where(which == 0, got, value))


def per_device(resid, norm_gain, keep_index, counts):
    z, x, c, y = (lax.axis_index(a) for a in ("z", "x", "c", "y"))
    place_y = y[None].astype(jnp.int32)
    gain = norm_gain.reshape(8, SLOTS)
    picked, sums, *turns = pick(place_y, resid, gain, keep_index, counts)
    turns = [trade(turn, "y", flip) for turn, flip in zip(turns, (1, 2, 3))]
    normed = norm(counts, picked, norm_gain[:, None], sums, turns)
    pieces = lax.all_to_all(normed, TOK, 0, 0, tiled=True)
    panel = panel_pieces(place_y, picked, gain, sums, turns)
    panel = lax.all_to_all(panel, TOK, 0, 0, tiled=True)

    loads = pieces[:, PIECE, 0].astype(jnp.int32)
    first = jnp.cumsum(loads) - loads
    part = 1.0 / jnp.sum(loads).astype(f32)

    streams = list(pack(first, pieces, (16, 16, 16, 16)))
    for step in range(4):
        for s in range(4):
            axis, flip = PARTNERS[(s + step) % 4]
            seen = [PARTNERS[(s + k) % 4][0] for k in range(step)]
            which = side(x if axis == "x" else z, flip, axis not in seen)
            streams[s] = meet(streams[s], axis, flip, which)
        if step == 0:
            panel = lax.optimization_barrier((panel, *[value[:8, :128] for value in streams]))[0]

    (rows,) = pack(first, panel, (PIECE,))
    rows = meet(rows, "y", 1, side(y, 1, True))
    rows = meet(rows, "y", 3, side(y, 3, False))
    rows = join(rows, swap(rows))

    own, got = [], []
    for s in range(4):
        kept, given = gram(rows, streams[s])
        own.append(kept)
        got.append(swap(given))
    info = jnp.stack([c, (z * 8 + x * 2 + c) * 256, y * WIDTH]).astype(jnp.int32)
    mean, gram_factor = finish(info, part[None], own, got)
    return (mean[0], gram_factor)


def solution(mesh):
    fine = Mesh(mesh.devices.reshape(4, 4, 2, 4), ("z", "x", "c", "y"))
    return jax.shard_map(
        per_device,
        mesh=fine,
        in_specs=(P(TOK, "y"), P("y"), P(TOK), P(TOK)),
        out_specs=(P("y"), P(TOK, "y")),
        check_vma=False,
    )
```

```python
import jax
import jax.numpy as jnp
from jax import lax
from jax.experimental import pallas as pl
from jax.experimental.pallas import tpu as pltpu
from jax.sharding import Mesh, PartitionSpec as P

epsilon = 1e-05
TOK = ("z", "x", "c")
SLOTS = 256
LIVE = 4096
WIDTH = 2048
PIECE = 64
EXTRA = 16
MIB = 1024 * 1024
bf16 = jnp.bfloat16
f32 = jnp.float32


def params(mib):
    return pltpu.CompilerParams(vmem_limit_bytes=mib * MIB)


def spread(value, place):
    high = value.astype(bf16).astype(f32)
    middle = (value - high).astype(bf16).astype(f32)
    low = value - high - middle
    rest = jnp.where(place == 2, low, 0.0)
    return jnp.where(place == 0, high, jnp.where(place == 1, middle, rest))


PARTNERS = (("x", 1), ("z", 1), ("x", 3), ("z", 3))


def side(place, flip, first):
    if flip == 1 and not first:
        return (place ^ (place >> 1)) & 1
    return place & 1 if flip == 1 else place >> 1


def slot_of(s, x, z):
    at, seen = 0, []
    for step in range(4):
        axis, flip = PARTNERS[(s + step) % 4]
        at += side(x if axis == "x" else z, flip, axis not in seen) << step
        seen.append(axis)
    return at


def live_slots(counts_ref):
    slot = lax.broadcasted_iota(jnp.int32, (1, SLOTS), 1)
    half = SLOTS // 2
    return slot < jnp.where(slot < half, counts_ref[0], half + counts_ref[1])


def pick_kernel(place_ref, index_ref, counts_ref, resid_ref, gain_ref, out_ref, *refs):
    turn_refs, picked_ref = refs[:4], refs[4]
    tokens = resid_ref.shape[0]
    token = lax.broadcasted_iota(jnp.int32, (tokens, SLOTS), 0)
    kept = jnp.where(live_slots(counts_ref), index_ref[...], -1)
    one_hot = jnp.where(token == kept, 1.0, 0.0).astype(bf16)
    live = (counts_ref[0] + counts_ref[1]).astype(f32)
    extra = jnp.full((EXTRA, SLOTS), live, f32).astype(bf16)
    for t in range(32):
        out_ref[t, PIECE:, :] = extra
    total = jnp.zeros((1, SLOTS), f32)
    for s in range(4):
        product = lax.dot_general(
            resid_ref[:, s * 512 : (s + 1) * 512],
            one_hot,
            (((0,), (0,)), ((), ())),
            preferred_element_type=f32,
        )
        total += jnp.sum(product * product, axis=0, keepdims=True)
        short = product.astype(bf16)
        picked_ref[s * 512 : (s + 1) * 512, :] = short
        for c in range(2):
            for z in range(4):
                for x in range(4):
                    at = c * 256 + slot_of(s, x, z) * 16
                    out_ref[z * 8 + x * 2 + c, s * 16 : (s + 1) * 16, :] = short[at : at + 16, :]
    row = lax.broadcasted_iota(jnp.int32, (EXTRA, SLOTS), 0)
    sum_terms = spread(total, row)
    for k in range(8):
        terms = jnp.where(row < 3, sum_terms, spread(gain_ref[k : k + 1, :], row - 3)).astype(bf16)
        for flip, ref in enumerate(turn_refs):
            first = pl.multiple_of((place_ref[0] ^ flip) * PIECE, PIECE)
            ref[k, :PIECE, :] = picked_ref[pl.ds(k * 256 + first, PIECE), :]
            ref[k, PIECE:, :] = terms


def pick(place, resid, gain, keep_index, counts):
    vmem = pl.BlockSpec(memory_space=pltpu.VMEM)
    smem = pl.BlockSpec(memory_space=pltpu.SMEM)
    return pl.pallas_call(
        pick_kernel,
        out_shape=(jax.ShapeDtypeStruct((32, PIECE + EXTRA, SLOTS), bf16),)
        + (jax.ShapeDtypeStruct((8, PIECE + EXTRA, SLOTS), bf16),) * 4,
        in_specs=[smem, vmem, smem, vmem, vmem],
        out_specs=(vmem,) * 5,
        scratch_shapes=[pltpu.VMEM((WIDTH, SLOTS), bf16)],
        compiler_params=params(16),
        name="pick",
    )(place, keep_index[None, :], counts, resid, gain)


def whole_terms(ref, k, first):
    terms = ref[k, PIECE:, :].astype(f32)
    return terms[first : first + 1, :] + (terms[first + 1 : first + 2, :] + terms[first + 2 : first + 3, :])


def panel_kernel(place_ref, counts_ref, t0, t1, t2, t3, out_ref, gain_ref):
    sums = [whole_terms(ref, 0, 0) for ref in (t0, t1, t2, t3)]
    scale = lax.rsqrt(((sums[0] + sums[2]) + (sums[1] + sums[3])) / 8192 + epsilon)
    row = lax.broadcasted_iota(jnp.int32, (EXTRA, SLOTS), 0)
    extra = spread(jnp.where(live_slots(counts_ref), scale, 0.0), row).astype(bf16)
    y = place_ref[0]
    first = pl.multiple_of(y * PIECE, PIECE)
    for flip, turn in enumerate((t0, t1, t2, t3)):
        gains = [whole_terms(turn, k, 3) for k in range(8)]
        gain_ref[...] = jnp.concatenate(gains + [jnp.zeros((120, SLOTS), f32)], axis=0).T
        for k in range(8):
            gain = gain_ref[pl.ds(first, PIECE), :][:, k : k + 1]
            rows = turn[k, :PIECE, :].astype(f32)
            out_ref[(y ^ flip) * 8 + k, :PIECE, :] = (rows * scale * gain).astype(bf16)
            out_ref[(y ^ flip) * 8 + k, PIECE:, :] = extra


def panel_pieces(place, counts, turns):
    return pl.pallas_call(
        panel_kernel,
        out_shape=jax.ShapeDtypeStruct((32, PIECE + EXTRA, SLOTS), bf16),
        in_specs=[pl.BlockSpec(memory_space=pltpu.SMEM)] * 2 + [pl.BlockSpec(memory_space=pltpu.VMEM)] * 4,
        out_specs=pl.BlockSpec(memory_space=pltpu.VMEM),
        scratch_shapes=[pltpu.VMEM((SLOTS, 128), f32)],
        compiler_params=params(10),
        name="panel",
    )(place, counts, *turns)


def pack_kernel(heights, scales, first_ref, in_ref, *refs):
    acc_ref, out_refs = refs[-1], refs[-1 - len(heights) - scales : -1]
    n_rows = acc_ref.shape[0]
    acc_ref[...] = jnp.zeros_like(acc_ref)
    group = 4

    def body(g, _):
        moved = []
        for k in range(group):
            t = g * group + k
            rows = in_ref[t, :n_rows, :].astype(f32)
            first = first_ref[t]
            base = pl.multiple_of((first // 128) * 128, 128)
            wide = jnp.concatenate([rows, jnp.zeros((n_rows, 128), f32)], axis=1)
            moved.append((base, pltpu.roll(wide, first - base, 1)))
        for base, rows in moved:
            acc_ref[:, pl.ds(base, SLOTS + 128)] += rows
        return 0

    lax.fori_loop(0, 32 // group, body, 0)
    start = 0
    for ref, height in zip(out_refs, heights):
        ref[...] = acc_ref[start : start + height, :LIVE].astype(bf16)
        start += height
    if scales:
        terms = acc_ref[PIECE : PIECE + 8, :LIVE]
        scale = terms[0:1, :] + (terms[1:2, :] + terms[2:3, :])
        out_refs[-1][...] = jnp.broadcast_to(scale, (8, LIVE))


def pack(first, pieces, heights, scales=False, after=()):
    vmem = pl.BlockSpec(memory_space=pltpu.VMEM)
    n_rows = PIECE + EXTRA if scales else PIECE
    out_shape = [jax.ShapeDtypeStruct((height, LIVE), bf16) for height in heights]
    if scales:
        out_shape.append(jax.ShapeDtypeStruct((8, LIVE), f32))
    return pl.pallas_call(
        lambda *refs: pack_kernel(heights, scales, *refs),
        out_shape=tuple(out_shape),
        in_specs=[pl.BlockSpec(memory_space=pltpu.SMEM), vmem]
        + [pl.BlockSpec(memory_space=pl.ANY)] * len(after),
        out_specs=(vmem,) * len(out_shape),
        scratch_shapes=[pltpu.VMEM((n_rows, LIVE + SLOTS + 128), f32)],
        compiler_params=params(10),
        name="pack",
    )(first, pieces, *after)


def gram_kernel(rows_ref, cols_ref, scale_ref, gain_ref, own_ref, given_ref):
    normed = (cols_ref[...].astype(f32) * scale_ref[0:1, :] * gain_ref[...]).astype(bf16)
    product = lax.dot_general(
        rows_ref[...], normed, (((1,), (1,)), ((), ())), preferred_element_type=f32
    )
    own_ref[:256, :] = product[:256]
    given_ref[:256, :] = product[256:]
    sums = jnp.sum(normed.astype(f32), axis=1, keepdims=True)
    sums = jnp.broadcast_to(sums, (256, 128)).T[:8, :]
    own_ref[256:, :] = sums
    given_ref[256:, :] = sums


def gram(rows, cols, scale, gain):
    return pl.pallas_call(
        gram_kernel,
        out_shape=(jax.ShapeDtypeStruct((264, 256), f32),) * 2,
        in_specs=[pl.BlockSpec(memory_space=pltpu.VMEM)] * 4,
        out_specs=(pl.BlockSpec(memory_space=pltpu.VMEM),) * 2,
        compiler_params=params(16),
        cost_estimate=pl.CostEstimate(
            flops=2 * 512 * 256 * LIVE, bytes_accessed=6 * 1024 * 1024, transcendentals=0
        ),
        name="gram",
    )(rows, cols, scale, gain)


def finish_kernel(info_ref, part_ref, *refs):
    own, got, (mean_ref, out_ref) = refs[:4], refs[4:8], refs[8:]
    core, row_first, col_first = info_ref[0], info_ref[1], info_ref[2]
    part = part_ref[0]
    row = row_first + lax.broadcasted_iota(jnp.int32, (256, 256), 0)
    col = col_first + lax.broadcasted_iota(jnp.int32, (256, 256), 1)
    for s in range(4):

        @pl.when(pl.program_id(0) == s)
        def _():
            for ref, which in ((own[s], core), (got[s], 1 - core)):
                at = pl.multiple_of(which * 256, 256)
                values = jnp.where(row <= col + (s * 512 + at), ref[:256, :] * part, 0.0)
                out_ref[:, pl.ds(at, 256)] = values
                mean_ref[:, pl.ds(at, 256)] = ref[256:264, :][:1] * part


def finish(info, part, own, got):
    vmem = pl.BlockSpec(memory_space=pltpu.VMEM)
    return pl.pallas_call(
        finish_kernel,
        grid=(4,),
        out_shape=(
            jax.ShapeDtypeStruct((1, WIDTH), f32),
            jax.ShapeDtypeStruct((256, WIDTH), f32),
        ),
        in_specs=[pl.BlockSpec(memory_space=pltpu.SMEM)] * 2 + [vmem] * 8,
        out_specs=(pl.BlockSpec((1, 512), lambda s: (0, s)), pl.BlockSpec((256, 512), lambda s: (0, s))),
        compiler_params=params(10),
        name="finish",
    )(info, part, *own, *got)


def swap(value):
    return lax.ppermute(value, "c", [(0, 1), (1, 0)])


def trade(value, axis, flip):
    return lax.ppermute(value, axis, [(i, i ^ flip) for i in range(4)])


def join(*values):
    return jnp.concatenate(values, axis=0)


def meet(value, axis, flip, which):
    got = trade(value, axis, flip)
    return join(jnp.where(which == 0, value, got), jnp.where(which == 0, got, value))


def per_device(resid, norm_gain, keep_index, counts):
    z, x, c, y = (lax.axis_index(a) for a in ("z", "x", "c", "y"))
    place_y = y[None].astype(jnp.int32)
    pieces, *turns = pick(place_y, resid, norm_gain.reshape(8, SLOTS), keep_index, counts)
    pieces = lax.all_to_all(pieces, TOK, 0, 0, tiled=True)
    turns = [turns[0]] + [trade(turns[flip], "y", flip) for flip in (1, 2, 3)]
    panel = lax.all_to_all(panel_pieces(place_y, counts, turns), TOK, 0, 0, tiled=True)

    loads = pieces[:, PIECE, 0].astype(jnp.int32)
    first = jnp.cumsum(loads) - loads
    part = 1.0 / jnp.sum(loads).astype(f32)

    streams = list(pack(first, pieces, (16, 16, 16, 16)))
    for step in range(4):
        for s in range(4):
            axis, flip = PARTNERS[(s + step) % 4]
            seen = [PARTNERS[(s + k) % 4][0] for k in range(step)]
            which = side(x if axis == "x" else z, flip, axis not in seen)
            streams[s] = meet(streams[s], axis, flip, which)
        if step == 1:
            rows, scale = pack(first, panel, (PIECE,), scales=True, after=streams)

    rows = meet(rows, "y", 1, side(y, 1, True))
    rows = meet(rows, "y", 3, side(y, 3, False))
    rows = join(rows, swap(rows))

    gains = lax.dynamic_index_in_dim(norm_gain.reshape(4, 2, 256), c, 1, keepdims=False)[:, :, None]
    own, got = [], []
    for s in range(4):
        kept, given = gram(rows, streams[s], scale, gains[s])
        own.append(kept)
        got.append(swap(given))
    info = jnp.stack([c, (z * 8 + x * 2 + c) * 256, y * WIDTH]).astype(jnp.int32)
    mean, gram_factor = finish(info, part[None], own, got)
    return (mean[0], gram_factor)


def solution(mesh):
    fine = Mesh(mesh.devices.reshape(4, 4, 2, 4), ("z", "x", "c", "y"))
    return jax.shard_map(
        per_device,
        mesh=fine,
        in_specs=(P(TOK, "y"), P("y"), P(TOK), P(TOK)),
        out_specs=(P("y"), P(TOK, "y")),
        check_vma=False,
    )
```

```python
import jax
import jax.numpy as jnp
from jax import lax
from jax.experimental import pallas as pl
from jax.experimental.pallas import tpu as pltpu
from jax.sharding import Mesh, PartitionSpec as P

epsilon = 1e-05
TOK = ("z", "x", "c")
SLOTS = 256
LIVE = 4096
WIDTH = 2048
PIECE = 64
EXTRA = 16
MIB = 1024 * 1024
bf16 = jnp.bfloat16
f32 = jnp.float32


def params(mib):
    return pltpu.CompilerParams(vmem_limit_bytes=mib * MIB)


def spread(value, place):
    high = value.astype(bf16).astype(f32)
    middle = (value - high).astype(bf16).astype(f32)
    low = value - high - middle
    rest = jnp.where(place == 2, low, 0.0)
    return jnp.where(place == 0, high, jnp.where(place == 1, middle, rest))


PARTNERS = (("x", 1), ("z", 1), ("x", 3), ("z", 3))


def side(place, flip, first):
    if flip == 1 and not first:
        return (place ^ (place >> 1)) & 1
    return place & 1 if flip == 1 else place >> 1


def slot_of(s, x, z):
    at, seen = 0, []
    for step in range(4):
        axis, flip = PARTNERS[(s + step) % 4]
        at += side(x if axis == "x" else z, flip, axis not in seen) << step
        seen.append(axis)
    return at


def live_slots(counts_ref):
    slot = lax.broadcasted_iota(jnp.int32, (1, SLOTS), 1)
    half = SLOTS // 2
    return slot < jnp.where(slot < half, counts_ref[0], half + counts_ref[1])


def pick_kernel(index_ref, counts_ref, resid_ref, out_ref, picked_ref, sums_ref):
    tokens = resid_ref.shape[0]
    token = lax.broadcasted_iota(jnp.int32, (tokens, SLOTS), 0)
    live = live_slots(counts_ref)
    kept = jnp.where(live, index_ref[...], -1)
    one_hot = jnp.where(token == kept, 1.0, 0.0).astype(bf16)
    row = lax.broadcasted_iota(jnp.int32, (16, 1), 0)
    mark = jnp.where(row == 0, jnp.where(live, 0.0, jnp.inf), 0.0).astype(bf16)
    total = jnp.zeros((1, SLOTS), f32)
    for s in range(4):
        product = lax.dot_general(
            resid_ref[:, s * 512 : (s + 1) * 512],
            one_hot,
            (((0,), (0,)), ((), ())),
            preferred_element_type=f32,
        )
        total += jnp.sum(product * product, axis=0, keepdims=True)
        short = product.astype(bf16)
        picked_ref[s * 512 : (s + 1) * 512, :] = short
        for c in range(2):
            for z in range(4):
                for x in range(4):
                    at = c * 256 + slot_of(s, x, z) * 16
                    part = short[at : at + 16, :]
                    out_ref[z * 8 + x * 2 + c, s * 16 : (s + 1) * 16, :] = part + mark if s == 0 else part
    sums_ref[...] = jnp.broadcast_to(total, (8, SLOTS))


def pick(resid, keep_index, counts):
    vmem = pl.BlockSpec(memory_space=pltpu.VMEM)
    smem = pl.BlockSpec(memory_space=pltpu.SMEM)
    return pl.pallas_call(
        pick_kernel,
        out_shape=(
            jax.ShapeDtypeStruct((32, PIECE, SLOTS), bf16),
            jax.ShapeDtypeStruct((WIDTH, SLOTS), bf16),
            jax.ShapeDtypeStruct((8, SLOTS), f32),
        ),
        in_specs=[vmem, smem, vmem],
        out_specs=(vmem,) * 3,
        compiler_params=params(16),
        name="pick",
    )(keep_index[None, :], counts, resid)


def turn_kernel(place_ref, picked_ref, sums_ref, gain_ref, *turn_refs):
    row = lax.broadcasted_iota(jnp.int32, (EXTRA, SLOTS), 0)
    sum_terms = spread(sums_ref[:1, :], row)
    for k in range(8):
        gain = gain_ref[:, k * 256 : (k + 1) * 256]
        terms = jnp.where(row < 3, sum_terms, spread(gain, row - 3)).astype(bf16)
        for flip, ref in enumerate(turn_refs):
            low, high = panel_rows(place_ref[0] ^ flip)
            ref[k, :32, :] = picked_ref[pl.ds(k * 256 + low, 32), :]
            ref[k, 32:PIECE, :] = picked_ref[pl.ds(k * 256 + high, 32), :]
            ref[k, PIECE:, :] = terms


def turn(place, picked, sums, gain):
    vmem = pl.BlockSpec(memory_space=pltpu.VMEM)
    return pl.pallas_call(
        turn_kernel,
        out_shape=(jax.ShapeDtypeStruct((8, PIECE + EXTRA, SLOTS), bf16),) * 4,
        in_specs=[pl.BlockSpec(memory_space=pltpu.SMEM)] + [vmem] * 3,
        out_specs=(vmem,) * 4,
        compiler_params=params(10),
        name="turn",
    )(place, picked, sums, gain)


def panel_rows(q):
    return pl.multiple_of(q * 32, 32), pl.multiple_of(128 + (side(q, 1, False) * 2 + side(q, 3, True)) * 32, 32)


def whole_terms(ref, k, first):
    terms = ref[k, PIECE:, :].astype(f32)
    return terms[first : first + 1, :] + (terms[first + 1 : first + 2, :] + terms[first + 2 : first + 3, :])


def panel_kernel(place_ref, counts_ref, t0, t1, t2, t3, *refs):
    out_ref, gain_ref = refs[-2:]
    sums = [whole_terms(ref, 0, 0) for ref in (t0, t1, t2, t3)]
    scale = lax.rsqrt(((sums[0] + sums[2]) + (sums[1] + sums[3])) / 8192 + epsilon)
    row = lax.broadcasted_iota(jnp.int32, (EXTRA, SLOTS), 0)
    extra = spread(jnp.where(live_slots(counts_ref), scale, 0.0), row).astype(bf16)
    y = place_ref[0]
    low, high = panel_rows(y)
    for flip, turn in enumerate((t0, t1, t2, t3)):
        gains = [whole_terms(turn, k, 3) for k in range(8)]
        gain_ref[...] = jnp.concatenate(gains + [jnp.zeros((120, SLOTS), f32)], axis=0).T
        for k in range(8):
            for at, first in ((0, low), (32, high)):
                gain = gain_ref[pl.ds(first, 32), :][:, k : k + 1]
                rows = turn[k, at : at + 32, :].astype(f32)
                out_ref[(y ^ flip) * 8 + k, at : at + 32, :] = (rows * scale * gain).astype(bf16)
            out_ref[(y ^ flip) * 8 + k, PIECE:, :] = extra


def panel_pieces(place, counts, turns, after):
    return pl.pallas_call(
        panel_kernel,
        out_shape=jax.ShapeDtypeStruct((32, PIECE + EXTRA, SLOTS), bf16),
        in_specs=[pl.BlockSpec(memory_space=pltpu.SMEM)] * 2
        + [pl.BlockSpec(memory_space=pltpu.VMEM)] * 4
        + [pl.BlockSpec(memory_space=pl.ANY)] * len(after),
        out_specs=pl.BlockSpec(memory_space=pltpu.VMEM),
        scratch_shapes=[pltpu.VMEM((SLOTS, 128), f32)],
        compiler_params=params(10),
        name="panel",
    )(place, counts, *turns, *after)


def pack_kernel(heights, scales, first_ref, in_ref, *refs):
    acc_ref, out_refs = refs[-1], refs[-1 - len(heights) - scales : -1]
    n_rows = acc_ref.shape[0]
    acc_ref[...] = jnp.zeros_like(acc_ref)
    group = 4

    def body(g, _):
        moved = []
        for k in range(group):
            t = g * group + k
            rows = in_ref[t, :n_rows, :].astype(f32)
            rows = jnp.where(rows < jnp.inf, rows, 0.0)
            first = first_ref[t]
            base = pl.multiple_of((first // 128) * 128, 128)
            wide = jnp.concatenate([rows, jnp.zeros((n_rows, 128), f32)], axis=1)
            moved.append((base, pltpu.roll(wide, first - base, 1)))
        for base, rows in moved:
            acc_ref[:, pl.ds(base, SLOTS + 128)] += rows
        return 0

    lax.fori_loop(0, 32 // group, body, 0)
    start = 0
    for ref, height in zip(out_refs, heights):
        ref[...] = acc_ref[start : start + height, :LIVE].astype(bf16)
        start += height
    if scales:
        terms = acc_ref[PIECE : PIECE + 8, :LIVE]
        scale = terms[0:1, :] + (terms[1:2, :] + terms[2:3, :])
        out_refs[-1][...] = jnp.broadcast_to(scale, (8, LIVE))


def pack(first, pieces, heights, scales=False):
    vmem = pl.BlockSpec(memory_space=pltpu.VMEM)
    n_rows = PIECE + EXTRA if scales else PIECE
    out_shape = [jax.ShapeDtypeStruct((height, LIVE), bf16) for height in heights]
    if scales:
        out_shape.append(jax.ShapeDtypeStruct((8, LIVE), f32))
    return pl.pallas_call(
        lambda *refs: pack_kernel(heights, scales, *refs),
        out_shape=tuple(out_shape),
        in_specs=[pl.BlockSpec(memory_space=pltpu.SMEM), vmem],
        out_specs=(vmem,) * len(out_shape),
        scratch_shapes=[pltpu.VMEM((n_rows, LIVE + SLOTS + 128), f32)],
        compiler_params=params(10),
        name="pack",
    )(first, pieces)


def gram_kernel(rows_ref, cols_ref, scale_ref, gain_ref, own_ref, given_ref):
    normed = (cols_ref[...].astype(f32) * scale_ref[0:1, :] * gain_ref[...]).astype(bf16)
    product = lax.dot_general(
        rows_ref[...], normed, (((1,), (1,)), ((), ())), preferred_element_type=f32
    )
    own_ref[:256, :] = product[:256]
    given_ref[:256, :] = product[256:]
    sums = jnp.sum(normed.astype(f32), axis=1, keepdims=True)
    sums = jnp.broadcast_to(sums, (256, 128)).T[:8, :]
    own_ref[256:, :] = sums
    given_ref[256:, :] = sums


def gram(rows, cols, scale, gain):
    return pl.pallas_call(
        gram_kernel,
        out_shape=(jax.ShapeDtypeStruct((264, 256), f32),) * 2,
        in_specs=[pl.BlockSpec(memory_space=pltpu.VMEM)] * 4,
        out_specs=(pl.BlockSpec(memory_space=pltpu.VMEM),) * 2,
        compiler_params=params(16),
        cost_estimate=pl.CostEstimate(
            flops=2 * 512 * 256 * LIVE, bytes_accessed=6 * 1024 * 1024, transcendentals=0
        ),
        name="gram",
    )(rows, cols, scale, gain)


def finish_kernel(info_ref, part_ref, *refs):
    own, got, (mean_ref, out_ref) = refs[:4], refs[4:8], refs[8:]
    core, row_first, col_first = info_ref[0], info_ref[1], info_ref[2]
    part = part_ref[0]
    row = row_first + lax.broadcasted_iota(jnp.int32, (256, 256), 0)
    col = col_first + lax.broadcasted_iota(jnp.int32, (256, 256), 1)
    for s in range(4):

        @pl.when(pl.program_id(0) == s)
        def _():
            for ref, which in ((own[s], core), (got[s], 1 - core)):
                at = pl.multiple_of(which * 256, 256)
                values = jnp.where(row <= col + (s * 512 + at), ref[:256, :] * part, 0.0)
                out_ref[:, pl.ds(at, 256)] = values
                mean_ref[:, pl.ds(at, 256)] = ref[256:264, :][:1] * part


def finish(info, part, own, got):
    vmem = pl.BlockSpec(memory_space=pltpu.VMEM)
    return pl.pallas_call(
        finish_kernel,
        grid=(4,),
        out_shape=(
            jax.ShapeDtypeStruct((1, WIDTH), f32),
            jax.ShapeDtypeStruct((256, WIDTH), f32),
        ),
        in_specs=[pl.BlockSpec(memory_space=pltpu.SMEM)] * 2 + [vmem] * 8,
        out_specs=(pl.BlockSpec((1, 512), lambda s: (0, s)), pl.BlockSpec((256, 512), lambda s: (0, s))),
        compiler_params=params(10),
        name="finish",
    )(info, part, *own, *got)


def swap(value):
    return lax.ppermute(value, "c", [(0, 1), (1, 0)])


def trade(value, axis, flip):
    return lax.ppermute(value, axis, [(i, i ^ flip) for i in range(4)])


def join(*values):
    return jnp.concatenate(values, axis=0)


def meet(value, axis, flip, which):
    got = trade(value, axis, flip)
    return join(jnp.where(which == 0, value, got), jnp.where(which == 0, got, value))


def per_device(resid, norm_gain, keep_index, counts):
    z, x, c, y = (lax.axis_index(a) for a in ("z", "x", "c", "y"))
    place_y = y[None].astype(jnp.int32)
    pieces, picked, sums = pick(resid, keep_index, counts)
    pieces = lax.all_to_all(pieces, TOK, 0, 0, tiled=True)
    turns = turn(place_y, picked, sums, norm_gain[None, :])
    turns = [turns[0]] + [trade(turns[flip], "y", flip) for flip in (1, 2, 3)]

    loads = jnp.sum((pieces[:, 0, :] < jnp.inf).astype(jnp.int32), axis=1)
    first = jnp.cumsum(loads) - loads
    part = 1.0 / jnp.sum(loads).astype(f32)

    streams = list(pack(first, pieces, (16, 16, 16, 16)))
    for step in range(4):
        for s in range(4):
            axis, flip = PARTNERS[(s + step) % 4]
            seen = [PARTNERS[(s + k) % 4][0] for k in range(step)]
            which = side(x if axis == "x" else z, flip, axis not in seen)
            streams[s] = meet(streams[s], axis, flip, which)
        if step == 1:
            panel = panel_pieces(place_y, counts, turns, after=streams)
            panel = lax.all_to_all(panel, TOK, 0, 0, tiled=True)

    low, high, scale = pack(first, panel, (32, 32), scales=True)
    low, high = meet(low, "y", 1, side(y, 1, True)), meet(high, "y", 3, side(y, 3, True))
    low, high = meet(low, "y", 3, side(y, 3, False)), meet(high, "y", 1, side(y, 1, False))
    rows = join(low, high)
    rows = join(rows, swap(rows))

    gains = lax.dynamic_index_in_dim(norm_gain.reshape(4, 2, 256), c, 1, keepdims=False)[:, :, None]
    own, got = [], []
    for s in range(4):
        kept, given = gram(rows, streams[s], scale, gains[s])
        own.append(kept)
        got.append(swap(given))
    info = jnp.stack([c, (z * 8 + x * 2 + c) * 256, y * WIDTH]).astype(jnp.int32)
    mean, gram_factor = finish(info, part[None], own, got)
    return (mean[0], gram_factor)


def solution(mesh):
    fine = Mesh(mesh.devices.reshape(4, 4, 2, 4), ("z", "x", "c", "y"))
    return jax.shard_map(
        per_device,
        mesh=fine,
        in_specs=(P(TOK, "y"), P("y"), P(TOK), P(TOK)),
        out_specs=(P("y"), P(TOK, "y")),
        check_vma=False,
    )
```

```python
import jax
import jax.numpy as jnp
from jax import lax
from jax.experimental import pallas as pl
from jax.experimental.pallas import tpu as pltpu
from jax.sharding import Mesh, PartitionSpec as P

epsilon = 1e-05
TOK = ("z", "x", "c")
SLOTS = 256
LIVE = 4096
WIDTH = 2048
PIECE = 64
LONG = LIVE + 128
MIB = 1024 * 1024
bf16 = jnp.bfloat16
f32 = jnp.float32


def params(mib):
    return pltpu.CompilerParams(vmem_limit_bytes=mib * MIB)


def spread(value, place):
    high = value.astype(bf16).astype(f32)
    middle = (value - high).astype(bf16).astype(f32)
    low = value - high - middle
    rest = jnp.where(place == 2, low, 0.0)
    return jnp.where(place == 0, high, jnp.where(place == 1, middle, rest))


PARTNERS = (("x", 1), ("z", 1), ("x", 3), ("z", 3))


def side(place, flip, first):
    if flip == 1 and not first:
        return (place ^ (place >> 1)) & 1
    return place & 1 if flip == 1 else place >> 1


def slot_of(s, x, z):
    at, seen = 0, []
    for step in range(4):
        axis, flip = PARTNERS[(s + step) % 4]
        at += side(x if axis == "x" else z, flip, axis not in seen) << step
        seen.append(axis)
    return at


def live_slots(counts_ref):
    slot = lax.broadcasted_iota(jnp.int32, (1, SLOTS), 1)
    half = SLOTS // 2
    return slot < jnp.where(slot < half, counts_ref[0], half + counts_ref[1])


def second_place(q):
    return side(q, 1, False) * 2 + side(q, 3, True)


def pick_kernel(index_ref, counts_ref, resid_ref, picked_ref, sums_ref):
    tokens = resid_ref.shape[0]
    token = lax.broadcasted_iota(jnp.int32, (tokens, SLOTS), 0)
    kept = jnp.where(live_slots(counts_ref), index_ref[...], -1)
    one_hot = jnp.where(token == kept, 1.0, 0.0).astype(bf16)
    total = jnp.zeros((1, SLOTS), f32)
    step = 512
    for k in range(WIDTH // step):
        part = lax.dot_general(
            resid_ref[:, k * step : (k + 1) * step],
            one_hot,
            (((0,), (0,)), ((), ())),
            preferred_element_type=f32,
        )
        total += jnp.sum(part * part, axis=0, keepdims=True)
        picked_ref[k * step : (k + 1) * step, :] = part.astype(bf16)
    sums_ref[...] = jnp.broadcast_to(total, sums_ref.shape)


def pick(resid, keep_index, counts):
    vmem = pl.BlockSpec(memory_space=pltpu.VMEM)
    return pl.pallas_call(
        pick_kernel,
        out_shape=(
            jax.ShapeDtypeStruct((WIDTH, SLOTS), bf16),
            jax.ShapeDtypeStruct((8, SLOTS), f32),
        ),
        in_specs=[vmem, pl.BlockSpec(memory_space=pltpu.SMEM), vmem],
        out_specs=(vmem,) * 2,
        compiler_params=params(16),
        name="pick",
    )(keep_index[None, :], counts, resid)


def norm_kernel(counts_ref, picked_ref, gain_ref, s0, s1, s2, s3, out_ref):
    squares = (s0[:1, :] + s2[:1, :]) + (s1[:1, :] + s3[:1, :])
    scale = lax.rsqrt(squares / 8192 + epsilon)
    row = lax.broadcasted_iota(jnp.int32, (32, 1), 0)
    mark = jnp.where(row == 0, jnp.where(live_slots(counts_ref), 0.0, jnp.inf), 0.0).astype(bf16)
    for x in range(4):
        for c in range(2):
            first = (x * 2 + c) * 256
            rows = picked_ref[first : first + 256, :].astype(f32)
            short = (rows * scale * gain_ref[first : first + 256, :]).astype(bf16)
            for z in range(4):
                low, high = z * 32, 128 + second_place(z) * 32
                out_ref[z * 8 + x * 2 + c, :32, :] = short[low : low + 32, :] + mark
                out_ref[z * 8 + x * 2 + c, 32:, :] = short[high : high + 32, :]


def norm(counts, picked, gain, sums):
    return pl.pallas_call(
        norm_kernel,
        out_shape=jax.ShapeDtypeStruct((32, PIECE, SLOTS), bf16),
        in_specs=[pl.BlockSpec(memory_space=pltpu.SMEM)] + [pl.BlockSpec(memory_space=pltpu.VMEM)] * 6,
        out_specs=pl.BlockSpec(memory_space=pltpu.VMEM),
        compiler_params=params(10),
        name="norm",
    )(counts, picked, gain, *sums)


def pack_kernel(first_ref, in_ref, *refs):
    out_refs, acc_ref = refs[:-1], refs[-1]
    acc_ref[...] = jnp.zeros_like(acc_ref)
    group = 4

    def body(g, _):
        moved = []
        for k in range(group):
            t = g * group + k
            rows = in_ref[t].astype(f32)
            rows = jnp.where(rows < jnp.inf, rows, 0.0)
            first = first_ref[t]
            base = pl.multiple_of((first // 128) * 128, 128)
            wide = jnp.concatenate([rows, jnp.zeros((PIECE, 128), f32)], axis=1)
            moved.append((base, pltpu.roll(wide, first - base, 1)))
        for base, rows in moved:
            acc_ref[:, pl.ds(base, SLOTS + 128)] += rows
        return 0

    lax.fori_loop(0, 32 // group, body, 0)
    whole_ref, part_refs = out_refs[0], out_refs[1:]
    rows = acc_ref[:, :LIVE]
    whole_ref[:, :LIVE] = rows.astype(bf16)
    lane = lax.broadcasted_iota(jnp.int32, (PIECE, 128), 1)
    whole_ref[:, LIVE:] = spread(jnp.sum(rows, axis=1, keepdims=True), lane).astype(bf16)
    for k, ref in enumerate(part_refs):
        ref[...] = whole_ref[k * 16 : (k + 1) * 16, :]


def pack(first, pieces):
    vmem = pl.BlockSpec(memory_space=pltpu.VMEM)
    return pl.pallas_call(
        pack_kernel,
        out_shape=(jax.ShapeDtypeStruct((PIECE, LONG), bf16),)
        + (jax.ShapeDtypeStruct((16, LONG), bf16),) * 4,
        in_specs=[pl.BlockSpec(memory_space=pltpu.SMEM), vmem],
        out_specs=(vmem,) * 5,
        scratch_shapes=[pltpu.VMEM((PIECE, LIVE + SLOTS + 128), f32)],
        compiler_params=params(10),
        name="pack",
    )(first, pieces)


def gram_kernel(blocks, rows_ref, *refs):
    streams, (own_ref, given_ref, cols_ref) = refs[:4], refs[4:]
    lane = lax.broadcasted_iota(jnp.int32, (16, 128), 1)
    terms = jnp.where(lane < 3, 1.0, 0.0).astype(bf16)
    for n, x in enumerate(blocks):
        for z in range(4):
            for s in range(4):
                at = (z if s < 2 else 4 + second_place(z)) * 32 + s % 2 * 16
                first = slot_of(s, x, z) * 16
                cols_ref[n * 256 + at : n * 256 + at + 16, :] = streams[s][first : first + 16, :]
        inside = slice(n * 256, (n + 1) * 256)
        product = lax.dot_general(
            rows_ref[:, :LIVE],
            cols_ref[inside, :LIVE],
            (((1,), (1,)), ((), ())),
            preferred_element_type=f32,
        )
        own_ref[:256, inside] = product[:256]
        given_ref[:256, inside] = product[256:]
        sums = lax.dot_general(
            terms, cols_ref[inside, LIVE:], (((1,), (1,)), ((), ())), preferred_element_type=f32
        )
        own_ref[256:, inside] = sums[:8]
        given_ref[256:, inside] = sums[:8]


def gram(blocks, rows, streams):
    vmem = pl.BlockSpec(memory_space=pltpu.VMEM)
    width = 256 * len(blocks)
    return pl.pallas_call(
        lambda *refs: gram_kernel(blocks, *refs),
        out_shape=(jax.ShapeDtypeStruct((264, width), f32),) * 2,
        in_specs=[vmem] * 5,
        out_specs=(vmem,) * 2,
        scratch_shapes=[pltpu.VMEM((width, LONG), bf16)],
        compiler_params=params(10),
        cost_estimate=pl.CostEstimate(
            flops=2 * 512 * width * LIVE, bytes_accessed=6 * 1024 * 1024, transcendentals=0
        ),
        name="gram",
    )(rows, *streams)


def finish_kernel(info_ref, part_ref, *refs):
    own, got, (mean_ref, out_ref) = refs[:2], refs[2:4], refs[4:]
    core, row_first, col_first = info_ref[0], info_ref[1], info_ref[2]
    part = part_ref[0]
    row = row_first + lax.broadcasted_iota(jnp.int32, (256, 256), 0)
    col = col_first + lax.broadcasted_iota(jnp.int32, (256, 256), 1)
    for x in range(4):
        inside = slice(x % 2 * 256, (x % 2 + 1) * 256)
        for ref, which in ((own[x // 2], core), (got[x // 2], 1 - core)):
            at = pl.multiple_of(x * 512 + which * 256, 256)
            out_ref[:, pl.ds(at, 256)] = jnp.where(row <= col + at, ref[:256, inside] * part, 0.0)
            mean_ref[:, pl.ds(at, 256)] = ref[256:264, inside][:1] * part


def finish(info, part, own, got):
    vmem = pl.BlockSpec(memory_space=pltpu.VMEM)
    return pl.pallas_call(
        finish_kernel,
        out_shape=(
            jax.ShapeDtypeStruct((1, WIDTH), f32),
            jax.ShapeDtypeStruct((256, WIDTH), f32),
        ),
        in_specs=[pl.BlockSpec(memory_space=pltpu.SMEM)] * 2 + [vmem] * 4,
        out_specs=(vmem,) * 2,
        compiler_params=params(10),
        name="finish",
    )(info, part, *own, *got)


def swap(value):
    return lax.ppermute(value, "c", [(0, 1), (1, 0)])


def trade(value, axis, flip):
    return lax.ppermute(value, axis, [(i, i ^ flip) for i in range(4)])


def join(*values):
    return jnp.concatenate(values, axis=0)


def meet(value, axis, flip, which):
    got = trade(value, axis, flip)
    return join(jnp.where(which == 0, value, got), jnp.where(which == 0, got, value))


def per_device(resid, norm_gain, keep_index, counts):
    z, x, c, y = (lax.axis_index(a) for a in ("z", "x", "c", "y"))
    picked, sums = pick(resid, keep_index, counts)
    all_sums = [sums] + [trade(sums, "y", flip) for flip in (1, 2, 3)]
    pieces = norm(counts, picked, norm_gain[:, None], all_sums)
    pieces = lax.all_to_all(pieces, TOK, 0, 0, tiled=True)

    loads = jnp.sum((pieces[:, 0, :] < jnp.inf).astype(jnp.int32), axis=1)
    first = jnp.cumsum(loads) - loads
    part = 1.0 / jnp.sum(loads).astype(f32)
    mine, *streams = pack(first, pieces)

    places = [(q, u) for q in range(4) for u in range(4)]
    turned = lax.ppermute(mine, ("z", "y"), [(q * 4 + u, u * 4 + (q ^ u)) for q, u in places])

    for step in range(4):
        for s in range(4):
            axis, flip = PARTNERS[(s + step) % 4]
            seen = [PARTNERS[(s + k) % 4][0] for k in range(step)]
            which = side(x if axis == "x" else z, flip, axis not in seen)
            streams[s] = meet(streams[s], axis, flip, which)

    q = y ^ z
    low, high = turned[:32], turned[32:]
    low, high = meet(low, "y", 1, side(q, 1, True)), meet(high, "y", 3, side(q, 3, True))
    low, high = meet(low, "y", 3, side(q, 3, False)), meet(high, "y", 1, side(q, 1, False))
    rows = join(low, high)
    rows = join(rows, swap(rows))

    own, got = [], []
    for blocks in ((0, 1), (2, 3)):
        kept, given = gram(blocks, rows, streams)
        own.append(kept)
        got.append(swap(given))
    info = jnp.stack([c, (z * 8 + x * 2 + c) * 256, y * WIDTH]).astype(jnp.int32)
    mean, gram_factor = finish(info, part[None], own, got)
    return (mean[0], gram_factor)


def solution(mesh):
    fine = Mesh(mesh.devices.reshape(4, 4, 2, 4), ("z", "x", "c", "y"))
    return jax.shard_map(
        per_device,
        mesh=fine,
        in_specs=(P(TOK, "y"), P("y"), P(TOK), P(TOK)),
        out_specs=(P("y"), P(TOK, "y")),
        check_vma=False,
    )
```

```python
import jax
import jax.numpy as jnp
from jax import lax
from jax.experimental import pallas as pl
from jax.experimental.pallas import tpu as pltpu
from jax.sharding import Mesh, PartitionSpec as P

epsilon = 1e-05
TOK = ("z", "x", "c")
SLOTS = 256
LIVE = 4096
WIDTH = 2048
PIECE = 64
LONG = LIVE + 128
MIB = 1024 * 1024
bf16 = jnp.bfloat16
f32 = jnp.float32


def params(mib):
    return pltpu.CompilerParams(vmem_limit_bytes=mib * MIB)


def spread(value, place):
    high = value.astype(bf16).astype(f32)
    middle = (value - high).astype(bf16).astype(f32)
    low = value - high - middle
    rest = jnp.where(place == 2, low, 0.0)
    return jnp.where(place == 0, high, jnp.where(place == 1, middle, rest))


PARTNERS = (("x", 1), ("z", 1), ("x", 3), ("z", 3))


def side(place, flip, first):
    if flip == 1 and not first:
        return (place ^ (place >> 1)) & 1
    return place & 1 if flip == 1 else place >> 1


def slot_of(s, x, z):
    at, seen = 0, []
    for step in range(4):
        axis, flip = PARTNERS[(s + step) % 4]
        at += side(x if axis == "x" else z, flip, axis not in seen) << step
        seen.append(axis)
    return at


def live_slots(counts_ref):
    slot = lax.broadcasted_iota(jnp.int32, (1, SLOTS), 1)
    half = SLOTS // 2
    return slot < jnp.where(slot < half, counts_ref[0], half + counts_ref[1])


def second_place(q):
    return side(q, 1, False) * 2 + side(q, 3, True)


def pick_kernel(index_ref, counts_ref, resid_ref, picked_ref, sums_ref):
    tokens = resid_ref.shape[0]
    token = lax.broadcasted_iota(jnp.int32, (tokens, SLOTS), 0)
    kept = jnp.where(live_slots(counts_ref), index_ref[...], -1)
    one_hot = jnp.where(token == kept, 1.0, 0.0).astype(bf16)
    total = jnp.zeros((1, SLOTS), f32)
    step = 512
    for k in range(WIDTH // step):
        part = lax.dot_general(
            resid_ref[:, k * step : (k + 1) * step],
            one_hot,
            (((0,), (0,)), ((), ())),
            preferred_element_type=f32,
        )
        total += jnp.sum(part * part, axis=0, keepdims=True)
        picked_ref[k * step : (k + 1) * step, :] = part.astype(bf16)
    sums_ref[...] = jnp.broadcast_to(total, sums_ref.shape)


def pick(resid, keep_index, counts):
    vmem = pl.BlockSpec(memory_space=pltpu.VMEM)
    return pl.pallas_call(
        pick_kernel,
        out_shape=(
            jax.ShapeDtypeStruct((WIDTH, SLOTS), bf16),
            jax.ShapeDtypeStruct((8, SLOTS), f32),
        ),
        in_specs=[vmem, pl.BlockSpec(memory_space=pltpu.SMEM), vmem],
        out_specs=(vmem,) * 2,
        compiler_params=params(16),
        name="pick",
    )(keep_index[None, :], counts, resid)


def norm_kernel(counts_ref, picked_ref, gain_ref, s0, s1, s2, s3, out_ref):
    squares = (s0[:1, :] + s2[:1, :]) + (s1[:1, :] + s3[:1, :])
    scale = lax.rsqrt(squares / 8192 + epsilon)
    row = lax.broadcasted_iota(jnp.int32, (32, 1), 0)
    mark = jnp.where(row == 0, jnp.where(live_slots(counts_ref), 0.0, jnp.inf), 0.0).astype(bf16)
    for x in range(4):
        for c in range(2):
            first = (x * 2 + c) * 256
            rows = picked_ref[first : first + 256, :].astype(f32)
            short = (rows * scale * gain_ref[first : first + 256, :]).astype(bf16)
            for z in range(4):
                low, high = z * 32, 128 + second_place(z) * 32
                out_ref[z * 8 + x * 2 + c, :32, :] = short[low : low + 32, :] + mark
                out_ref[z * 8 + x * 2 + c, 32:, :] = short[high : high + 32, :]


def norm(counts, picked, gain, sums):
    return pl.pallas_call(
        norm_kernel,
        out_shape=jax.ShapeDtypeStruct((32, PIECE, SLOTS), bf16),
        in_specs=[pl.BlockSpec(memory_space=pltpu.SMEM)] + [pl.BlockSpec(memory_space=pltpu.VMEM)] * 6,
        out_specs=pl.BlockSpec(memory_space=pltpu.VMEM),
        compiler_params=params(10),
        name="norm",
    )(counts, picked, gain, *sums)


def pack_kernel(first_ref, in_ref, *refs):
    out_refs, acc_ref = refs[:-1], refs[-1]
    acc_ref[...] = jnp.zeros_like(acc_ref)
    group = 4

    def body(g, _):
        moved = []
        for k in range(group):
            t = g * group + k
            rows = in_ref[t].astype(f32)
            rows = jnp.where(rows < jnp.inf, rows, 0.0)
            first = first_ref[t]
            base = pl.multiple_of((first // 128) * 128, 128)
            wide = jnp.concatenate([rows, jnp.zeros((PIECE, 128), f32)], axis=1)
            moved.append((base, pltpu.roll(wide, first - base, 1)))
        for base, rows in moved:
            acc_ref[:, pl.ds(base, SLOTS + 128)] += rows
        return 0

    lax.fori_loop(0, 32 // group, body, 0)
    whole_ref, part_refs = out_refs[0], out_refs[1:]
    rows = acc_ref[:, :LIVE]
    whole_ref[:, :LIVE] = rows.astype(bf16)
    lane = lax.broadcasted_iota(jnp.int32, (PIECE, 128), 1)
    whole_ref[:, LIVE:] = spread(jnp.sum(rows, axis=1, keepdims=True), lane).astype(bf16)
    for k, ref in enumerate(part_refs):
        ref[...] = whole_ref[k * 16 : (k + 1) * 16, :]


def pack(first, pieces):
    vmem = pl.BlockSpec(memory_space=pltpu.VMEM)
    return pl.pallas_call(
        pack_kernel,
        out_shape=(jax.ShapeDtypeStruct((PIECE, LONG), bf16),)
        + (jax.ShapeDtypeStruct((16, LONG), bf16),) * 4,
        in_specs=[pl.BlockSpec(memory_space=pltpu.SMEM), vmem],
        out_specs=(vmem,) * 5,
        scratch_shapes=[pltpu.VMEM((PIECE, LIVE + SLOTS + 128), f32)],
        compiler_params=params(10),
        name="pack",
    )(first, pieces)


def halve_kernel(in_ref, *refs):
    low_ref, high_ref = refs[-2:]
    low_ref[...] = in_ref[: PIECE // 2, :]
    high_ref[...] = in_ref[PIECE // 2 :, :]


def halve(value, after):
    vmem = pl.BlockSpec(memory_space=pltpu.VMEM)
    return pl.pallas_call(
        halve_kernel,
        out_shape=(jax.ShapeDtypeStruct((PIECE // 2, LONG), bf16),) * 2,
        in_specs=[vmem] + [pl.BlockSpec(memory_space=pl.ANY)] * len(after),
        out_specs=(vmem,) * 2,
        compiler_params=params(4),
        name="halve",
    )(value, *after)


def gram_kernel(blocks, rows_ref, *refs):
    streams, (own_ref, given_ref, cols_ref) = refs[:4], refs[4:]
    lane = lax.broadcasted_iota(jnp.int32, (16, 128), 1)
    terms = jnp.where(lane < 3, 1.0, 0.0).astype(bf16)
    for n, x in enumerate(blocks):
        for z in range(4):
            for s in range(4):
                at = (z if s < 2 else 4 + second_place(z)) * 32 + s % 2 * 16
                first = slot_of(s, x, z) * 16
                cols_ref[n * 256 + at : n * 256 + at + 16, :] = streams[s][first : first + 16, :]
        inside = slice(n * 256, (n + 1) * 256)
        product = lax.dot_general(
            rows_ref[:, :LIVE],
            cols_ref[inside, :LIVE],
            (((1,), (1,)), ((), ())),
            preferred_element_type=f32,
        )
        own_ref[:256, inside] = product[:256]
        given_ref[:256, inside] = product[256:]
        sums = lax.dot_general(
            terms, cols_ref[inside, LIVE:], (((1,), (1,)), ((), ())), preferred_element_type=f32
        )
        own_ref[256:, inside] = sums[:8]
        given_ref[256:, inside] = sums[:8]


def gram(blocks, rows, streams):
    vmem = pl.BlockSpec(memory_space=pltpu.VMEM)
    width = 256 * len(blocks)
    return pl.pallas_call(
        lambda *refs: gram_kernel(blocks, *refs),
        out_shape=(jax.ShapeDtypeStruct((264, width), f32),) * 2,
        in_specs=[vmem] * 5,
        out_specs=(vmem,) * 2,
        scratch_shapes=[pltpu.VMEM((width, LONG), bf16)],
        compiler_params=params(10),
        cost_estimate=pl.CostEstimate(
            flops=2 * 512 * width * LIVE, bytes_accessed=6 * 1024 * 1024, transcendentals=0
        ),
        name="gram",
    )(rows, *streams)


def finish_kernel(info_ref, part_ref, *refs):
    own, got, (mean_ref, out_ref) = refs[:2], refs[2:4], refs[4:]
    core, row_first, col_first = info_ref[0], info_ref[1], info_ref[2]
    part = part_ref[0]
    row = row_first + lax.broadcasted_iota(jnp.int32, (256, 256), 0)
    col = col_first + lax.broadcasted_iota(jnp.int32, (256, 256), 1)
    for x in range(4):
        inside = slice(x % 2 * 256, (x % 2 + 1) * 256)
        for ref, which in ((own[x // 2], core), (got[x // 2], 1 - core)):
            at = pl.multiple_of(x * 512 + which * 256, 256)
            out_ref[:, pl.ds(at, 256)] = jnp.where(row <= col + at, ref[:256, inside] * part, 0.0)
            mean_ref[:, pl.ds(at, 256)] = ref[256:264, inside][:1] * part


def finish(info, part, own, got):
    vmem = pl.BlockSpec(memory_space=pltpu.VMEM)
    return pl.pallas_call(
        finish_kernel,
        out_shape=(
            jax.ShapeDtypeStruct((1, WIDTH), f32),
            jax.ShapeDtypeStruct((256, WIDTH), f32),
        ),
        in_specs=[pl.BlockSpec(memory_space=pltpu.SMEM)] * 2 + [vmem] * 4,
        out_specs=(vmem,) * 2,
        compiler_params=params(10),
        name="finish",
    )(info, part, *own, *got)


def swap(value):
    return lax.ppermute(value, "c", [(0, 1), (1, 0)])


def trade(value, axis, flip):
    return lax.ppermute(value, axis, [(i, i ^ flip) for i in range(4)])


def join(*values):
    return jnp.concatenate(values, axis=0)


def meet(value, axis, flip, which):
    got = trade(value, axis, flip)
    return join(jnp.where(which == 0, value, got), jnp.where(which == 0, got, value))


def per_device(resid, norm_gain, keep_index, counts):
    z, x, c, y = (lax.axis_index(a) for a in ("z", "x", "c", "y"))
    picked, sums = pick(resid, keep_index, counts)
    all_sums = [sums] + [trade(sums, "y", flip) for flip in (1, 2, 3)]
    pieces = norm(counts, picked, norm_gain[:, None], all_sums)
    pieces = lax.all_to_all(pieces, TOK, 0, 0, tiled=True)

    loads = jnp.sum((pieces[:, 0, :] < jnp.inf).astype(jnp.int32), axis=1)
    first = jnp.cumsum(loads) - loads
    part = 1.0 / jnp.sum(loads).astype(f32)
    mine, *streams = pack(first, pieces)

    places = [(q, u) for q in range(4) for u in range(4)]
    turned = lax.ppermute(mine, ("z", "y"), [(q * 4 + u, u * 4 + (q ^ u)) for q, u in places])

    for step in range(4):
        for s in range(4):
            axis, flip = PARTNERS[(s + step) % 4]
            seen = [PARTNERS[(s + k) % 4][0] for k in range(step)]
            which = side(x if axis == "x" else z, flip, axis not in seen)
            streams[s] = meet(streams[s], axis, flip, which)
        if step == 2:
            low, high = halve(turned, after=streams[:1])

    q = y ^ z
    low, high = meet(low, "y", 1, side(q, 1, True)), meet(high, "y", 3, side(q, 3, True))
    low, high = meet(low, "y", 3, side(q, 3, False)), meet(high, "y", 1, side(q, 1, False))
    rows = join(low, high)
    rows = join(rows, swap(rows))

    own, got = [], []
    for blocks in ((0, 1), (2, 3)):
        kept, given = gram(blocks, rows, streams)
        own.append(kept)
        got.append(swap(given))
    info = jnp.stack([c, (z * 8 + x * 2 + c) * 256, y * WIDTH]).astype(jnp.int32)
    mean, gram_factor = finish(info, part[None], own, got)
    return (mean[0], gram_factor)


def solution(mesh):
    fine = Mesh(mesh.devices.reshape(4, 4, 2, 4), ("z", "x", "c", "y"))
    return jax.shard_map(
        per_device,
        mesh=fine,
        in_specs=(P(TOK, "y"), P("y"), P(TOK), P(TOK)),
        out_specs=(P("y"), P(TOK, "y")),
        check_vma=False,
    )
```

```python
import jax
import jax.numpy as jnp
from jax import lax
from jax.experimental import pallas as pl
from jax.experimental.pallas import tpu as pltpu
from jax.sharding import Mesh, PartitionSpec as P

epsilon = 1e-05
TOK = ("z", "x", "c")
SLOTS = 256
LIVE = 4096
WIDTH = 2048
PIECE = 64
LONG = LIVE + 128
MIB = 1024 * 1024
bf16 = jnp.bfloat16
f32 = jnp.float32


def params(mib):
    return pltpu.CompilerParams(vmem_limit_bytes=mib * MIB)


def spread(value, place):
    high = value.astype(bf16).astype(f32)
    middle = (value - high).astype(bf16).astype(f32)
    low = value - high - middle
    rest = jnp.where(place == 2, low, 0.0)
    return jnp.where(place == 0, high, jnp.where(place == 1, middle, rest))


PARTNERS = (("x", 1), ("z", 1), ("x", 3), ("z", 3))


def side(place, flip, first):
    if flip == 1 and not first:
        return (place ^ (place >> 1)) & 1
    return place & 1 if flip == 1 else place >> 1


def slot_of(s, x, z):
    at, seen = 0, []
    for step in range(4):
        axis, flip = PARTNERS[(s + step) % 4]
        at += side(x if axis == "x" else z, flip, axis not in seen) << step
        seen.append(axis)
    return at


def live_slots(counts_ref):
    slot = lax.broadcasted_iota(jnp.int32, (1, SLOTS), 1)
    half = SLOTS // 2
    return slot < jnp.where(slot < half, counts_ref[0], half + counts_ref[1])


def pick_kernel(index_ref, counts_ref, resid_ref, picked_ref, sums_ref):
    tokens = resid_ref.shape[0]
    token = lax.broadcasted_iota(jnp.int32, (tokens, SLOTS), 0)
    kept = jnp.where(live_slots(counts_ref), index_ref[...], -1)
    one_hot = jnp.where(token == kept, 1.0, 0.0).astype(bf16)
    total = jnp.zeros((1, SLOTS), f32)
    step = 512
    for k in range(WIDTH // step):
        part = lax.dot_general(
            resid_ref[:, k * step : (k + 1) * step],
            one_hot,
            (((0,), (0,)), ((), ())),
            preferred_element_type=f32,
        )
        total += jnp.sum(part * part, axis=0, keepdims=True)
        picked_ref[k * step : (k + 1) * step, :] = part.astype(bf16)
    sums_ref[...] = jnp.broadcast_to(total, sums_ref.shape)


def pick(resid, keep_index, counts):
    vmem = pl.BlockSpec(memory_space=pltpu.VMEM)
    return pl.pallas_call(
        pick_kernel,
        out_shape=(
            jax.ShapeDtypeStruct((WIDTH, SLOTS), bf16),
            jax.ShapeDtypeStruct((8, SLOTS), f32),
        ),
        in_specs=[vmem, pl.BlockSpec(memory_space=pltpu.SMEM), vmem],
        out_specs=(vmem,) * 2,
        compiler_params=params(16),
        name="pick",
    )(keep_index[None, :], counts, resid)


def norm_kernel(counts_ref, picked_ref, gain_ref, s0, s1, s2, s3, out_ref):
    squares = (s0[:1, :] + s2[:1, :]) + (s1[:1, :] + s3[:1, :])
    scale = lax.rsqrt(squares / 8192 + epsilon)
    row = lax.broadcasted_iota(jnp.int32, (PIECE, 1), 0)
    mark = jnp.where(row == 0, jnp.where(live_slots(counts_ref), 0.0, jnp.inf), 0.0).astype(bf16)
    for x in range(4):
        for c in range(2):
            first = (x * 2 + c) * 256
            rows = picked_ref[first : first + 256, :].astype(f32)
            short = (rows * scale * gain_ref[first : first + 256, :]).astype(bf16)
            for z in range(4):
                out_ref[z * 8 + x * 2 + c] = short[z * PIECE : (z + 1) * PIECE, :] + mark


def norm(counts, picked, gain, sums):
    return pl.pallas_call(
        norm_kernel,
        out_shape=jax.ShapeDtypeStruct((32, PIECE, SLOTS), bf16),
        in_specs=[pl.BlockSpec(memory_space=pltpu.SMEM)] + [pl.BlockSpec(memory_space=pltpu.VMEM)] * 6,
        out_specs=pl.BlockSpec(memory_space=pltpu.VMEM),
        compiler_params=params(10),
        name="norm",
    )(counts, picked, gain, *sums)


def pack_kernel(first_ref, in_ref, *refs):
    out_refs, acc_ref = refs[:-1], refs[-1]
    acc_ref[...] = jnp.zeros_like(acc_ref)
    group = 4

    def body(g, _):
        moved = []
        for k in range(group):
            t = g * group + k
            rows = in_ref[t].astype(f32)
            rows = jnp.where(rows < jnp.inf, rows, 0.0)
            first = first_ref[t]
            base = pl.multiple_of((first // 128) * 128, 128)
            wide = jnp.concatenate([rows, jnp.zeros((PIECE, 128), f32)], axis=1)
            moved.append((base, pltpu.roll(wide, first - base, 1)))
        for base, rows in moved:
            acc_ref[:, pl.ds(base, SLOTS + 128)] += rows
        return 0

    lax.fori_loop(0, 32 // group, body, 0)
    whole_ref, part_refs = out_refs[0], out_refs[1:]
    rows = acc_ref[:, :LIVE]
    whole_ref[:, :LIVE] = rows.astype(bf16)
    lane = lax.broadcasted_iota(jnp.int32, (PIECE, 128), 1)
    whole_ref[:, LIVE:] = spread(jnp.sum(rows, axis=1, keepdims=True), lane).astype(bf16)
    for k, ref in enumerate(part_refs):
        ref[...] = whole_ref[k * 16 : (k + 1) * 16, :]


def pack(first, pieces):
    vmem = pl.BlockSpec(memory_space=pltpu.VMEM)
    return pl.pallas_call(
        pack_kernel,
        out_shape=(jax.ShapeDtypeStruct((PIECE, LONG), bf16),)
        + (jax.ShapeDtypeStruct((16, LONG), bf16),) * 4,
        in_specs=[pl.BlockSpec(memory_space=pltpu.SMEM), vmem],
        out_specs=(vmem,) * 5,
        scratch_shapes=[pltpu.VMEM((PIECE, LIVE + SLOTS + 128), f32)],
        compiler_params=params(10),
        name="pack",
    )(first, pieces)


def behind_kernel(in_ref, *refs):
    refs[-1][...] = in_ref[...]


def behind(value, after):
    vmem = pl.BlockSpec(memory_space=pltpu.VMEM)
    return pl.pallas_call(
        behind_kernel,
        out_shape=jax.ShapeDtypeStruct(value.shape, value.dtype),
        in_specs=[vmem] + [pl.BlockSpec(memory_space=pl.ANY)] * len(after),
        out_specs=vmem,
        compiler_params=params(4),
        name="behind",
    )(value, *after)


def gram_kernel(blocks, rows_ref, *refs):
    streams, (own_ref, given_ref, cols_ref) = refs[:4], refs[4:]
    lane = lax.broadcasted_iota(jnp.int32, (16, 128), 1)
    terms = jnp.where(lane < 3, 1.0, 0.0).astype(bf16)
    for n, x in enumerate(blocks):
        for z in range(4):
            for s in range(4):
                at = z * PIECE + s * 16
                first = slot_of(s, x, z) * 16
                cols_ref[n * 256 + at : n * 256 + at + 16, :] = streams[s][first : first + 16, :]
        inside = slice(n * 256, (n + 1) * 256)
        product = lax.dot_general(
            rows_ref[:, :LIVE],
            cols_ref[inside, :LIVE],
            (((1,), (1,)), ((), ())),
            preferred_element_type=f32,
        )
        own_ref[:256, inside] = product[:256]
        given_ref[:256, inside] = product[256:]
        sums = lax.dot_general(
            terms, cols_ref[inside, LIVE:], (((1,), (1,)), ((), ())), preferred_element_type=f32
        )
        own_ref[256:, inside] = sums[:8]
        given_ref[256:, inside] = sums[:8]


def gram(blocks, rows, streams):
    vmem = pl.BlockSpec(memory_space=pltpu.VMEM)
    width = 256 * len(blocks)
    return pl.pallas_call(
        lambda *refs: gram_kernel(blocks, *refs),
        out_shape=(jax.ShapeDtypeStruct((264, width), f32),) * 2,
        in_specs=[vmem] * 5,
        out_specs=(vmem,) * 2,
        scratch_shapes=[pltpu.VMEM((width, LONG), bf16)],
        compiler_params=params(10),
        cost_estimate=pl.CostEstimate(
            flops=2 * 512 * width * LIVE, bytes_accessed=6 * 1024 * 1024, transcendentals=0
        ),
        name="gram",
    )(rows, *streams)


def finish_kernel(info_ref, part_ref, *refs):
    own, got, (mean_ref, out_ref) = refs[:2], refs[2:4], refs[4:]
    core, row_first, col_first = info_ref[0], info_ref[1], info_ref[2]
    part = part_ref[0]
    row = row_first + lax.broadcasted_iota(jnp.int32, (256, 256), 0)
    col = col_first + lax.broadcasted_iota(jnp.int32, (256, 256), 1)
    for x in range(4):
        inside = slice(x % 2 * 256, (x % 2 + 1) * 256)
        for ref, which in ((own[x // 2], core), (got[x // 2], 1 - core)):
            at = pl.multiple_of(x * 512 + which * 256, 256)
            out_ref[:, pl.ds(at, 256)] = jnp.where(row <= col + at, ref[:256, inside] * part, 0.0)
            mean_ref[:, pl.ds(at, 256)] = ref[256:264, inside][:1] * part


def finish(info, part, own, got):
    vmem = pl.BlockSpec(memory_space=pltpu.VMEM)
    return pl.pallas_call(
        finish_kernel,
        out_shape=(
            jax.ShapeDtypeStruct((1, WIDTH), f32),
            jax.ShapeDtypeStruct((256, WIDTH), f32),
        ),
        in_specs=[pl.BlockSpec(memory_space=pltpu.SMEM)] * 2 + [vmem] * 4,
        out_specs=(vmem,) * 2,
        compiler_params=params(10),
        name="finish",
    )(info, part, *own, *got)


def swap(value):
    return lax.ppermute(value, "c", [(0, 1), (1, 0)])


def trade(value, axis, flip):
    return lax.ppermute(value, axis, [(i, i ^ flip) for i in range(4)])


def join(*values):
    return jnp.concatenate(values, axis=0)


def meet(value, axis, flip, which):
    got = trade(value, axis, flip)
    return join(jnp.where(which == 0, value, got), jnp.where(which == 0, got, value))


def per_device(resid, norm_gain, keep_index, counts):
    z, x, c, y = (lax.axis_index(a) for a in ("z", "x", "c", "y"))
    picked, sums = pick(resid, keep_index, counts)
    all_sums = [sums] + [trade(sums, "y", flip) for flip in (1, 2, 3)]
    pieces = norm(counts, picked, norm_gain[:, None], all_sums)
    pieces = lax.all_to_all(pieces, TOK, 0, 0, tiled=True)

    loads = jnp.sum((pieces[:, 0, :] < jnp.inf).astype(jnp.int32), axis=1)
    first = jnp.cumsum(loads) - loads
    part = 1.0 / jnp.sum(loads).astype(f32)
    mine, *streams = pack(first, pieces)

    for step in range(4):
        for s in range(4):
            axis, flip = PARTNERS[(s + step) % 4]
            seen = [PARTNERS[(s + k) % 4][0] for k in range(step)]
            which = side(x if axis == "x" else z, flip, axis not in seen)
            streams[s] = meet(streams[s], axis, flip, which)
        if step == 0:
            places = [(q, u) for q in range(4) for u in range(4)]
            turned = lax.ppermute(
                behind(mine, streams), ("z", "y"), [(q * 4 + u, u * 4 + (q ^ u)) for q, u in places]
            )
        if step == 1:
            rows = behind(turned, streams)

    q = y ^ z
    rows = meet(rows, "y", 1, side(q, 1, True))
    rows = meet(rows, "y", 3, side(q, 3, False))
    rows = join(rows, swap(rows))

    own, got = [], []
    for blocks in ((0, 1), (2, 3)):
        kept, given = gram(blocks, rows, streams)
        own.append(kept)
        got.append(swap(given))
    info = jnp.stack([c, (z * 8 + x * 2 + c) * 256, y * WIDTH]).astype(jnp.int32)
    mean, gram_factor = finish(info, part[None], own, got)
    return (mean[0], gram_factor)


def solution(mesh):
    fine = Mesh(mesh.devices.reshape(4, 4, 2, 4), ("z", "x", "c", "y"))
    return jax.shard_map(
        per_device,
        mesh=fine,
        in_specs=(P(TOK, "y"), P("y"), P(TOK), P(TOK)),
        out_specs=(P("y"), P(TOK, "y")),
        check_vma=False,
    )
```

```python
import jax
import jax.numpy as jnp
from jax import lax
from jax.experimental import pallas as pl
from jax.experimental.pallas import tpu as pltpu
from jax.sharding import Mesh, PartitionSpec as P

epsilon = 1e-05
TOK = ("z", "x", "c")
SLOTS = 256
LIVE = 4096
WIDTH = 2048
PIECE = 64
LONG = LIVE + 128
MIB = 1024 * 1024
bf16 = jnp.bfloat16
f32 = jnp.float32


def params(mib):
    return pltpu.CompilerParams(vmem_limit_bytes=mib * MIB)


def spread(value, place):
    high = value.astype(bf16).astype(f32)
    middle = (value - high).astype(bf16).astype(f32)
    low = value - high - middle
    rest = jnp.where(place == 2, low, 0.0)
    return jnp.where(place == 0, high, jnp.where(place == 1, middle, rest))


PARTNERS = (("x", 1), ("z", 1), ("x", 3), ("z", 3))


def side(place, flip, first):
    if flip == 1 and not first:
        return (place ^ (place >> 1)) & 1
    return place & 1 if flip == 1 else place >> 1


def slot_of(s, x, z):
    at, seen = 0, []
    for step in range(4):
        axis, flip = PARTNERS[(s + step) % 4]
        at += side(x if axis == "x" else z, flip, axis not in seen) << step
        seen.append(axis)
    return at


def live_slots(counts_ref):
    slot = lax.broadcasted_iota(jnp.int32, (1, SLOTS), 1)
    half = SLOTS // 2
    return slot < jnp.where(slot < half, counts_ref[0], half + counts_ref[1])


def pick_kernel(index_ref, counts_ref, resid_ref, picked_ref, sums_ref):
    tokens = resid_ref.shape[0]
    token = lax.broadcasted_iota(jnp.int32, (tokens, SLOTS), 0)
    kept = jnp.where(live_slots(counts_ref), index_ref[...], -1)
    one_hot = jnp.where(token == kept, 1.0, 0.0).astype(bf16)
    total = jnp.zeros((1, SLOTS), f32)
    step = 512
    for k in range(WIDTH // step):
        part = lax.dot_general(
            resid_ref[:, k * step : (k + 1) * step],
            one_hot,
            (((0,), (0,)), ((), ())),
            preferred_element_type=f32,
        )
        total += jnp.sum(part * part, axis=0, keepdims=True)
        picked_ref[k * step : (k + 1) * step, :] = part.astype(bf16)
    sums_ref[...] = jnp.broadcast_to(total, sums_ref.shape)


def pick(resid, keep_index, counts):
    vmem = pl.BlockSpec(memory_space=pltpu.VMEM)
    return pl.pallas_call(
        pick_kernel,
        out_shape=(
            jax.ShapeDtypeStruct((WIDTH, SLOTS), bf16),
            jax.ShapeDtypeStruct((8, SLOTS), f32),
        ),
        in_specs=[vmem, pl.BlockSpec(memory_space=pltpu.SMEM), vmem],
        out_specs=(vmem,) * 2,
        compiler_params=params(16),
        name="pick",
    )(keep_index[None, :], counts, resid)


def norm_kernel(counts_ref, picked_ref, gain_ref, s0, s1, s2, s3, out_ref):
    squares = (s0[:1, :] + s2[:1, :]) + (s1[:1, :] + s3[:1, :])
    scale = lax.rsqrt(squares / 8192 + epsilon)
    row = lax.broadcasted_iota(jnp.int32, (PIECE, 1), 0)
    mark = jnp.where(row == 0, jnp.where(live_slots(counts_ref), 0.0, jnp.inf), 0.0).astype(bf16)
    for x in range(4):
        for c in range(2):
            first = (x * 2 + c) * 256
            rows = picked_ref[first : first + 256, :].astype(f32)
            short = (rows * scale * gain_ref[first : first + 256, :]).astype(bf16)
            for z in range(4):
                out_ref[z * 8 + x * 2 + c] = short[z * PIECE : (z + 1) * PIECE, :] + mark


def norm(counts, picked, gain, sums):
    return pl.pallas_call(
        norm_kernel,
        out_shape=jax.ShapeDtypeStruct((32, PIECE, SLOTS), bf16),
        in_specs=[pl.BlockSpec(memory_space=pltpu.SMEM)] + [pl.BlockSpec(memory_space=pltpu.VMEM)] * 6,
        out_specs=pl.BlockSpec(memory_space=pltpu.VMEM),
        compiler_params=params(10),
        name="norm",
    )(counts, picked, gain, *sums)


def pack_kernel(first_ref, in_ref, *refs):
    out_refs, acc_ref = refs[:-1], refs[-1]
    acc_ref[...] = jnp.zeros_like(acc_ref)
    group = 4

    def body(g, _):
        moved = []
        for k in range(group):
            t = g * group + k
            rows = in_ref[t].astype(f32)
            rows = jnp.where(rows < jnp.inf, rows, 0.0)
            first = first_ref[t]
            base = pl.multiple_of((first // 128) * 128, 128)
            wide = jnp.concatenate([rows, jnp.zeros((PIECE, 128), f32)], axis=1)
            moved.append((base, pltpu.roll(wide, first - base, 1)))
        for base, rows in moved:
            acc_ref[:, pl.ds(base, SLOTS + 128)] += rows
        return 0

    lax.fori_loop(0, 32 // group, body, 0)
    for k, ref in enumerate(out_refs[2:]):
        rows = acc_ref[k * 16 : (k + 1) * 16, :LIVE]
        lane = lax.broadcasted_iota(jnp.int32, (16, 128), 1)
        sums = spread(jnp.sum(rows, axis=1, keepdims=True), lane)
        for into in (ref, out_refs[k // 2].at[pl.ds(k % 2 * 16, 16)]):
            into[:, :LIVE] = rows.astype(bf16)
            into[:, LIVE:] = sums.astype(bf16)


def pack(first, pieces):
    vmem = pl.BlockSpec(memory_space=pltpu.VMEM)
    return pl.pallas_call(
        pack_kernel,
        out_shape=(jax.ShapeDtypeStruct((32, LONG), bf16),) * 2
        + (jax.ShapeDtypeStruct((16, LONG), bf16),) * 4,
        in_specs=[pl.BlockSpec(memory_space=pltpu.SMEM), vmem],
        out_specs=(vmem,) * 6,
        scratch_shapes=[pltpu.VMEM((PIECE, LIVE + SLOTS + 128), f32)],
        compiler_params=params(10),
        name="pack",
    )(first, pieces)


def behind_kernel(in_ref, *refs):
    refs[-1][...] = in_ref[...]


def behind(value, after):
    vmem = pl.BlockSpec(memory_space=pltpu.VMEM)
    return pl.pallas_call(
        behind_kernel,
        out_shape=jax.ShapeDtypeStruct(value.shape, value.dtype),
        in_specs=[vmem] + [pl.BlockSpec(memory_space=pl.ANY)] * len(after),
        out_specs=vmem,
        compiler_params=params(4),
        name="behind",
    )(value, *after)


def gram_kernel(blocks, rows_ref, *refs):
    streams, (own_ref, given_ref, cols_ref) = refs[:4], refs[4:]
    lane = lax.broadcasted_iota(jnp.int32, (16, 128), 1)
    terms = jnp.where(lane < 3, 1.0, 0.0).astype(bf16)
    for n, x in enumerate(blocks):
        for z in range(4):
            for s in range(4):
                at = z * PIECE + s * 16
                first = slot_of(s, x, z) * 16
                cols_ref[n * 256 + at : n * 256 + at + 16, :] = streams[s][first : first + 16, :]
        inside = slice(n * 256, (n + 1) * 256)
        product = lax.dot_general(
            rows_ref[:, :LIVE],
            cols_ref[inside, :LIVE],
            (((1,), (1,)), ((), ())),
            preferred_element_type=f32,
        )
        own_ref[:256, inside] = product[:256]
        given_ref[:256, inside] = product[256:]
        sums = lax.dot_general(
            terms, cols_ref[inside, LIVE:], (((1,), (1,)), ((), ())), preferred_element_type=f32
        )
        own_ref[256:, inside] = sums[:8]
        given_ref[256:, inside] = sums[:8]


def gram(blocks, rows, streams):
    vmem = pl.BlockSpec(memory_space=pltpu.VMEM)
    width = 256 * len(blocks)
    return pl.pallas_call(
        lambda *refs: gram_kernel(blocks, *refs),
        out_shape=(jax.ShapeDtypeStruct((264, width), f32),) * 2,
        in_specs=[vmem] * 5,
        out_specs=(vmem,) * 2,
        scratch_shapes=[pltpu.VMEM((width, LONG), bf16)],
        compiler_params=params(10),
        cost_estimate=pl.CostEstimate(
            flops=2 * 512 * width * LIVE, bytes_accessed=6 * 1024 * 1024, transcendentals=0
        ),
        name="gram",
    )(rows, *streams)


def finish_kernel(info_ref, part_ref, *refs):
    own, got, (mean_ref, out_ref) = refs[:2], refs[2:4], refs[4:]
    core, row_first, col_first = info_ref[0], info_ref[1], info_ref[2]
    part = part_ref[0]
    row = row_first + lax.broadcasted_iota(jnp.int32, (256, 256), 0)
    col = col_first + lax.broadcasted_iota(jnp.int32, (256, 256), 1)
    for x in range(4):
        inside = slice(x % 2 * 256, (x % 2 + 1) * 256)
        for ref, which in ((own[x // 2], core), (got[x // 2], 1 - core)):
            at = pl.multiple_of(x * 512 + which * 256, 256)
            out_ref[:, pl.ds(at, 256)] = jnp.where(row <= col + at, ref[:256, inside] * part, 0.0)
            mean_ref[:, pl.ds(at, 256)] = ref[256:264, inside][:1] * part


def finish(info, part, own, got):
    vmem = pl.BlockSpec(memory_space=pltpu.VMEM)
    return pl.pallas_call(
        finish_kernel,
        out_shape=(
            jax.ShapeDtypeStruct((1, WIDTH), f32),
            jax.ShapeDtypeStruct((256, WIDTH), f32),
        ),
        in_specs=[pl.BlockSpec(memory_space=pltpu.SMEM)] * 2 + [vmem] * 4,
        out_specs=(vmem,) * 2,
        compiler_params=params(10),
        name="finish",
    )(info, part, *own, *got)


def swap(value):
    return lax.ppermute(value, "c", [(0, 1), (1, 0)])


def trade(value, axis, flip):
    return lax.ppermute(value, axis, [(i, i ^ flip) for i in range(4)])


def join(*values):
    return jnp.concatenate(values, axis=0)


def meet(value, axis, flip, which):
    got = trade(value, axis, flip)
    return join(jnp.where(which == 0, value, got), jnp.where(which == 0, got, value))


def per_device(resid, norm_gain, keep_index, counts):
    z, x, c, y = (lax.axis_index(a) for a in ("z", "x", "c", "y"))
    picked, sums = pick(resid, keep_index, counts)
    all_sums = [sums] + [trade(sums, "y", flip) for flip in (1, 2, 3)]
    pieces = norm(counts, picked, norm_gain[:, None], all_sums)
    pieces = lax.all_to_all(pieces, TOK, 0, 0, tiled=True)

    loads = jnp.sum((pieces[:, 0, :] < jnp.inf).astype(jnp.int32), axis=1)
    first = jnp.cumsum(loads) - loads
    part = 1.0 / jnp.sum(loads).astype(f32)
    *halves, s0, s1, s2, s3 = pack(first, pieces)
    streams, turned = [s0, s1, s2, s3], []

    for step in range(4):
        for s in range(4):
            axis, flip = PARTNERS[(s + step) % 4]
            seen = [PARTNERS[(s + k) % 4][0] for k in range(step)]
            which = side(x if axis == "x" else z, flip, axis not in seen)
            streams[s] = meet(streams[s], axis, flip, which)
        if step < 2:
            places = [(q, u) for q in range(4) for u in range(4)]
            turned.append(
                lax.ppermute(
                    behind(halves[step], streams[:1]),
                    ("z", "y"),
                    [(q * 4 + u, u * 4 + (q ^ u)) for q, u in places],
                )
            )
        if step == 1:
            rows = behind(join(*turned), streams)

    q = y ^ z
    rows = meet(rows, "y", 1, side(q, 1, True))
    rows = meet(rows, "y", 3, side(q, 3, False))
    rows = join(rows, swap(rows))

    own, got = [], []
    for blocks in ((0, 1), (2, 3)):
        kept, given = gram(blocks, rows, streams)
        own.append(kept)
        got.append(swap(given))
    info = jnp.stack([c, (z * 8 + x * 2 + c) * 256, y * WIDTH]).astype(jnp.int32)
    mean, gram_factor = finish(info, part[None], own, got)
    return (mean[0], gram_factor)


def solution(mesh):
    fine = Mesh(mesh.devices.reshape(4, 4, 2, 4), ("z", "x", "c", "y"))
    return jax.shard_map(
        per_device,
        mesh=fine,
        in_specs=(P(TOK, "y"), P("y"), P(TOK), P(TOK)),
        out_specs=(P("y"), P(TOK, "y")),
        check_vma=False,
    )
```

```python
import jax
import jax.numpy as jnp
from jax import lax
from jax.experimental import pallas as pl
from jax.experimental.pallas import tpu as pltpu
from jax.sharding import Mesh, PartitionSpec as P

epsilon = 1e-05
TOK = ("z", "x", "c")
SLOTS = 256
LIVE = 4096
WIDTH = 2048
PIECE = 64
LONG = LIVE + 128
MIB = 1024 * 1024
bf16 = jnp.bfloat16
f32 = jnp.float32


def params(mib):
    return pltpu.CompilerParams(vmem_limit_bytes=mib * MIB)


def spread(value, place):
    high = value.astype(bf16).astype(f32)
    middle = (value - high).astype(bf16).astype(f32)
    low = value - high - middle
    rest = jnp.where(place == 2, low, 0.0)
    return jnp.where(place == 0, high, jnp.where(place == 1, middle, rest))


PARTNERS = (("x", 1), ("z", 1), ("x", 3), ("z", 3))


def side(place, flip, first):
    if flip == 1 and not first:
        return (place ^ (place >> 1)) & 1
    return place & 1 if flip == 1 else place >> 1


def slot_of(s, x, z):
    at, seen = 0, []
    for step in range(4):
        axis, flip = PARTNERS[(s + step) % 4]
        at += side(x if axis == "x" else z, flip, axis not in seen) << step
        seen.append(axis)
    return at


def live_slots(counts_ref):
    slot = lax.broadcasted_iota(jnp.int32, (1, SLOTS), 1)
    half = SLOTS // 2
    return slot < jnp.where(slot < half, counts_ref[0], half + counts_ref[1])


def pick_kernel(index_ref, counts_ref, resid_ref, picked_ref, sums_ref):
    tokens = resid_ref.shape[0]
    token = lax.broadcasted_iota(jnp.int32, (tokens, SLOTS), 0)
    kept = jnp.where(live_slots(counts_ref), index_ref[...], -1)
    one_hot = jnp.where(token == kept, 1.0, 0.0).astype(bf16)
    total = jnp.zeros((1, SLOTS), f32)
    step = 512
    for k in range(WIDTH // step):
        part = lax.dot_general(
            resid_ref[:, k * step : (k + 1) * step],
            one_hot,
            (((0,), (0,)), ((), ())),
            preferred_element_type=f32,
        )
        total += jnp.sum(part * part, axis=0, keepdims=True)
        picked_ref[k * step : (k + 1) * step, :] = part.astype(bf16)
    sums_ref[...] = jnp.broadcast_to(total, sums_ref.shape)


def pick(resid, keep_index, counts):
    vmem = pl.BlockSpec(memory_space=pltpu.VMEM)
    return pl.pallas_call(
        pick_kernel,
        out_shape=(
            jax.ShapeDtypeStruct((WIDTH, SLOTS), bf16),
            jax.ShapeDtypeStruct((8, SLOTS), f32),
        ),
        in_specs=[vmem, pl.BlockSpec(memory_space=pltpu.SMEM), vmem],
        out_specs=(vmem,) * 2,
        compiler_params=params(16),
        name="pick",
    )(keep_index[None, :], counts, resid)


def norm_kernel(counts_ref, picked_ref, gain_ref, s0, s1, s2, s3, out_ref):
    squares = (s0[:1, :] + s2[:1, :]) + (s1[:1, :] + s3[:1, :])
    scale = lax.rsqrt(squares / 8192 + epsilon)
    row = lax.broadcasted_iota(jnp.int32, (32, 1), 0)
    mark = jnp.where(row == 0, jnp.where(live_slots(counts_ref), 0.0, jnp.inf), 0.0).astype(bf16)
    for x in range(4):
        for c in range(2):
            first = (x * 2 + c) * 256
            rows = picked_ref[first : first + 256, :].astype(f32)
            short = (rows * scale * gain_ref[first : first + 256, :]).astype(bf16)
            for z in range(4):
                low, high = z * PIECE, (z ^ 2) * PIECE + 32
                out_ref[z * 8 + x * 2 + c, :32, :] = short[low : low + 32, :] + mark
                out_ref[z * 8 + x * 2 + c, 32:, :] = short[high : high + 32, :]


def norm(counts, picked, gain, sums):
    return pl.pallas_call(
        norm_kernel,
        out_shape=jax.ShapeDtypeStruct((32, PIECE, SLOTS), bf16),
        in_specs=[pl.BlockSpec(memory_space=pltpu.SMEM)] + [pl.BlockSpec(memory_space=pltpu.VMEM)] * 6,
        out_specs=pl.BlockSpec(memory_space=pltpu.VMEM),
        compiler_params=params(10),
        name="norm",
    )(counts, picked, gain, *sums)


def pack_kernel(first_ref, in_ref, *refs):
    out_refs, acc_ref = refs[:-1], refs[-1]
    acc_ref[...] = jnp.zeros_like(acc_ref)
    group = 4

    def body(g, _):
        moved = []
        for k in range(group):
            t = g * group + k
            rows = in_ref[t].astype(f32)
            rows = jnp.where(rows < jnp.inf, rows, 0.0)
            first = first_ref[t]
            base = pl.multiple_of((first // 128) * 128, 128)
            wide = jnp.concatenate([rows, jnp.zeros((PIECE, 128), f32)], axis=1)
            moved.append((base, pltpu.roll(wide, first - base, 1)))
        for base, rows in moved:
            acc_ref[:, pl.ds(base, SLOTS + 128)] += rows
        return 0

    lax.fori_loop(0, 32 // group, body, 0)
    for k, ref in enumerate(out_refs[2:]):
        rows = acc_ref[k * 16 : (k + 1) * 16, :LIVE]
        lane = lax.broadcasted_iota(jnp.int32, (16, 128), 1)
        sums = spread(jnp.sum(rows, axis=1, keepdims=True), lane)
        for into in (ref, out_refs[k // 2].at[pl.ds(k % 2 * 16, 16)]):
            into[:, :LIVE] = rows.astype(bf16)
            into[:, LIVE:] = sums.astype(bf16)


def pack(first, pieces):
    vmem = pl.BlockSpec(memory_space=pltpu.VMEM)
    return pl.pallas_call(
        pack_kernel,
        out_shape=(jax.ShapeDtypeStruct((32, LONG), bf16),) * 2
        + (jax.ShapeDtypeStruct((16, LONG), bf16),) * 4,
        in_specs=[pl.BlockSpec(memory_space=pltpu.SMEM), vmem],
        out_specs=(vmem,) * 6,
        scratch_shapes=[pltpu.VMEM((PIECE, LIVE + SLOTS + 128), f32)],
        compiler_params=params(10),
        name="pack",
    )(first, pieces)


def behind_kernel(in_ref, *refs):
    refs[-1][...] = in_ref[...]


def behind(value, after):
    vmem = pl.BlockSpec(memory_space=pltpu.VMEM)
    return pl.pallas_call(
        behind_kernel,
        out_shape=jax.ShapeDtypeStruct(value.shape, value.dtype),
        in_specs=[vmem] + [pl.BlockSpec(memory_space=pl.ANY)] * len(after),
        out_specs=vmem,
        compiler_params=params(4),
        name="behind",
    )(value, *after)


def gram_kernel(blocks, rows_ref, *refs):
    streams, (own_ref, given_ref, cols_ref) = refs[:4], refs[4:]
    lane = lax.broadcasted_iota(jnp.int32, (16, 128), 1)
    terms = jnp.where(lane < 3, 1.0, 0.0).astype(bf16)
    for n, x in enumerate(blocks):
        for z in range(4):
            for s in range(4):
                at = (z if s < 2 else z ^ 2) * PIECE + s * 16
                first = slot_of(s, x, z) * 16
                cols_ref[n * 256 + at : n * 256 + at + 16, :] = streams[s][first : first + 16, :]
        inside = slice(n * 256, (n + 1) * 256)
        product = lax.dot_general(
            rows_ref[:, :LIVE],
            cols_ref[inside, :LIVE],
            (((1,), (1,)), ((), ())),
            preferred_element_type=f32,
        )
        own_ref[:256, inside] = product[:256]
        given_ref[:256, inside] = product[256:]
        sums = lax.dot_general(
            terms, cols_ref[inside, LIVE:], (((1,), (1,)), ((), ())), preferred_element_type=f32
        )
        own_ref[256:, inside] = sums[:8]
        given_ref[256:, inside] = sums[:8]


def gram(blocks, rows, streams):
    vmem = pl.BlockSpec(memory_space=pltpu.VMEM)
    width = 256 * len(blocks)
    return pl.pallas_call(
        lambda *refs: gram_kernel(blocks, *refs),
        out_shape=(jax.ShapeDtypeStruct((264, width), f32),) * 2,
        in_specs=[vmem] * 5,
        out_specs=(vmem,) * 2,
        scratch_shapes=[pltpu.VMEM((width, LONG), bf16)],
        compiler_params=params(10),
        cost_estimate=pl.CostEstimate(
            flops=2 * 512 * width * LIVE, bytes_accessed=6 * 1024 * 1024, transcendentals=0
        ),
        name="gram",
    )(rows, *streams)


def finish_kernel(info_ref, part_ref, *refs):
    own, got, (mean_ref, out_ref) = refs[:2], refs[2:4], refs[4:]
    core, row_first, col_first = info_ref[0], info_ref[1], info_ref[2]
    part = part_ref[0]
    row = row_first + lax.broadcasted_iota(jnp.int32, (256, 256), 0)
    col = col_first + lax.broadcasted_iota(jnp.int32, (256, 256), 1)
    for x in range(4):
        inside = slice(x % 2 * 256, (x % 2 + 1) * 256)
        for ref, which in ((own[x // 2], core), (got[x // 2], 1 - core)):
            at = pl.multiple_of(x * 512 + which * 256, 256)
            out_ref[:, pl.ds(at, 256)] = jnp.where(row <= col + at, ref[:256, inside] * part, 0.0)
            mean_ref[:, pl.ds(at, 256)] = ref[256:264, inside][:1] * part


def finish(info, part, own, got):
    vmem = pl.BlockSpec(memory_space=pltpu.VMEM)
    return pl.pallas_call(
        finish_kernel,
        out_shape=(
            jax.ShapeDtypeStruct((1, WIDTH), f32),
            jax.ShapeDtypeStruct((256, WIDTH), f32),
        ),
        in_specs=[pl.BlockSpec(memory_space=pltpu.SMEM)] * 2 + [vmem] * 4,
        out_specs=(vmem,) * 2,
        compiler_params=params(10),
        name="finish",
    )(info, part, *own, *got)


def swap(value):
    return lax.ppermute(value, "c", [(0, 1), (1, 0)])


def trade(value, axis, flip):
    return lax.ppermute(value, axis, [(i, i ^ flip) for i in range(4)])


def join(*values):
    return jnp.concatenate(values, axis=0)


def meet(value, axis, flip, which):
    got = trade(value, axis, flip)
    return join(jnp.where(which == 0, value, got), jnp.where(which == 0, got, value))


def per_device(resid, norm_gain, keep_index, counts):
    z, x, c, y = (lax.axis_index(a) for a in ("z", "x", "c", "y"))
    picked, sums = pick(resid, keep_index, counts)
    all_sums = [sums] + [trade(sums, "y", flip) for flip in (1, 2, 3)]
    pieces = norm(counts, picked, norm_gain[:, None], all_sums)
    pieces = lax.all_to_all(pieces, TOK, 0, 0, tiled=True)

    loads = jnp.sum((pieces[:, 0, :] < jnp.inf).astype(jnp.int32), axis=1)
    first = jnp.cumsum(loads) - loads
    part = 1.0 / jnp.sum(loads).astype(f32)
    *halves, s0, s1, s2, s3 = pack(first, pieces)
    streams, turned = [s0, s1, s2, s3], []

    def send(half, turn):
        places = [(q, u) for q in range(4) for u in range(4)]
        return lax.ppermute(half, ("z", "y"), [(q * 4 + u, u * 4 + (q ^ u ^ turn)) for q, u in places])

    turned.append(send(halves[0], 0))

    for step in range(4):
        for s in range(4):
            axis, flip = PARTNERS[(s + step) % 4]
            seen = [PARTNERS[(s + k) % 4][0] for k in range(step)]
            which = side(x if axis == "x" else z, flip, axis not in seen)
            streams[s] = meet(streams[s], axis, flip, which)
        if step == 0:
            turned.append(send(behind(halves[1], streams[:1]), 2))
        if step == 1:
            rows = behind(join(*turned), streams)

    q = y ^ z
    rows = meet(rows, "y", 1, side(q, 1, True))
    rows = meet(rows, "y", 3, side(q, 3, False))
    rows = join(rows, swap(rows))

    own, got = [], []
    for blocks in ((0, 1), (2, 3)):
        kept, given = gram(blocks, rows, streams)
        own.append(kept)
        got.append(swap(given))
    info = jnp.stack([c, (z * 8 + x * 2 + c) * 256, y * WIDTH]).astype(jnp.int32)
    mean, gram_factor = finish(info, part[None], own, got)
    return (mean[0], gram_factor)


def solution(mesh):
    fine = Mesh(mesh.devices.reshape(4, 4, 2, 4), ("z", "x", "c", "y"))
    return jax.shard_map(
        per_device,
        mesh=fine,
        in_specs=(P(TOK, "y"), P("y"), P(TOK), P(TOK)),
        out_specs=(P("y"), P(TOK, "y")),
        check_vma=False,
    )
```

```python
import jax
import jax.numpy as jnp
from jax import lax
from jax.experimental import pallas as pl
from jax.experimental.pallas import tpu as pltpu
from jax.sharding import Mesh, PartitionSpec as P

epsilon = 1e-05
TOK = ("z", "x", "c")
SLOTS = 256
LIVE = 4096
WIDTH = 2048
PIECE = 64
LONG = LIVE + 128
MIB = 1024 * 1024
bf16 = jnp.bfloat16
f32 = jnp.float32


def params(mib):
    return pltpu.CompilerParams(vmem_limit_bytes=mib * MIB)


def spread(value, place):
    high = value.astype(bf16).astype(f32)
    middle = (value - high).astype(bf16).astype(f32)
    low = value - high - middle
    rest = jnp.where(place == 2, low, 0.0)
    return jnp.where(place == 0, high, jnp.where(place == 1, middle, rest))


PARTNERS = (("x", 1), ("z", 1), ("x", 3), ("z", 3))


def side(place, flip, first):
    if flip == 1 and not first:
        return (place ^ (place >> 1)) & 1
    return place & 1 if flip == 1 else place >> 1


def slot_of(s, x, z):
    at, seen = 0, []
    for step in range(4):
        axis, flip = PARTNERS[(s + step) % 4]
        at += side(x if axis == "x" else z, flip, axis not in seen) << step
        seen.append(axis)
    return at


def live_slots(counts_ref):
    slot = lax.broadcasted_iota(jnp.int32, (1, SLOTS), 1)
    half = SLOTS // 2
    return slot < jnp.where(slot < half, counts_ref[0], half + counts_ref[1])


def pick_kernel(index_ref, counts_ref, resid_ref, picked_ref, sums_ref):
    tokens = resid_ref.shape[0]
    token = lax.broadcasted_iota(jnp.int32, (tokens, SLOTS), 0)
    kept = jnp.where(live_slots(counts_ref), index_ref[...], -1)
    one_hot = jnp.where(token == kept, 1.0, 0.0).astype(bf16)
    total = jnp.zeros((1, SLOTS), f32)
    step = 512
    for k in range(WIDTH // step):
        part = lax.dot_general(
            resid_ref[:, k * step : (k + 1) * step],
            one_hot,
            (((0,), (0,)), ((), ())),
            preferred_element_type=f32,
        )
        total += jnp.sum(part * part, axis=0, keepdims=True)
        picked_ref[k * step : (k + 1) * step, :] = part.astype(bf16)
    sums_ref[...] = jnp.broadcast_to(total, sums_ref.shape)


def pick(resid, keep_index, counts):
    vmem = pl.BlockSpec(memory_space=pltpu.VMEM)
    return pl.pallas_call(
        pick_kernel,
        out_shape=(
            jax.ShapeDtypeStruct((WIDTH, SLOTS), bf16),
            jax.ShapeDtypeStruct((8, SLOTS), f32),
        ),
        in_specs=[vmem, pl.BlockSpec(memory_space=pltpu.SMEM), vmem],
        out_specs=(vmem,) * 2,
        compiler_params=params(16),
        name="pick",
    )(keep_index[None, :], counts, resid)


def norm_kernel(counts_ref, picked_ref, gain_ref, s0, s1, s2, s3, out_ref):
    squares = (s0[:1, :] + s2[:1, :]) + (s1[:1, :] + s3[:1, :])
    scale = lax.rsqrt(squares / 8192 + epsilon)
    row = lax.broadcasted_iota(jnp.int32, (32, 1), 0)
    mark = jnp.where(row == 0, jnp.where(live_slots(counts_ref), 0.0, jnp.inf), 0.0).astype(bf16)
    for x in range(4):
        for c in range(2):
            first = (x * 2 + c) * 256
            rows = picked_ref[first : first + 256, :].astype(f32)
            short = (rows * scale * gain_ref[first : first + 256, :]).astype(bf16)
            for z in range(4):
                low, high = z * PIECE, (z ^ 2) * PIECE + 32
                out_ref[z * 8 + x * 2 + c, :32, :] = short[low : low + 32, :] + mark
                out_ref[z * 8 + x * 2 + c, 32:, :] = short[high : high + 32, :]


def norm(counts, picked, gain, sums):
    return pl.pallas_call(
        norm_kernel,
        out_shape=jax.ShapeDtypeStruct((32, PIECE, SLOTS), bf16),
        in_specs=[pl.BlockSpec(memory_space=pltpu.SMEM)] + [pl.BlockSpec(memory_space=pltpu.VMEM)] * 6,
        out_specs=pl.BlockSpec(memory_space=pltpu.VMEM),
        compiler_params=params(10),
        name="norm",
    )(counts, picked, gain, *sums)


def pack_kernel(first_ref, in_ref, *refs):
    out_refs, acc_ref = refs[:-1], refs[-1]
    acc_ref[...] = jnp.zeros_like(acc_ref)
    group = 4

    def body(g, _):
        moved = []
        for k in range(group):
            t = g * group + k
            rows = in_ref[t].astype(f32)
            rows = jnp.where(rows < jnp.inf, rows, 0.0)
            first = first_ref[t]
            base = pl.multiple_of((first // 128) * 128, 128)
            wide = jnp.concatenate([rows, jnp.zeros((PIECE, 128), f32)], axis=1)
            moved.append((base, pltpu.roll(wide, first - base, 1)))
        for base, rows in moved:
            acc_ref[:, pl.ds(base, SLOTS + 128)] += rows
        return 0

    lax.fori_loop(0, 32 // group, body, 0)
    for k, ref in enumerate(out_refs[2:]):
        rows = acc_ref[k * 16 : (k + 1) * 16, :LIVE]
        lane = lax.broadcasted_iota(jnp.int32, (16, 128), 1)
        sums = spread(jnp.sum(rows, axis=1, keepdims=True), lane)
        for into in (ref, out_refs[k // 2].at[pl.ds(k % 2 * 16, 16)]):
            into[:, :LIVE] = rows.astype(bf16)
            into[:, LIVE:] = sums.astype(bf16)


def pack(first, pieces):
    vmem = pl.BlockSpec(memory_space=pltpu.VMEM)
    return pl.pallas_call(
        pack_kernel,
        out_shape=(jax.ShapeDtypeStruct((32, LONG), bf16),) * 2
        + (jax.ShapeDtypeStruct((16, LONG), bf16),) * 4,
        in_specs=[pl.BlockSpec(memory_space=pltpu.SMEM), vmem],
        out_specs=(vmem,) * 6,
        scratch_shapes=[pltpu.VMEM((PIECE, LIVE + SLOTS + 128), f32)],
        compiler_params=params(10),
        name="pack",
    )(first, pieces)


def behind_kernel(in_ref, *refs):
    refs[-1][...] = in_ref[...]


def behind(value, after):
    vmem = pl.BlockSpec(memory_space=pltpu.VMEM)
    return pl.pallas_call(
        behind_kernel,
        out_shape=jax.ShapeDtypeStruct(value.shape, value.dtype),
        in_specs=[vmem] + [pl.BlockSpec(memory_space=pl.ANY)] * len(after),
        out_specs=vmem,
        compiler_params=params(4),
        name="behind",
    )(value, *after)


def gram_kernel(blocks, rows_ref, *refs):
    streams, (own_ref, given_ref, cols_ref) = refs[:4], refs[4:]
    lane = lax.broadcasted_iota(jnp.int32, (16, 128), 1)
    terms = jnp.where(lane < 3, 1.0, 0.0).astype(bf16)
    for n, x in enumerate(blocks):
        for z in range(4):
            for s in range(4):
                at = (z if s < 2 else z ^ 2) * PIECE + s * 16
                first = slot_of(s, x, z) * 16
                cols_ref[n * 256 + at : n * 256 + at + 16, :] = streams[s][first : first + 16, :]
        inside = slice(n * 256, (n + 1) * 256)
        product = lax.dot_general(
            rows_ref[:, :LIVE],
            cols_ref[inside, :LIVE],
            (((1,), (1,)), ((), ())),
            preferred_element_type=f32,
        )
        own_ref[:256, inside] = product[:256]
        given_ref[:256, inside] = product[256:]
        sums = lax.dot_general(
            terms, cols_ref[inside, LIVE:], (((1,), (1,)), ((), ())), preferred_element_type=f32
        )
        own_ref[256:, inside] = sums[:8]
        given_ref[256:, inside] = sums[:8]


def gram(blocks, rows, streams):
    vmem = pl.BlockSpec(memory_space=pltpu.VMEM)
    width = 256 * len(blocks)
    return pl.pallas_call(
        lambda *refs: gram_kernel(blocks, *refs),
        out_shape=(jax.ShapeDtypeStruct((264, width), f32),) * 2,
        in_specs=[vmem] * 5,
        out_specs=(vmem,) * 2,
        scratch_shapes=[pltpu.VMEM((width, LONG), bf16)],
        compiler_params=params(10),
        cost_estimate=pl.CostEstimate(
            flops=2 * 512 * width * LIVE, bytes_accessed=6 * 1024 * 1024, transcendentals=0
        ),
        name="gram",
    )(rows, *streams)


def finish_kernel(info_ref, part_ref, *refs):
    own, got, (mean_ref, out_ref) = refs[:2], refs[2:4], refs[4:]
    core, row_first, col_first = info_ref[0], info_ref[1], info_ref[2]
    part = part_ref[0]
    row = row_first + lax.broadcasted_iota(jnp.int32, (256, 256), 0)
    col = col_first + lax.broadcasted_iota(jnp.int32, (256, 256), 1)
    for x in range(4):
        inside = slice(x % 2 * 256, (x % 2 + 1) * 256)
        for ref, which in ((own[x // 2], core), (got[x // 2], 1 - core)):
            at = pl.multiple_of(x * 512 + which * 256, 256)
            out_ref[:, pl.ds(at, 256)] = jnp.where(row <= col + at, ref[:256, inside] * part, 0.0)
            mean_ref[:, pl.ds(at, 256)] = ref[256:264, inside][:1] * part


def finish(info, part, own, got):
    vmem = pl.BlockSpec(memory_space=pltpu.VMEM)
    return pl.pallas_call(
        finish_kernel,
        out_shape=(
            jax.ShapeDtypeStruct((1, WIDTH), f32),
            jax.ShapeDtypeStruct((256, WIDTH), f32),
        ),
        in_specs=[pl.BlockSpec(memory_space=pltpu.SMEM)] * 2 + [vmem] * 4,
        out_specs=(vmem,) * 2,
        compiler_params=params(10),
        name="finish",
    )(info, part, *own, *got)


def swap(value):
    return lax.ppermute(value, "c", [(0, 1), (1, 0)])


def trade(value, axis, flip):
    return lax.ppermute(value, axis, [(i, i ^ flip) for i in range(4)])


def join(*values):
    return jnp.concatenate(values, axis=0)


def meet(value, axis, flip, which):
    got = trade(value, axis, flip)
    return join(jnp.where(which == 0, value, got), jnp.where(which == 0, got, value))


def per_device(resid, norm_gain, keep_index, counts):
    z, x, c, y = (lax.axis_index(a) for a in ("z", "x", "c", "y"))
    picked, sums = pick(resid, keep_index, counts)
    all_sums = [sums] + [trade(sums, "y", flip) for flip in (1, 2, 3)]
    pieces = norm(counts, picked, norm_gain[:, None], all_sums)
    pieces = lax.all_to_all(pieces, TOK, 0, 0, tiled=True)

    loads = jnp.sum((pieces[:, 0, :] < jnp.inf).astype(jnp.int32), axis=1)
    first = jnp.cumsum(loads) - loads
    part = 1.0 / jnp.sum(loads).astype(f32)
    *halves, s0, s1, s2, s3 = pack(first, pieces)
    streams = [s0, s1, s2, s3]

    def send(half, turn):
        places = [(q, u) for q in range(4) for u in range(4)]
        return lax.ppermute(half, ("z", "y"), [(q * 4 + u, u * 4 + (q ^ u ^ turn)) for q, u in places])

    for step in range(4):
        for s in range(4):
            axis, flip = PARTNERS[(s + step) % 4]
            seen = [PARTNERS[(s + k) % 4][0] for k in range(step)]
            which = side(x if axis == "x" else z, flip, axis not in seen)
            streams[s] = meet(streams[s], axis, flip, which)
        if step == 0:
            turned = [send(behind(half, streams), turn) for half, turn in zip(halves, (0, 2))]
        if step == 2:
            rows = behind(join(*turned), streams[:1])

    q = y ^ z
    rows = meet(rows, "y", 1, side(q, 1, True))
    rows = meet(rows, "y", 3, side(q, 3, False))
    rows = join(rows, swap(rows))

    own, got = [], []
    for blocks in ((0, 1), (2, 3)):
        kept, given = gram(blocks, rows, streams)
        own.append(kept)
        got.append(swap(given))
    info = jnp.stack([c, (z * 8 + x * 2 + c) * 256, y * WIDTH]).astype(jnp.int32)
    mean, gram_factor = finish(info, part[None], own, got)
    return (mean[0], gram_factor)


def solution(mesh):
    fine = Mesh(mesh.devices.reshape(4, 4, 2, 4), ("z", "x", "c", "y"))
    return jax.shard_map(
        per_device,
        mesh=fine,
        in_specs=(P(TOK, "y"), P("y"), P(TOK), P(TOK)),
        out_specs=(P("y"), P(TOK, "y")),
        check_vma=False,
    )
```

```python
import jax
import jax.numpy as jnp
from jax import lax
from jax.experimental import pallas as pl
from jax.experimental.pallas import tpu as pltpu
from jax.sharding import Mesh, PartitionSpec as P

epsilon = 1e-05
TOK = ("z", "x", "c")
SLOTS = 256
LIVE = 4096
WIDTH = 2048
PIECE = 64
LONG = LIVE + 128
MIB = 1024 * 1024
bf16 = jnp.bfloat16
f32 = jnp.float32


def params(mib):
    return pltpu.CompilerParams(vmem_limit_bytes=mib * MIB)


def spread(value, place):
    high = value.astype(bf16).astype(f32)
    middle = (value - high).astype(bf16).astype(f32)
    low = value - high - middle
    rest = jnp.where(place == 2, low, 0.0)
    return jnp.where(place == 0, high, jnp.where(place == 1, middle, rest))


PARTNERS = (("x", 1), ("z", 1), ("x", 3), ("z", 3))


def side(place, flip, first):
    if flip == 1 and not first:
        return (place ^ (place >> 1)) & 1
    return place & 1 if flip == 1 else place >> 1


def slot_of(s, x, z):
    at, seen = 0, []
    for step in range(4):
        axis, flip = PARTNERS[(s + step) % 4]
        at += side(x if axis == "x" else z, flip, axis not in seen) << step
        seen.append(axis)
    return at


def live_slots(counts_ref):
    slot = lax.broadcasted_iota(jnp.int32, (1, SLOTS), 1)
    half = SLOTS // 2
    return slot < jnp.where(slot < half, counts_ref[0], half + counts_ref[1])


def pick_kernel(index_ref, counts_ref, resid_ref, picked_ref, sums_ref):
    tokens = resid_ref.shape[0]
    token = lax.broadcasted_iota(jnp.int32, (tokens, SLOTS), 0)
    kept = jnp.where(live_slots(counts_ref), index_ref[...], -1)
    one_hot = jnp.where(token == kept, 1.0, 0.0).astype(bf16)
    total = jnp.zeros((1, SLOTS), f32)
    step = 512
    for k in range(WIDTH // step):
        part = lax.dot_general(
            resid_ref[:, k * step : (k + 1) * step],
            one_hot,
            (((0,), (0,)), ((), ())),
            preferred_element_type=f32,
        )
        total += jnp.sum(part * part, axis=0, keepdims=True)
        picked_ref[k * step : (k + 1) * step, :] = part.astype(bf16)
    sums_ref[...] = jnp.broadcast_to(total, sums_ref.shape)


def pick(resid, keep_index, counts):
    vmem = pl.BlockSpec(memory_space=pltpu.VMEM)
    return pl.pallas_call(
        pick_kernel,
        out_shape=(
            jax.ShapeDtypeStruct((WIDTH, SLOTS), bf16),
            jax.ShapeDtypeStruct((8, SLOTS), f32),
        ),
        in_specs=[vmem, pl.BlockSpec(memory_space=pltpu.SMEM), vmem],
        out_specs=(vmem,) * 2,
        compiler_params=params(16),
        name="pick",
    )(keep_index[None, :], counts, resid)


def norm_kernel(counts_ref, picked_ref, gain_ref, s0, s1, s2, s3, out_ref):
    squares = (s0[:1, :] + s2[:1, :]) + (s1[:1, :] + s3[:1, :])
    scale = lax.rsqrt(squares / 8192 + epsilon)
    row = lax.broadcasted_iota(jnp.int32, (32, 1), 0)
    mark = jnp.where(row == 0, jnp.where(live_slots(counts_ref), 0.0, jnp.inf), 0.0).astype(bf16)
    for x in range(4):
        for c in range(2):
            first = (x * 2 + c) * 256
            rows = picked_ref[first : first + 256, :].astype(f32)
            short = (rows * scale * gain_ref[first : first + 256, :]).astype(bf16)
            for z in range(4):
                low, high = z * PIECE, (z ^ 2) * PIECE + 32
                out_ref[z * 8 + x * 2 + c, :32, :] = short[low : low + 32, :] + mark
                out_ref[z * 8 + x * 2 + c, 32:, :] = short[high : high + 32, :]


def norm(counts, picked, gain, sums):
    return pl.pallas_call(
        norm_kernel,
        out_shape=jax.ShapeDtypeStruct((32, PIECE, SLOTS), bf16),
        in_specs=[pl.BlockSpec(memory_space=pltpu.SMEM)] + [pl.BlockSpec(memory_space=pltpu.VMEM)] * 6,
        out_specs=pl.BlockSpec(memory_space=pltpu.VMEM),
        compiler_params=params(10),
        name="norm",
    )(counts, picked, gain, *sums)


def pack_kernel(first_ref, in_ref, *refs):
    out_refs, acc_ref = refs[:-1], refs[-1]
    acc_ref[...] = jnp.zeros_like(acc_ref)
    group = 4

    def body(g, _):
        moved = []
        for k in range(group):
            t = g * group + k
            rows = in_ref[t].astype(f32)
            rows = jnp.where(rows < jnp.inf, rows, 0.0)
            first = first_ref[t]
            base = pl.multiple_of((first // 128) * 128, 128)
            wide = jnp.concatenate([rows, jnp.zeros((PIECE, 128), f32)], axis=1)
            moved.append((base, pltpu.roll(wide, first - base, 1)))
        for base, rows in moved:
            acc_ref[:, pl.ds(base, SLOTS + 128)] += rows
        return 0

    lax.fori_loop(0, 32 // group, body, 0)
    for k, ref in enumerate(out_refs[2:]):
        rows = acc_ref[k * 16 : (k + 1) * 16, :LIVE]
        lane = lax.broadcasted_iota(jnp.int32, (16, 128), 1)
        sums = spread(jnp.sum(rows, axis=1, keepdims=True), lane)
        for into in (ref, out_refs[k // 2].at[pl.ds(k % 2 * 16, 16)]):
            into[:, :LIVE] = rows.astype(bf16)
            into[:, LIVE:] = sums.astype(bf16)


def pack(first, pieces):
    vmem = pl.BlockSpec(memory_space=pltpu.VMEM)
    return pl.pallas_call(
        pack_kernel,
        out_shape=(jax.ShapeDtypeStruct((32, LONG), bf16),) * 2
        + (jax.ShapeDtypeStruct((16, LONG), bf16),) * 4,
        in_specs=[pl.BlockSpec(memory_space=pltpu.SMEM), vmem],
        out_specs=(vmem,) * 6,
        scratch_shapes=[pltpu.VMEM((PIECE, LIVE + SLOTS + 128), f32)],
        compiler_params=params(10),
        name="pack",
    )(first, pieces)


def behind_kernel(in_ref, *refs):
    refs[-1][...] = in_ref[...]


def behind(value, after):
    vmem = pl.BlockSpec(memory_space=pltpu.VMEM)
    return pl.pallas_call(
        behind_kernel,
        out_shape=jax.ShapeDtypeStruct(value.shape, value.dtype),
        in_specs=[vmem] + [pl.BlockSpec(memory_space=pl.ANY)] * len(after),
        out_specs=vmem,
        compiler_params=params(4),
        name="behind",
    )(value, *after)


def gram_kernel(blocks, rows_ref, *refs):
    streams, (own_ref, given_ref, cols_ref) = refs[:4], refs[4:]
    lane = lax.broadcasted_iota(jnp.int32, (16, 128), 1)
    terms = jnp.where(lane < 3, 1.0, 0.0).astype(bf16)
    for n, x in enumerate(blocks):
        for z in range(4):
            for s in range(4):
                at = (z if s < 2 else z ^ 2) * PIECE + s * 16
                first = slot_of(s, x, z) * 16
                cols_ref[n * 256 + at : n * 256 + at + 16, :] = streams[s][first : first + 16, :]
        inside = slice(n * 256, (n + 1) * 256)
        product = lax.dot_general(
            rows_ref[:, :LIVE],
            cols_ref[inside, :LIVE],
            (((1,), (1,)), ((), ())),
            preferred_element_type=f32,
        )
        own_ref[:256, inside] = product[:256]
        given_ref[:256, inside] = product[256:]
        sums = lax.dot_general(
            terms, cols_ref[inside, LIVE:], (((1,), (1,)), ((), ())), preferred_element_type=f32
        )
        own_ref[256:, inside] = sums[:8]
        given_ref[256:, inside] = sums[:8]


def gram(blocks, rows, streams):
    vmem = pl.BlockSpec(memory_space=pltpu.VMEM)
    width = 256 * len(blocks)
    return pl.pallas_call(
        lambda *refs: gram_kernel(blocks, *refs),
        out_shape=(jax.ShapeDtypeStruct((264, width), f32),) * 2,
        in_specs=[vmem] * 5,
        out_specs=(vmem,) * 2,
        scratch_shapes=[pltpu.VMEM((width, LONG), bf16)],
        compiler_params=params(10),
        cost_estimate=pl.CostEstimate(
            flops=2 * 512 * width * LIVE, bytes_accessed=6 * 1024 * 1024, transcendentals=0
        ),
        name="gram",
    )(rows, *streams)


def finish_kernel(info_ref, part_ref, *refs):
    own, got, (mean_ref, out_ref) = refs[:2], refs[2:4], refs[4:]
    core, row_first, col_first = info_ref[0], info_ref[1], info_ref[2]
    part = part_ref[0]
    row = row_first + lax.broadcasted_iota(jnp.int32, (256, 256), 0)
    col = col_first + lax.broadcasted_iota(jnp.int32, (256, 256), 1)
    for x in range(4):
        inside = slice(x % 2 * 256, (x % 2 + 1) * 256)
        for ref, which in ((own[x // 2], core), (got[x // 2], 1 - core)):
            at = pl.multiple_of(x * 512 + which * 256, 256)
            out_ref[:, pl.ds(at, 256)] = jnp.where(row <= col + at, ref[:256, inside] * part, 0.0)
            mean_ref[:, pl.ds(at, 256)] = ref[256:264, inside][:1] * part


def finish(info, part, own, got):
    vmem = pl.BlockSpec(memory_space=pltpu.VMEM)
    return pl.pallas_call(
        finish_kernel,
        out_shape=(
            jax.ShapeDtypeStruct((1, WIDTH), f32),
            jax.ShapeDtypeStruct((256, WIDTH), f32),
        ),
        in_specs=[pl.BlockSpec(memory_space=pltpu.SMEM)] * 2 + [vmem] * 4,
        out_specs=(vmem,) * 2,
        compiler_params=params(10),
        name="finish",
    )(info, part, *own, *got)


def swap(value):
    return lax.ppermute(value, "c", [(0, 1), (1, 0)])


def trade(value, axis, flip):
    return lax.ppermute(value, axis, [(i, i ^ flip) for i in range(4)])


def join(*values):
    return jnp.concatenate(values, axis=0)


def meet(value, axis, flip, which):
    got = trade(value, axis, flip)
    return join(jnp.where(which == 0, value, got), jnp.where(which == 0, got, value))


def per_device(resid, norm_gain, keep_index, counts):
    z, x, c, y = (lax.axis_index(a) for a in ("z", "x", "c", "y"))
    picked, sums = pick(resid, keep_index, counts)
    all_sums = [sums] + [trade(sums, "y", flip) for flip in (1, 2, 3)]
    pieces = norm(counts, picked, norm_gain[:, None], all_sums)
    pieces = lax.all_to_all(pieces, TOK, 0, 0, tiled=True)

    loads = jnp.sum((pieces[:, 0, :] < jnp.inf).astype(jnp.int32), axis=1)
    first = jnp.cumsum(loads) - loads
    part = 1.0 / jnp.sum(loads).astype(f32)
    *halves, s0, s1, s2, s3 = pack(first, pieces)
    streams = [s0, s1, s2, s3]

    def send(half, turn):
        places = [(q, u) for q in range(4) for u in range(4)]
        return lax.ppermute(half, ("z", "y"), [(q * 4 + u, u * 4 + (q ^ u ^ turn)) for q, u in places])

    for step in range(4):
        for s in range(4):
            axis, flip = PARTNERS[(s + step) % 4]
            seen = [PARTNERS[(s + k) % 4][0] for k in range(step)]
            which = side(x if axis == "x" else z, flip, axis not in seen)
            streams[s] = meet(streams[s], axis, flip, which)
        if step == 0:
            turned = [send(behind(halves[0], streams[:1]), 0), send(behind(halves[1], streams), 2)]
        if step == 1:
            rows = behind(join(*turned), streams)

    q = y ^ z
    rows = meet(rows, "y", 1, side(q, 1, True))
    rows = meet(rows, "y", 3, side(q, 3, False))
    rows = join(rows, swap(rows))

    own, got = [], []
    for blocks in ((0, 1), (2, 3)):
        kept, given = gram(blocks, rows, streams)
        own.append(kept)
        got.append(swap(given))
    info = jnp.stack([c, (z * 8 + x * 2 + c) * 256, y * WIDTH]).astype(jnp.int32)
    mean, gram_factor = finish(info, part[None], own, got)
    return (mean[0], gram_factor)


def solution(mesh):
    fine = Mesh(mesh.devices.reshape(4, 4, 2, 4), ("z", "x", "c", "y"))
    return jax.shard_map(
        per_device,
        mesh=fine,
        in_specs=(P(TOK, "y"), P("y"), P(TOK), P(TOK)),
        out_specs=(P("y"), P(TOK, "y")),
        check_vma=False,
    )
```

```python
import jax
import jax.numpy as jnp
from jax import lax
from jax.experimental import pallas as pl
from jax.experimental.pallas import tpu as pltpu
from jax.sharding import Mesh, PartitionSpec as P

epsilon = 1e-05
TOK = ("z", "x", "c")
SLOTS = 256
LIVE = 4096
WIDTH = 2048
PIECE = 64
LONG = LIVE + 128
MIB = 1024 * 1024
bf16 = jnp.bfloat16
f32 = jnp.float32


def params(mib):
    return pltpu.CompilerParams(vmem_limit_bytes=mib * MIB)


def spread(value, place):
    high = value.astype(bf16).astype(f32)
    middle = (value - high).astype(bf16).astype(f32)
    low = value - high - middle
    rest = jnp.where(place == 2, low, 0.0)
    return jnp.where(place == 0, high, jnp.where(place == 1, middle, rest))


PARTNERS = (("x", 1), ("z", 1), ("x", 3), ("z", 3))


def side(place, flip, first):
    if flip == 1 and not first:
        return (place ^ (place >> 1)) & 1
    return place & 1 if flip == 1 else place >> 1


def slot_of(s, x, z):
    at, seen = 0, []
    for step in range(4):
        axis, flip = PARTNERS[(s + step) % 4]
        at += side(x if axis == "x" else z, flip, axis not in seen) << step
        seen.append(axis)
    return at


def live_slots(kept_ref):
    slot = lax.broadcasted_iota(jnp.int32, (1, SLOTS), 1)
    half = SLOTS // 2
    counts = kept_ref[:, SLOTS : SLOTS + 128]
    return slot < jnp.where(slot < half, counts[:, 0:1], half + counts[:, 1:2])


def pick_kernel(kept_ref, resid_ref, picked_ref, sums_ref):
    tokens = resid_ref.shape[0]
    token = lax.broadcasted_iota(jnp.int32, (tokens, SLOTS), 0)
    kept = jnp.where(live_slots(kept_ref), kept_ref[:, :SLOTS], -1)
    one_hot = jnp.where(token == kept, 1.0, 0.0).astype(bf16)
    total = jnp.zeros((1, SLOTS), f32)
    step = 512
    for k in range(WIDTH // step):
        part = lax.dot_general(
            resid_ref[:, k * step : (k + 1) * step],
            one_hot,
            (((0,), (0,)), ((), ())),
            preferred_element_type=f32,
        )
        total += jnp.sum(part * part, axis=0, keepdims=True)
        picked_ref[k * step : (k + 1) * step, :] = part.astype(bf16)
    sums_ref[...] = jnp.broadcast_to(total, sums_ref.shape)


def pick(resid, kept):
    vmem = pl.BlockSpec(memory_space=pltpu.VMEM)
    return pl.pallas_call(
        pick_kernel,
        out_shape=(
            jax.ShapeDtypeStruct((WIDTH, SLOTS), bf16),
            jax.ShapeDtypeStruct((8, SLOTS), f32),
        ),
        in_specs=[vmem] * 2,
        out_specs=(vmem,) * 2,
        compiler_params=params(16),
        name="pick",
    )(kept, resid)


def norm_kernel(kept_ref, picked_ref, gain_ref, s0, s1, s2, s3, out_ref):
    squares = (s0[:1, :] + s2[:1, :]) + (s1[:1, :] + s3[:1, :])
    scale = lax.rsqrt(squares / 8192 + epsilon)
    row = lax.broadcasted_iota(jnp.int32, (32, 1), 0)
    mark = jnp.where(row == 0, jnp.where(live_slots(kept_ref), 0.0, jnp.inf), 0.0).astype(bf16)
    for x in range(4):
        for c in range(2):
            first = (x * 2 + c) * 256
            rows = picked_ref[first : first + 256, :].astype(f32)
            short = (rows * scale * gain_ref[first : first + 256, :]).astype(bf16)
            for z in range(4):
                low, high = z * PIECE, (z ^ 2) * PIECE + 32
                out_ref[z * 8 + x * 2 + c, :32, :] = short[low : low + 32, :] + mark
                out_ref[z * 8 + x * 2 + c, 32:, :] = short[high : high + 32, :]


def norm(kept, picked, gain, sums):
    return pl.pallas_call(
        norm_kernel,
        out_shape=jax.ShapeDtypeStruct((32, PIECE, SLOTS), bf16),
        in_specs=[pl.BlockSpec(memory_space=pltpu.VMEM)] * 7,
        out_specs=pl.BlockSpec(memory_space=pltpu.VMEM),
        compiler_params=params(10),
        name="norm",
    )(kept, picked, gain, *sums)


def pack_kernel(first_ref, in_ref, *refs):
    out_refs, acc_ref = refs[:-1], refs[-1]
    acc_ref[...] = jnp.zeros_like(acc_ref)
    group = 4

    def body(g, _):
        moved = []
        for k in range(group):
            t = g * group + k
            rows = in_ref[t].astype(f32)
            rows = jnp.where(rows < jnp.inf, rows, 0.0)
            first = first_ref[t]
            base = pl.multiple_of((first // 128) * 128, 128)
            wide = jnp.concatenate([rows, jnp.zeros((PIECE, 128), f32)], axis=1)
            moved.append((base, pltpu.roll(wide, first - base, 1)))
        for base, rows in moved:
            acc_ref[:, pl.ds(base, SLOTS + 128)] += rows
        return 0

    lax.fori_loop(0, 32 // group, body, 0)
    for k, ref in enumerate(out_refs[2:]):
        rows = acc_ref[k * 16 : (k + 1) * 16, :LIVE]
        lane = lax.broadcasted_iota(jnp.int32, (16, 128), 1)
        sums = spread(jnp.sum(rows, axis=1, keepdims=True), lane)
        for into in (ref, out_refs[k // 2].at[pl.ds(k % 2 * 16, 16)]):
            into[:, :LIVE] = rows.astype(bf16)
            into[:, LIVE:] = sums.astype(bf16)


def pack(first, pieces):
    vmem = pl.BlockSpec(memory_space=pltpu.VMEM)
    return pl.pallas_call(
        pack_kernel,
        out_shape=(jax.ShapeDtypeStruct((32, LONG), bf16),) * 2
        + (jax.ShapeDtypeStruct((16, LONG), bf16),) * 4,
        in_specs=[pl.BlockSpec(memory_space=pltpu.SMEM), vmem],
        out_specs=(vmem,) * 6,
        scratch_shapes=[pltpu.VMEM((PIECE, LIVE + SLOTS + 128), f32)],
        compiler_params=params(10),
        name="pack",
    )(first, pieces)


def behind_kernel(in_ref, *refs):
    refs[-1][...] = in_ref[...]


def behind(value, after):
    vmem = pl.BlockSpec(memory_space=pltpu.VMEM)
    return pl.pallas_call(
        behind_kernel,
        out_shape=jax.ShapeDtypeStruct(value.shape, value.dtype),
        in_specs=[vmem] * (1 + len(after)),
        out_specs=vmem,
        compiler_params=params(4),
        name="behind",
    )(value, *after)


def gram_kernel(blocks, rows_ref, *refs):
    streams, (own_ref, given_ref, cols_ref) = refs[:4], refs[4:]
    lane = lax.broadcasted_iota(jnp.int32, (16, 128), 1)
    terms = jnp.where(lane < 3, 1.0, 0.0).astype(bf16)
    for n, x in enumerate(blocks):
        for z in range(4):
            for s in range(4):
                at = (z if s < 2 else z ^ 2) * PIECE + s * 16
                first = slot_of(s, x, z) * 16
                cols_ref[n * 256 + at : n * 256 + at + 16, :] = streams[s][first : first + 16, :]
        inside = slice(n * 256, (n + 1) * 256)
        product = lax.dot_general(
            rows_ref[:, :LIVE],
            cols_ref[inside, :LIVE],
            (((1,), (1,)), ((), ())),
            preferred_element_type=f32,
        )
        own_ref[:256, inside] = product[:256]
        given_ref[:256, inside] = product[256:]
        sums = lax.dot_general(
            terms, cols_ref[inside, LIVE:], (((1,), (1,)), ((), ())), preferred_element_type=f32
        )
        own_ref[256:, inside] = sums[:8]
        given_ref[256:, inside] = sums[:8]


def gram(blocks, rows, streams):
    vmem = pl.BlockSpec(memory_space=pltpu.VMEM)
    width = 256 * len(blocks)
    return pl.pallas_call(
        lambda *refs: gram_kernel(blocks, *refs),
        out_shape=(jax.ShapeDtypeStruct((264, width), f32),) * 2,
        in_specs=[vmem] * 5,
        out_specs=(vmem,) * 2,
        scratch_shapes=[pltpu.VMEM((width, LONG), bf16)],
        compiler_params=params(10),
        cost_estimate=pl.CostEstimate(
            flops=2 * 512 * width * LIVE, bytes_accessed=6 * 1024 * 1024, transcendentals=0
        ),
        name="gram",
    )(rows, *streams)


def finish_kernel(info_ref, part_ref, *refs):
    own, got, (mean_ref, out_ref) = refs[:2], refs[2:4], refs[4:]
    core, row_first, col_first = info_ref[0], info_ref[1], info_ref[2]
    part = part_ref[0]
    row = row_first + lax.broadcasted_iota(jnp.int32, (256, 256), 0)
    col = col_first + lax.broadcasted_iota(jnp.int32, (256, 256), 1)
    for x in range(4):
        inside = slice(x % 2 * 256, (x % 2 + 1) * 256)
        for ref, which in ((own[x // 2], core), (got[x // 2], 1 - core)):
            at = pl.multiple_of(x * 512 + which * 256, 256)
            out_ref[:, pl.ds(at, 256)] = jnp.where(row <= col + at, ref[:256, inside] * part, 0.0)
            mean_ref[:, pl.ds(at, 256)] = ref[256:264, inside][:1] * part


def finish(info, part, own, got):
    vmem = pl.BlockSpec(memory_space=pltpu.VMEM)
    return pl.pallas_call(
        finish_kernel,
        out_shape=(
            jax.ShapeDtypeStruct((1, WIDTH), f32),
            jax.ShapeDtypeStruct((256, WIDTH), f32),
        ),
        in_specs=[pl.BlockSpec(memory_space=pltpu.SMEM)] * 2 + [vmem] * 4,
        out_specs=(vmem,) * 2,
        compiler_params=params(10),
        name="finish",
    )(info, part, *own, *got)


def swap(value):
    return lax.ppermute(value, "c", [(0, 1), (1, 0)])


def trade(value, axis, flip):
    return lax.ppermute(value, axis, [(i, i ^ flip) for i in range(4)])


def join(*values):
    return jnp.concatenate(values, axis=0)


def meet(value, axis, flip, which):
    got = trade(value, axis, flip)
    return join(jnp.where(which == 0, value, got), jnp.where(which == 0, got, value))


def per_device(resid, norm_gain, keep_index, counts):
    z, x, c, y = (lax.axis_index(a) for a in ("z", "x", "c", "y"))
    kept = jnp.concatenate([keep_index, counts, jnp.zeros((126,), jnp.int32)])[None, :]
    picked, sums = pick(resid, kept)
    all_sums = [sums] + [trade(sums, "y", flip) for flip in (1, 2, 3)]
    pieces = norm(kept, picked, norm_gain[:, None], all_sums)
    pieces = lax.all_to_all(pieces, TOK, 0, 0, tiled=True)

    loads = jnp.sum((pieces[:, 0, :] < jnp.inf).astype(jnp.int32), axis=1)
    first = jnp.cumsum(loads) - loads
    part = 1.0 / jnp.sum(loads).astype(f32)
    *halves, s0, s1, s2, s3 = pack(first, pieces)
    streams = [s0, s1, s2, s3]

    def send(half, turn):
        places = [(q, u) for q in range(4) for u in range(4)]
        return lax.ppermute(half, ("z", "y"), [(q * 4 + u, u * 4 + (q ^ u ^ turn)) for q, u in places])

    for step in range(4):
        for s in range(4):
            axis, flip = PARTNERS[(s + step) % 4]
            seen = [PARTNERS[(s + k) % 4][0] for k in range(step)]
            which = side(x if axis == "x" else z, flip, axis not in seen)
            streams[s] = meet(streams[s], axis, flip, which)
        if step == 0:
            turned = [send(behind(halves[0], streams[:1]), 0), send(behind(halves[1], streams), 2)]
        if step == 1:
            rows = meet(behind(join(*turned), streams), "y", 1, side(y ^ z, 1, True))
        if step == 2:
            rows = meet(behind(rows, streams), "y", 3, side(y ^ z, 3, False))

    rows = join(rows, swap(rows))

    own, got = [], []
    for blocks in ((0, 1), (2, 3)):
        kept, given = gram(blocks, rows, streams)
        own.append(kept)
        got.append(swap(given))
    info = jnp.stack([c, (z * 8 + x * 2 + c) * 256, y * WIDTH]).astype(jnp.int32)
    mean, gram_factor = finish(info, part[None], own, got)
    return (mean[0], gram_factor)


def solution(mesh):
    fine = Mesh(mesh.devices.reshape(4, 4, 2, 4), ("z", "x", "c", "y"))
    return jax.shard_map(
        per_device,
        mesh=fine,
        in_specs=(P(TOK, "y"), P("y"), P(TOK), P(TOK)),
        out_specs=(P("y"), P(TOK, "y")),
        check_vma=False,
    )
```

```python
import jax
import jax.numpy as jnp
from jax import lax
from jax.experimental import pallas as pl
from jax.experimental.pallas import tpu as pltpu
from jax.sharding import Mesh, PartitionSpec as P

epsilon = 1e-05
TOK = ("z", "x", "c")
SLOTS = 256
LIVE = 4096
WIDTH = 2048
PIECE = 64
LONG = LIVE + 128
MIB = 1024 * 1024
bf16 = jnp.bfloat16
f32 = jnp.float32


def params(mib):
    return pltpu.CompilerParams(vmem_limit_bytes=mib * MIB)


def spread(value, place):
    high = value.astype(bf16).astype(f32)
    middle = (value - high).astype(bf16).astype(f32)
    low = value - high - middle
    rest = jnp.where(place == 2, low, 0.0)
    return jnp.where(place == 0, high, jnp.where(place == 1, middle, rest))


PARTNERS = (("x", 1), ("z", 1), ("x", 3), ("z", 3))


def side(place, flip, first):
    if flip == 1 and not first:
        return (place ^ (place >> 1)) & 1
    return place & 1 if flip == 1 else place >> 1


def slot_of(s, x, z):
    at, seen = 0, []
    for step in range(4):
        axis, flip = PARTNERS[(s + step) % 4]
        at += side(x if axis == "x" else z, flip, axis not in seen) << step
        seen.append(axis)
    return at


def live_slots(kept_ref):
    slot = lax.broadcasted_iota(jnp.int32, (1, SLOTS), 1)
    half = SLOTS // 2
    counts = kept_ref[:, SLOTS : SLOTS + 128]
    return slot < jnp.where(slot < half, counts[:, 0:1], half + counts[:, 1:2])


def pick_kernel(kept_ref, resid_ref, picked_ref, sums_ref):
    tokens = resid_ref.shape[0]
    token = lax.broadcasted_iota(jnp.int32, (tokens, SLOTS), 0)
    kept = jnp.where(live_slots(kept_ref), kept_ref[:, :SLOTS], -1)
    one_hot = jnp.where(token == kept, 1.0, 0.0).astype(bf16)
    total = jnp.zeros((1, SLOTS), f32)
    step = 512
    for k in range(WIDTH // step):
        part = lax.dot_general(
            resid_ref[:, k * step : (k + 1) * step],
            one_hot,
            (((0,), (0,)), ((), ())),
            preferred_element_type=f32,
        )
        total += jnp.sum(part * part, axis=0, keepdims=True)
        picked_ref[k * step : (k + 1) * step, :] = part.astype(bf16)
    sums_ref[...] = jnp.broadcast_to(total, sums_ref.shape)


def pick(resid, kept):
    vmem = pl.BlockSpec(memory_space=pltpu.VMEM)
    return pl.pallas_call(
        pick_kernel,
        out_shape=(
            jax.ShapeDtypeStruct((WIDTH, SLOTS), bf16),
            jax.ShapeDtypeStruct((8, SLOTS), f32),
        ),
        in_specs=[vmem] * 2,
        out_specs=(vmem,) * 2,
        compiler_params=params(16),
        name="pick",
    )(kept, resid)


def norm_kernel(kept_ref, picked_ref, gain_ref, s0, s1, s2, s3, out_ref):
    squares = (s0[:1, :] + s2[:1, :]) + (s1[:1, :] + s3[:1, :])
    scale = lax.rsqrt(squares / 8192 + epsilon)
    row = lax.broadcasted_iota(jnp.int32, (32, 1), 0)
    mark = jnp.where(row == 0, jnp.where(live_slots(kept_ref), 0.0, jnp.inf), 0.0).astype(bf16)
    for x in range(4):
        for c in range(2):
            first = (x * 2 + c) * 256
            rows = picked_ref[first : first + 256, :].astype(f32)
            short = (rows * scale * gain_ref[first : first + 256, :]).astype(bf16)
            for z in range(4):
                low, high = z * PIECE, (z ^ 2) * PIECE + 32
                out_ref[z * 8 + x * 2 + c, :32, :] = short[low : low + 32, :] + mark
                out_ref[z * 8 + x * 2 + c, 32:, :] = short[high : high + 32, :]


def norm(kept, picked, gain, sums):
    return pl.pallas_call(
        norm_kernel,
        out_shape=jax.ShapeDtypeStruct((32, PIECE, SLOTS), bf16),
        in_specs=[pl.BlockSpec(memory_space=pltpu.VMEM)] * 7,
        out_specs=pl.BlockSpec(memory_space=pltpu.VMEM),
        compiler_params=params(10),
        name="norm",
    )(kept, picked, gain, *sums)


def pack_kernel(first_ref, in_ref, *refs):
    out_refs, acc_ref = refs[:-1], refs[-1]
    acc_ref[...] = jnp.zeros_like(acc_ref)
    group = 4

    def body(g, _):
        moved = []
        for k in range(group):
            t = g * group + k
            rows = in_ref[t].astype(f32)
            rows = jnp.where(rows < jnp.inf, rows, 0.0)
            first = first_ref[t]
            base = pl.multiple_of((first // 128) * 128, 128)
            wide = jnp.concatenate([rows, jnp.zeros((PIECE, 128), f32)], axis=1)
            moved.append((base, pltpu.roll(wide, first - base, 1)))
        for base, rows in moved:
            acc_ref[:, pl.ds(base, SLOTS + 128)] += rows
        return 0

    lax.fori_loop(0, 32 // group, body, 0)
    for k, ref in enumerate(out_refs[2:]):
        rows = acc_ref[k * 16 : (k + 1) * 16, :LIVE]
        lane = lax.broadcasted_iota(jnp.int32, (16, 128), 1)
        sums = spread(jnp.sum(rows, axis=1, keepdims=True), lane)
        for into in (ref, out_refs[k // 2].at[pl.ds(k % 2 * 16, 16)]):
            into[:, :LIVE] = rows.astype(bf16)
            into[:, LIVE:] = sums.astype(bf16)


def pack(first, pieces):
    vmem = pl.BlockSpec(memory_space=pltpu.VMEM)
    return pl.pallas_call(
        pack_kernel,
        out_shape=(jax.ShapeDtypeStruct((32, LONG), bf16),) * 2
        + (jax.ShapeDtypeStruct((16, LONG), bf16),) * 4,
        in_specs=[pl.BlockSpec(memory_space=pltpu.SMEM), vmem],
        out_specs=(vmem,) * 6,
        scratch_shapes=[pltpu.VMEM((PIECE, LIVE + SLOTS + 128), f32)],
        compiler_params=params(10),
        name="pack",
    )(first, pieces)


def behind_kernel(in_ref, *refs):
    refs[-1][...] = in_ref[...]


def behind(value, after):
    vmem = pl.BlockSpec(memory_space=pltpu.VMEM)
    return pl.pallas_call(
        behind_kernel,
        out_shape=jax.ShapeDtypeStruct(value.shape, value.dtype),
        in_specs=[vmem] * (1 + len(after)),
        out_specs=vmem,
        compiler_params=params(4),
        name="behind",
    )(value, *after)


def gram_kernel(blocks, rows_ref, *refs):
    streams, (own_ref, given_ref, cols_ref) = refs[:4], refs[4:]
    lane = lax.broadcasted_iota(jnp.int32, (16, 128), 1)
    terms = jnp.where(lane < 3, 1.0, 0.0).astype(bf16)
    for n, x in enumerate(blocks):
        for z in range(4):
            for s in range(4):
                at = (z if s < 2 else z ^ 2) * PIECE + s * 16
                first = slot_of(s, x, z) * 16
                cols_ref[n * 256 + at : n * 256 + at + 16, :] = streams[s][first : first + 16, :]
        inside = slice(n * 256, (n + 1) * 256)
        product = lax.dot_general(
            rows_ref[:, :LIVE],
            cols_ref[inside, :LIVE],
            (((1,), (1,)), ((), ())),
            preferred_element_type=f32,
        )
        own_ref[:256, inside] = product[:256]
        given_ref[:256, inside] = product[256:]
        sums = lax.dot_general(
            terms, cols_ref[inside, LIVE:], (((1,), (1,)), ((), ())), preferred_element_type=f32
        )
        own_ref[256:, inside] = sums[:8]
        given_ref[256:, inside] = sums[:8]


def gram(blocks, rows, streams):
    vmem = pl.BlockSpec(memory_space=pltpu.VMEM)
    width = 256 * len(blocks)
    return pl.pallas_call(
        lambda *refs: gram_kernel(blocks, *refs),
        out_shape=(jax.ShapeDtypeStruct((264, width), f32),) * 2,
        in_specs=[vmem] * 5,
        out_specs=(vmem,) * 2,
        scratch_shapes=[pltpu.VMEM((width, LONG), bf16)],
        compiler_params=params(10),
        cost_estimate=pl.CostEstimate(
            flops=2 * 512 * width * LIVE, bytes_accessed=6 * 1024 * 1024, transcendentals=0
        ),
        name="gram",
    )(rows, *streams)


def finish_kernel(info_ref, part_ref, *refs):
    own, got, (mean_ref, out_ref) = refs[:2], refs[2:4], refs[4:]
    core, row_first, col_first = info_ref[0], info_ref[1], info_ref[2]
    part = part_ref[0]
    row = row_first + lax.broadcasted_iota(jnp.int32, (256, 256), 0)
    col = col_first + lax.broadcasted_iota(jnp.int32, (256, 256), 1)
    for x in range(4):
        inside = slice(x % 2 * 256, (x % 2 + 1) * 256)
        for ref, which in ((own[x // 2], core), (got[x // 2], 1 - core)):
            at = pl.multiple_of(x * 512 + which * 256, 256)
            out_ref[:, pl.ds(at, 256)] = jnp.where(row <= col + at, ref[:256, inside] * part, 0.0)
            mean_ref[:, pl.ds(at, 256)] = ref[256:264, inside][:1] * part


def finish(info, part, own, got):
    vmem = pl.BlockSpec(memory_space=pltpu.VMEM)
    return pl.pallas_call(
        finish_kernel,
        out_shape=(
            jax.ShapeDtypeStruct((1, WIDTH), f32),
            jax.ShapeDtypeStruct((256, WIDTH), f32),
        ),
        in_specs=[pl.BlockSpec(memory_space=pltpu.SMEM)] * 2 + [vmem] * 4,
        out_specs=(vmem,) * 2,
        compiler_params=params(10),
        name="finish",
    )(info, part, *own, *got)


def swap(value):
    return lax.ppermute(value, "c", [(0, 1), (1, 0)])


def trade(value, axis, flip):
    return lax.ppermute(value, axis, [(i, i ^ flip) for i in range(4)])


def join(*values):
    return jnp.concatenate(values, axis=0)


def meet(value, axis, flip, which):
    got = trade(value, axis, flip)
    return join(jnp.where(which == 0, value, got), jnp.where(which == 0, got, value))


def per_device(resid, norm_gain, keep_index, counts):
    z, x, c, y = (lax.axis_index(a) for a in ("z", "x", "c", "y"))
    kept = jnp.concatenate([keep_index, counts, jnp.zeros((126,), jnp.int32)])[None, :]
    picked, sums = pick(resid, kept)
    all_sums = [sums] + [trade(sums, "y", flip) for flip in (1, 2, 3)]
    pieces = norm(kept, picked, norm_gain[:, None], all_sums)
    pieces = lax.all_to_all(pieces, TOK, 0, 0, tiled=True)

    loads = jnp.sum((pieces[:, 0, :] < jnp.inf).astype(jnp.int32), axis=1)
    first = jnp.cumsum(loads) - loads
    part = 1.0 / jnp.sum(loads).astype(f32)
    *halves, s0, s1, s2, s3 = pack(first, pieces)
    streams = [s0, s1, s2, s3]

    def send(half, turn):
        places = [(q, u) for q in range(4) for u in range(4)]
        return lax.ppermute(half, ("z", "y"), [(q * 4 + u, u * 4 + (q ^ u ^ turn)) for q, u in places])

    for step in range(4):
        for s in range(4):
            axis, flip = PARTNERS[(s + step) % 4]
            seen = [PARTNERS[(s + k) % 4][0] for k in range(step)]
            which = side(x if axis == "x" else z, flip, axis not in seen)
            streams[s] = meet(streams[s], axis, flip, which)
        marks = [value[:16, :128] for value in streams]
        if step == 0:
            turned = [send(behind(halves[0], marks[:1]), 0), send(behind(halves[1], marks), 2)]
        if step == 1:
            rows = behind(join(*turned), [swap(join(*marks))])

    rows = meet(rows, "y", 1, side(y ^ z, 1, True))
    rows = meet(rows, "y", 3, side(y ^ z, 3, False))
    rows = join(rows, swap(rows))

    own, got = [], []
    for blocks in ((0, 1), (2, 3)):
        kept, given = gram(blocks, rows, streams)
        own.append(kept)
        got.append(swap(given))
    info = jnp.stack([c, (z * 8 + x * 2 + c) * 256, y * WIDTH]).astype(jnp.int32)
    mean, gram_factor = finish(info, part[None], own, got)
    return (mean[0], gram_factor)


def solution(mesh):
    fine = Mesh(mesh.devices.reshape(4, 4, 2, 4), ("z", "x", "c", "y"))
    return jax.shard_map(
        per_device,
        mesh=fine,
        in_specs=(P(TOK, "y"), P("y"), P(TOK), P(TOK)),
        out_specs=(P("y"), P(TOK, "y")),
        check_vma=False,
    )
```

```python
import jax
import jax.numpy as jnp
from jax import lax
from jax.experimental import pallas as pl
from jax.experimental.pallas import tpu as pltpu
from jax.sharding import Mesh, PartitionSpec as P

epsilon = 1e-05
TOK = ("z", "x", "c")
SLOTS = 256
LIVE = 4096
WIDTH = 2048
PIECE = 64
LONG = LIVE + 128
MIB = 1024 * 1024
bf16 = jnp.bfloat16
f32 = jnp.float32


def params(mib):
    return pltpu.CompilerParams(vmem_limit_bytes=mib * MIB)


def spread(value, place):
    high = value.astype(bf16).astype(f32)
    middle = (value - high).astype(bf16).astype(f32)
    low = value - high - middle
    rest = jnp.where(place == 2, low, 0.0)
    return jnp.where(place == 0, high, jnp.where(place == 1, middle, rest))


PARTNERS = (("x", 1), ("z", 1), ("x", 3), ("z", 3))


def side(place, flip, first):
    if flip == 1 and not first:
        return (place ^ (place >> 1)) & 1
    return place & 1 if flip == 1 else place >> 1


def slot_of(s, x, z):
    at, seen = 0, []
    for step in range(4):
        axis, flip = PARTNERS[(s + step) % 4]
        at += side(x if axis == "x" else z, flip, axis not in seen) << step
        seen.append(axis)
    return at


def live_slots(kept_ref):
    slot = lax.broadcasted_iota(jnp.int32, (1, SLOTS), 1)
    half = SLOTS // 2
    counts = kept_ref[:, SLOTS : SLOTS + 128]
    return slot < jnp.where(slot < half, counts[:, 0:1], half + counts[:, 1:2])


def pick_kernel(kept_ref, resid_ref, picked_ref, sums_ref):
    tokens = resid_ref.shape[0]
    token = lax.broadcasted_iota(jnp.int32, (tokens, SLOTS), 0)
    kept = jnp.where(live_slots(kept_ref), kept_ref[:, :SLOTS], -1)
    one_hot = jnp.where(token == kept, 1.0, 0.0).astype(bf16)
    total = jnp.zeros((1, SLOTS), f32)
    step = 512
    for k in range(WIDTH // step):
        part = lax.dot_general(
            resid_ref[:, k * step : (k + 1) * step],
            one_hot,
            (((0,), (0,)), ((), ())),
            preferred_element_type=f32,
        )
        total += jnp.sum(part * part, axis=0, keepdims=True)
        picked_ref[k * step : (k + 1) * step, :] = part.astype(bf16)
    sums_ref[...] = jnp.broadcast_to(total, sums_ref.shape)


def pick(resid, kept):
    vmem = pl.BlockSpec(memory_space=pltpu.VMEM)
    return pl.pallas_call(
        pick_kernel,
        out_shape=(
            jax.ShapeDtypeStruct((WIDTH, SLOTS), bf16),
            jax.ShapeDtypeStruct((8, SLOTS), f32),
        ),
        in_specs=[vmem] * 2,
        out_specs=(vmem,) * 2,
        compiler_params=params(16),
        name="pick",
    )(kept, resid)


def norm_kernel(kept_ref, picked_ref, gain_ref, s0, s1, s2, s3, out_ref):
    squares = (s0[:1, :] + s2[:1, :]) + (s1[:1, :] + s3[:1, :])
    scale = lax.rsqrt(squares / 8192 + epsilon)
    row = lax.broadcasted_iota(jnp.int32, (32, 1), 0)
    mark = jnp.where(row == 0, jnp.where(live_slots(kept_ref), 0.0, jnp.inf), 0.0).astype(bf16)
    for x in range(4):
        for c in range(2):
            first = (x * 2 + c) * 256
            rows = picked_ref[first : first + 256, :].astype(f32)
            short = (rows * scale * gain_ref[first : first + 256, :]).astype(bf16)
            for z in range(4):
                low, high = z * PIECE, (z ^ 2) * PIECE + 32
                out_ref[z * 8 + x * 2 + c, :32, :] = short[low : low + 32, :] + mark
                out_ref[z * 8 + x * 2 + c, 32:, :] = short[high : high + 32, :]


def norm(kept, picked, gain, sums):
    return pl.pallas_call(
        norm_kernel,
        out_shape=jax.ShapeDtypeStruct((32, PIECE, SLOTS), bf16),
        in_specs=[pl.BlockSpec(memory_space=pltpu.VMEM)] * 7,
        out_specs=pl.BlockSpec(memory_space=pltpu.VMEM),
        compiler_params=params(10),
        name="norm",
    )(kept, picked, gain, *sums)


def pack_kernel(first_ref, in_ref, *refs):
    out_refs, acc_ref = refs[:-1], refs[-1]
    acc_ref[...] = jnp.zeros_like(acc_ref)
    group = 4

    def body(g, _):
        moved = []
        for k in range(group):
            t = g * group + k
            rows = in_ref[t].astype(f32)
            rows = jnp.where(rows < jnp.inf, rows, 0.0)
            first = first_ref[t]
            base = pl.multiple_of((first // 128) * 128, 128)
            wide = jnp.concatenate([rows, jnp.zeros((PIECE, 128), f32)], axis=1)
            moved.append((base, pltpu.roll(wide, first - base, 1)))
        for base, rows in moved:
            acc_ref[:, pl.ds(base, SLOTS + 128)] += rows
        return 0

    lax.fori_loop(0, 32 // group, body, 0)
    for k, ref in enumerate(out_refs[2:]):
        rows = acc_ref[k * 16 : (k + 1) * 16, :LIVE]
        lane = lax.broadcasted_iota(jnp.int32, (16, 128), 1)
        sums = spread(jnp.sum(rows, axis=1, keepdims=True), lane)
        for into in (ref, out_refs[k // 2].at[pl.ds(k % 2 * 16, 16)]):
            into[:, :LIVE] = rows.astype(bf16)
            into[:, LIVE:] = sums.astype(bf16)


def pack(first, pieces):
    vmem = pl.BlockSpec(memory_space=pltpu.VMEM)
    return pl.pallas_call(
        pack_kernel,
        out_shape=(jax.ShapeDtypeStruct((32, LONG), bf16),) * 2
        + (jax.ShapeDtypeStruct((16, LONG), bf16),) * 4,
        in_specs=[pl.BlockSpec(memory_space=pltpu.SMEM), vmem],
        out_specs=(vmem,) * 6,
        scratch_shapes=[pltpu.VMEM((PIECE, LIVE + SLOTS + 128), f32)],
        compiler_params=params(10),
        name="pack",
    )(first, pieces)


def behind_kernel(in_ref, *refs):
    refs[-1][...] = in_ref[...]


def behind(value, after):
    vmem = pl.BlockSpec(memory_space=pltpu.VMEM)
    return pl.pallas_call(
        behind_kernel,
        out_shape=jax.ShapeDtypeStruct(value.shape, value.dtype),
        in_specs=[vmem] + [pl.BlockSpec(memory_space=pl.ANY)] * len(after),
        out_specs=vmem,
        compiler_params=params(4),
        name="behind",
    )(value, *after)


def gram_kernel(blocks, rows_ref, *refs):
    streams, (own_ref, given_ref, cols_ref) = refs[:4], refs[4:]
    lane = lax.broadcasted_iota(jnp.int32, (16, 128), 1)
    terms = jnp.where(lane < 3, 1.0, 0.0).astype(bf16)
    for n, x in enumerate(blocks):
        for z in range(4):
            for s in range(4):
                at = (z if s < 2 else z ^ 2) * PIECE + s * 16
                first = slot_of(s, x, z) * 16
                cols_ref[n * 256 + at : n * 256 + at + 16, :] = streams[s][first : first + 16, :]
        inside = slice(n * 256, (n + 1) * 256)
        product = lax.dot_general(
            rows_ref[:, :LIVE],
            cols_ref[inside, :LIVE],
            (((1,), (1,)), ((), ())),
            preferred_element_type=f32,
        )
        own_ref[:256, inside] = product[:256]
        given_ref[:256, inside] = product[256:]
        sums = lax.dot_general(
            terms, cols_ref[inside, LIVE:], (((1,), (1,)), ((), ())), preferred_element_type=f32
        )
        own_ref[256:, inside] = sums[:8]
        given_ref[256:, inside] = sums[:8]


def gram(blocks, rows, streams):
    vmem = pl.BlockSpec(memory_space=pltpu.VMEM)
    width = 256 * len(blocks)
    return pl.pallas_call(
        lambda *refs: gram_kernel(blocks, *refs),
        out_shape=(jax.ShapeDtypeStruct((264, width), f32),) * 2,
        in_specs=[vmem] * 5,
        out_specs=(vmem,) * 2,
        scratch_shapes=[pltpu.VMEM((width, LONG), bf16)],
        compiler_params=params(10),
        cost_estimate=pl.CostEstimate(
            flops=2 * 512 * width * LIVE, bytes_accessed=6 * 1024 * 1024, transcendentals=0
        ),
        name="gram",
    )(rows, *streams)


def finish_kernel(info_ref, part_ref, *refs):
    own, got, (mean_ref, out_ref) = refs[:2], refs[2:4], refs[4:]
    core, row_first, col_first = info_ref[0], info_ref[1], info_ref[2]
    part = part_ref[0]
    row = row_first + lax.broadcasted_iota(jnp.int32, (256, 256), 0)
    col = col_first + lax.broadcasted_iota(jnp.int32, (256, 256), 1)
    for x in range(4):
        inside = slice(x % 2 * 256, (x % 2 + 1) * 256)
        for ref, which in ((own[x // 2], core), (got[x // 2], 1 - core)):
            at = pl.multiple_of(x * 512 + which * 256, 256)
            out_ref[:, pl.ds(at, 256)] = jnp.where(row <= col + at, ref[:256, inside] * part, 0.0)
            mean_ref[:, pl.ds(at, 256)] = ref[256:264, inside][:1] * part


def finish(info, part, own, got):
    vmem = pl.BlockSpec(memory_space=pltpu.VMEM)
    return pl.pallas_call(
        finish_kernel,
        out_shape=(
            jax.ShapeDtypeStruct((1, WIDTH), f32),
            jax.ShapeDtypeStruct((256, WIDTH), f32),
        ),
        in_specs=[pl.BlockSpec(memory_space=pltpu.SMEM)] * 2 + [vmem] * 4,
        out_specs=(vmem,) * 2,
        compiler_params=params(10),
        name="finish",
    )(info, part, *own, *got)


def swap(value):
    return lax.ppermute(value, "c", [(0, 1), (1, 0)])


def trade(value, axis, flip):
    return lax.ppermute(value, axis, [(i, i ^ flip) for i in range(4)])


def join(*values):
    return jnp.concatenate(values, axis=0)


def meet(value, axis, flip, which):
    got = trade(value, axis, flip)
    return join(jnp.where(which == 0, value, got), jnp.where(which == 0, got, value))


def per_device(resid, norm_gain, keep_index, counts):
    z, x, c, y = (lax.axis_index(a) for a in ("z", "x", "c", "y"))
    kept = jnp.concatenate([keep_index, counts, jnp.zeros((126,), jnp.int32)])[None, :]
    picked, sums = pick(resid, kept)
    all_sums = [sums] + [trade(sums, "y", flip) for flip in (1, 2, 3)]
    pieces = norm(kept, picked, norm_gain[:, None], all_sums)
    pieces = lax.all_to_all(pieces, TOK, 0, 0, tiled=True)

    loads = jnp.sum((pieces[:, 0, :] < jnp.inf).astype(jnp.int32), axis=1)
    first = jnp.cumsum(loads) - loads
    part = 1.0 / jnp.sum(loads).astype(f32)
    *halves, s0, s1, s2, s3 = pack(first, pieces)
    streams = [s0, s1, s2, s3]

    def send(half, turn):
        places = [(q, u) for q in range(4) for u in range(4)]
        return lax.ppermute(half, ("z", "y"), [(q * 4 + u, u * 4 + (q ^ u ^ turn)) for q, u in places])

    for step in range(4):
        for s in range(4):
            axis, flip = PARTNERS[(s + step) % 4]
            seen = [PARTNERS[(s + k) % 4][0] for k in range(step)]
            which = side(x if axis == "x" else z, flip, axis not in seen)
            streams[s] = meet(streams[s], axis, flip, which)
        if step == 0:
            turned = [send(behind(halves[0], streams[:1]), 0), send(behind(halves[1], streams), 2)]
        if step == 1:
            rows = behind(join(*turned), streams)

    q = y ^ z
    rows = meet(rows, "y", 1, side(q, 1, True))
    rows = meet(rows, "y", 3, side(q, 3, False))
    rows = join(rows, swap(rows))

    own, got = [], []
    for blocks in ((0, 1), (2, 3)):
        kept, given = gram(blocks, rows, streams)
        own.append(kept)
        got.append(swap(given))
    info = jnp.stack([c, (z * 8 + x * 2 + c) * 256, y * WIDTH]).astype(jnp.int32)
    mean, gram_factor = finish(info, part[None], own, got)
    return (mean[0], gram_factor)


def solution(mesh):
    fine = Mesh(mesh.devices.reshape(4, 4, 2, 4), ("z", "x", "c", "y"))
    return jax.shard_map(
        per_device,
        mesh=fine,
        in_specs=(P(TOK, "y"), P("y"), P(TOK), P(TOK)),
        out_specs=(P("y"), P(TOK, "y")),
        check_vma=False,
    )
```

```python
import jax
import jax.numpy as jnp
from jax import lax
from jax.experimental import pallas as pl
from jax.experimental.pallas import tpu as pltpu
from jax.sharding import Mesh, PartitionSpec as P

epsilon = 1e-05
TOK = ("z", "x", "c")
SLOTS = 256
LIVE = 4096
WIDTH = 2048
PIECE = 64
LONG = LIVE + 128
MIB = 1024 * 1024
bf16 = jnp.bfloat16
f32 = jnp.float32


def params(mib):
    return pltpu.CompilerParams(vmem_limit_bytes=mib * MIB)


def spread(value, place):
    high = value.astype(bf16).astype(f32)
    middle = (value - high).astype(bf16).astype(f32)
    low = value - high - middle
    rest = jnp.where(place == 2, low, 0.0)
    return jnp.where(place == 0, high, jnp.where(place == 1, middle, rest))


PARTNERS = (("x", 1), ("z", 1), ("x", 3), ("z", 3))


def side(place, flip, first):
    if flip == 1 and not first:
        return (place ^ (place >> 1)) & 1
    return place & 1 if flip == 1 else place >> 1


def slot_of(s, x, z):
    at, seen = 0, []
    for step in range(4):
        axis, flip = PARTNERS[(s + step) % 4]
        at += side(x if axis == "x" else z, flip, axis not in seen) << step
        seen.append(axis)
    return at


def live_slots(kept_ref):
    slot = lax.broadcasted_iota(jnp.int32, (1, SLOTS), 1)
    half = SLOTS // 2
    counts = kept_ref[:, SLOTS : SLOTS + 128]
    return slot < jnp.where(slot < half, counts[:, 0:1], half + counts[:, 1:2])


def pick_kernel(kept_ref, resid_ref, picked_ref, sums_ref):
    tokens = resid_ref.shape[0]
    token = lax.broadcasted_iota(jnp.int32, (tokens, SLOTS), 0)
    kept = jnp.where(live_slots(kept_ref), kept_ref[:, :SLOTS], -1)
    one_hot = jnp.where(token == kept, 1.0, 0.0).astype(bf16)
    total = jnp.zeros((1, SLOTS), f32)
    step = 512
    for k in range(WIDTH // step):
        part = lax.dot_general(
            resid_ref[:, k * step : (k + 1) * step],
            one_hot,
            (((0,), (0,)), ((), ())),
            preferred_element_type=f32,
        )
        total += jnp.sum(part * part, axis=0, keepdims=True)
        picked_ref[k * step : (k + 1) * step, :] = part.astype(bf16)
    sums_ref[...] = jnp.broadcast_to(total, sums_ref.shape)


def pick(resid, kept):
    vmem = pl.BlockSpec(memory_space=pltpu.VMEM)
    return pl.pallas_call(
        pick_kernel,
        out_shape=(
            jax.ShapeDtypeStruct((WIDTH, SLOTS), bf16),
            jax.ShapeDtypeStruct((8, SLOTS), f32),
        ),
        in_specs=[vmem] * 2,
        out_specs=(vmem,) * 2,
        compiler_params=params(16),
        name="pick",
    )(kept, resid)


def norm_kernel(kept_ref, picked_ref, gain_ref, s0, s1, s2, s3, out_ref):
    squares = (s0[:1, :] + s2[:1, :]) + (s1[:1, :] + s3[:1, :])
    scale = lax.rsqrt(squares / 8192 + epsilon)
    row = lax.broadcasted_iota(jnp.int32, (32, 1), 0)
    mark = jnp.where(row == 0, jnp.where(live_slots(kept_ref), 0.0, jnp.inf), 0.0).astype(bf16)
    for x in range(4):
        for c in range(2):
            first = (x * 2 + c) * 256
            rows = picked_ref[first : first + 256, :].astype(f32)
            short = (rows * scale * gain_ref[first : first + 256, :]).astype(bf16)
            for z in range(4):
                low, high = z * PIECE, (z ^ 2) * PIECE + 32
                out_ref[z * 8 + x * 2 + c, :32, :] = short[low : low + 32, :] + mark
                out_ref[z * 8 + x * 2 + c, 32:, :] = short[high : high + 32, :]


def norm(kept, picked, gain, sums):
    return pl.pallas_call(
        norm_kernel,
        out_shape=jax.ShapeDtypeStruct((32, PIECE, SLOTS), bf16),
        in_specs=[pl.BlockSpec(memory_space=pltpu.VMEM)] * 7,
        out_specs=pl.BlockSpec(memory_space=pltpu.VMEM),
        compiler_params=params(10),
        name="norm",
    )(kept, picked, gain, *sums)


def pack_kernel(first_ref, in_ref, *refs):
    out_refs, acc_ref = refs[:-1], refs[-1]
    acc_ref[...] = jnp.zeros_like(acc_ref)
    group = 4

    def body(g, _):
        moved = []
        for k in range(group):
            t = g * group + k
            rows = in_ref[t].astype(f32)
            rows = jnp.where(rows < jnp.inf, rows, 0.0)
            first = first_ref[t]
            base = pl.multiple_of((first // 128) * 128, 128)
            wide = jnp.concatenate([rows, jnp.zeros((PIECE, 128), f32)], axis=1)
            moved.append((base, pltpu.roll(wide, first - base, 1)))
        for base, rows in moved:
            acc_ref[:, pl.ds(base, SLOTS + 128)] += rows
        return 0

    lax.fori_loop(0, 32 // group, body, 0)
    for k, ref in enumerate(out_refs[2:]):
        rows = acc_ref[k * 16 : (k + 1) * 16, :LIVE]
        lane = lax.broadcasted_iota(jnp.int32, (16, 128), 1)
        sums = spread(jnp.sum(rows, axis=1, keepdims=True), lane)
        for into in (ref, out_refs[k // 2].at[pl.ds(k % 2 * 16, 16)]):
            into[:, :LIVE] = rows.astype(bf16)
            into[:, LIVE:] = sums.astype(bf16)


def pack(first, pieces):
    vmem = pl.BlockSpec(memory_space=pltpu.VMEM)
    return pl.pallas_call(
        pack_kernel,
        out_shape=(jax.ShapeDtypeStruct((32, LONG), bf16),) * 2
        + (jax.ShapeDtypeStruct((16, LONG), bf16),) * 4,
        in_specs=[pl.BlockSpec(memory_space=pltpu.SMEM), vmem],
        out_specs=(vmem,) * 6,
        scratch_shapes=[pltpu.VMEM((PIECE, LIVE + SLOTS + 128), f32)],
        compiler_params=params(10),
        name="pack",
    )(first, pieces)


def behind_kernel(in_ref, *refs):
    refs[-1][...] = in_ref[...]


def behind(value, after):
    vmem = pl.BlockSpec(memory_space=pltpu.VMEM)
    return pl.pallas_call(
        behind_kernel,
        out_shape=jax.ShapeDtypeStruct(value.shape, value.dtype),
        in_specs=[vmem] + [pl.BlockSpec(memory_space=pl.ANY)] * len(after),
        out_specs=vmem,
        compiler_params=params(4),
        name="behind",
    )(value, *after)


def gram_kernel(blocks, rows_ref, *refs):
    streams, (own_ref, given_ref, cols_ref) = refs[:4], refs[4:]
    lane = lax.broadcasted_iota(jnp.int32, (16, 128), 1)
    terms = jnp.where(lane < 3, 1.0, 0.0).astype(bf16)
    for n, x in enumerate(blocks):
        for z in range(4):
            for s in range(4):
                at = (z if s < 2 else z ^ 2) * PIECE + s * 16
                first = slot_of(s, x, z) * 16
                cols_ref[n * 256 + at : n * 256 + at + 16, :] = streams[s][first : first + 16, :]
        inside = slice(n * 256, (n + 1) * 256)
        product = lax.dot_general(
            rows_ref[:, :LIVE],
            cols_ref[inside, :LIVE],
            (((1,), (1,)), ((), ())),
            preferred_element_type=f32,
        )
        own_ref[:256, inside] = product[:256]
        given_ref[:256, inside] = product[256:]
        sums = lax.dot_general(
            terms, cols_ref[inside, LIVE:], (((1,), (1,)), ((), ())), preferred_element_type=f32
        )
        own_ref[256:, inside] = sums[:8]
        given_ref[256:, inside] = sums[:8]


def gram(blocks, rows, streams):
    vmem = pl.BlockSpec(memory_space=pltpu.VMEM)
    width = 256 * len(blocks)
    return pl.pallas_call(
        lambda *refs: gram_kernel(blocks, *refs),
        out_shape=(jax.ShapeDtypeStruct((264, width), f32),) * 2,
        in_specs=[vmem] * 5,
        out_specs=(vmem,) * 2,
        scratch_shapes=[pltpu.VMEM((width, LONG), bf16)],
        compiler_params=params(10),
        cost_estimate=pl.CostEstimate(
            flops=2 * 512 * width * LIVE, bytes_accessed=6 * 1024 * 1024, transcendentals=0
        ),
        name="gram",
    )(rows, *streams)


def finish_kernel(info_ref, part_ref, *refs):
    own, got, (mean_ref, out_ref) = refs[:2], refs[2:4], refs[4:]
    core, row_block, col_block = info_ref[0], info_ref[1], info_ref[2]
    part = part_ref[0]

    def put(ref, inside, block):
        at = pl.multiple_of(block * 256, 256)
        mean_ref[:, pl.ds(at, 256)] = ref[256:264, inside][:1] * part

        @pl.when(col_block + block > row_block)
        def _():
            out_ref[:, pl.ds(at, 256)] = ref[:256, inside] * part

        @pl.when(col_block + block == row_block)
        def _():
            row = lax.broadcasted_iota(jnp.int32, (256, 256), 0)
            col = lax.broadcasted_iota(jnp.int32, (256, 256), 1)
            out_ref[:, pl.ds(at, 256)] = jnp.where(row <= col, ref[:256, inside] * part, 0.0)

        @pl.when(col_block + block < row_block)
        def _():
            out_ref[:, pl.ds(at, 256)] = jnp.zeros((256, 256), f32)

    for x in range(4):
        inside = slice(x % 2 * 256, (x % 2 + 1) * 256)
        put(own[x // 2], inside, x * 2 + core)
        put(got[x // 2], inside, x * 2 + 1 - core)


def finish(info, part, own, got):
    vmem = pl.BlockSpec(memory_space=pltpu.VMEM)
    return pl.pallas_call(
        finish_kernel,
        out_shape=(
            jax.ShapeDtypeStruct((1, WIDTH), f32),
            jax.ShapeDtypeStruct((256, WIDTH), f32),
        ),
        in_specs=[pl.BlockSpec(memory_space=pltpu.SMEM)] * 2 + [vmem] * 4,
        out_specs=(vmem,) * 2,
        compiler_params=params(10),
        name="finish",
    )(info, part, *own, *got)


def swap(value):
    return lax.ppermute(value, "c", [(0, 1), (1, 0)])


def trade(value, axis, flip):
    return lax.ppermute(value, axis, [(i, i ^ flip) for i in range(4)])


def join(*values):
    return jnp.concatenate(values, axis=0)


def meet(value, axis, flip, which):
    got = trade(value, axis, flip)
    return join(jnp.where(which == 0, value, got), jnp.where(which == 0, got, value))


def per_device(resid, norm_gain, keep_index, counts):
    z, x, c, y = (lax.axis_index(a) for a in ("z", "x", "c", "y"))
    kept = jnp.concatenate([keep_index, counts, jnp.zeros((126,), jnp.int32)])[None, :]
    picked, sums = pick(resid, kept)
    all_sums = [sums] + [trade(sums, "y", flip) for flip in (1, 2, 3)]
    pieces = norm(kept, picked, norm_gain[:, None], all_sums)
    pieces = lax.all_to_all(pieces, TOK, 0, 0, tiled=True)

    loads = jnp.sum((pieces[:, 0, :] < jnp.inf).astype(jnp.int32), axis=1)
    first = jnp.cumsum(loads) - loads
    part = 1.0 / jnp.sum(loads).astype(f32)
    *halves, s0, s1, s2, s3 = pack(first, pieces)
    streams = [s0, s1, s2, s3]

    def send(half, turn):
        places = [(q, u) for q in range(4) for u in range(4)]
        return lax.ppermute(half, ("z", "y"), [(q * 4 + u, u * 4 + (q ^ u ^ turn)) for q, u in places])

    for step in range(4):
        for s in range(4):
            axis, flip = PARTNERS[(s + step) % 4]
            seen = [PARTNERS[(s + k) % 4][0] for k in range(step)]
            which = side(x if axis == "x" else z, flip, axis not in seen)
            streams[s] = meet(streams[s], axis, flip, which)
        if step == 0:
            low_t = send(behind(halves[0], streams[:1]), 0)
        if step == 0:
            high_t = send(behind(halves[1], streams), 2)
        if step == 1:
            rows = meet(behind(join(low_t, high_t), streams), "y", 1, side(y ^ z, 1, True))
        if step == 2:
            rows = meet(behind(rows, streams[:1]), "y", 3, side(y ^ z, 3, False))

    rows = join(rows, swap(rows))

    own, got = [], []
    for blocks in ((0, 1), (2, 3)):
        kept, given = gram(blocks, rows, streams)
        own.append(kept)
        got.append(swap(given))
    info = jnp.stack([c, z * 8 + x * 2 + c, y * 8]).astype(jnp.int32)
    mean, gram_factor = finish(info, part[None], own, got)
    return (mean[0], gram_factor)


def solution(mesh):
    fine = Mesh(mesh.devices.reshape(4, 4, 2, 4), ("z", "x", "c", "y"))
    return jax.shard_map(
        per_device,
        mesh=fine,
        in_specs=(P(TOK, "y"), P("y"), P(TOK), P(TOK)),
        out_specs=(P("y"), P(TOK, "y")),
        check_vma=False,
    )
```

```python
import jax
import jax.numpy as jnp
from jax import lax
from jax.experimental import pallas as pl
from jax.experimental.pallas import tpu as pltpu
from jax.sharding import Mesh, PartitionSpec as P

epsilon = 1e-05
TOK = ("z", "x", "c")
SLOTS = 256
LIVE = 4096
WIDTH = 2048
PIECE = 64
LONG = LIVE + 128
MIB = 1024 * 1024
bf16 = jnp.bfloat16
f32 = jnp.float32


def params(mib):
    return pltpu.CompilerParams(vmem_limit_bytes=mib * MIB)


def spread(value, place):
    high = value.astype(bf16).astype(f32)
    middle = (value - high).astype(bf16).astype(f32)
    low = value - high - middle
    rest = jnp.where(place == 2, low, 0.0)
    return jnp.where(place == 0, high, jnp.where(place == 1, middle, rest))


PARTNERS = (("x", 1), ("z", 1), ("x", 3), ("z", 3))


def side(place, flip, first):
    if flip == 1 and not first:
        return (place ^ (place >> 1)) & 1
    return place & 1 if flip == 1 else place >> 1


def slot_of(s, x, z):
    at, seen = 0, []
    for step in range(4):
        axis, flip = PARTNERS[(s + step) % 4]
        at += side(x if axis == "x" else z, flip, axis not in seen) << step
        seen.append(axis)
    return at


def live_slots(kept_ref):
    slot = lax.broadcasted_iota(jnp.int32, (1, SLOTS), 1)
    half = SLOTS // 2
    counts = kept_ref[:, SLOTS : SLOTS + 128]
    return slot < jnp.where(slot < half, counts[:, 0:1], half + counts[:, 1:2])


def pick_kernel(kept_ref, resid_ref, picked_ref, sums_ref):
    tokens = resid_ref.shape[0]
    token = lax.broadcasted_iota(jnp.int32, (tokens, SLOTS), 0)
    kept = jnp.where(live_slots(kept_ref), kept_ref[:, :SLOTS], -1)
    one_hot = jnp.where(token == kept, 1.0, 0.0).astype(bf16)
    total = jnp.zeros((1, SLOTS), f32)
    step = 512
    for k in range(WIDTH // step):
        part = lax.dot_general(
            resid_ref[:, k * step : (k + 1) * step],
            one_hot,
            (((0,), (0,)), ((), ())),
            preferred_element_type=f32,
        )
        total += jnp.sum(part * part, axis=0, keepdims=True)
        picked_ref[k * step : (k + 1) * step, :] = part.astype(bf16)
    sums_ref[...] = jnp.broadcast_to(total, sums_ref.shape)


def pick(resid, kept):
    vmem = pl.BlockSpec(memory_space=pltpu.VMEM)
    return pl.pallas_call(
        pick_kernel,
        out_shape=(
            jax.ShapeDtypeStruct((WIDTH, SLOTS), bf16),
            jax.ShapeDtypeStruct((8, SLOTS), f32),
        ),
        in_specs=[vmem] * 2,
        out_specs=(vmem,) * 2,
        compiler_params=params(16),
        name="pick",
    )(kept, resid)


def norm_kernel(kept_ref, picked_ref, gain_ref, s0, s1, s2, s3, out_ref):
    squares = (s0[:1, :] + s2[:1, :]) + (s1[:1, :] + s3[:1, :])
    scale = lax.rsqrt(squares / 8192 + epsilon)
    row = lax.broadcasted_iota(jnp.int32, (32, 1), 0)
    mark = jnp.where(row == 0, jnp.where(live_slots(kept_ref), 0.0, jnp.inf), 0.0).astype(bf16)
    for x in range(4):
        for c in range(2):
            first = (x * 2 + c) * 256
            rows = picked_ref[first : first + 256, :].astype(f32)
            short = (rows * scale * gain_ref[first : first + 256, :]).astype(bf16)
            for z in range(4):
                low, high = z * PIECE, (z ^ 2) * PIECE + 32
                out_ref[z * 8 + x * 2 + c, :32, :] = short[low : low + 32, :] + mark
                out_ref[z * 8 + x * 2 + c, 32:, :] = short[high : high + 32, :]


def norm(kept, picked, gain, sums):
    return pl.pallas_call(
        norm_kernel,
        out_shape=jax.ShapeDtypeStruct((32, PIECE, SLOTS), bf16),
        in_specs=[pl.BlockSpec(memory_space=pltpu.VMEM)] * 7,
        out_specs=pl.BlockSpec(memory_space=pltpu.VMEM),
        compiler_params=params(10),
        name="norm",
    )(kept, picked, gain, *sums)


def pack_kernel(first_ref, in_ref, *refs):
    out_refs, acc_ref = refs[:-1], refs[-1]
    acc_ref[...] = jnp.zeros_like(acc_ref)
    group = 4

    def body(g, _):
        moved = []
        for k in range(group):
            t = g * group + k
            rows = in_ref[t].astype(f32)
            rows = jnp.where(rows < jnp.inf, rows, 0.0)
            first = first_ref[t]
            base = pl.multiple_of((first // 128) * 128, 128)
            wide = jnp.concatenate([rows, jnp.zeros((PIECE, 128), f32)], axis=1)
            moved.append((base, pltpu.roll(wide, first - base, 1)))
        for base, rows in moved:
            acc_ref[:, pl.ds(base, SLOTS + 128)] += rows
        return 0

    lax.fori_loop(0, 32 // group, body, 0)
    for k, ref in enumerate(out_refs[2:]):
        rows = acc_ref[k * 16 : (k + 1) * 16, :LIVE]
        lane = lax.broadcasted_iota(jnp.int32, (16, 128), 1)
        sums = spread(jnp.sum(rows, axis=1, keepdims=True), lane)
        for into in (ref, out_refs[k // 2].at[pl.ds(k % 2 * 16, 16)]):
            into[:, :LIVE] = rows.astype(bf16)
            into[:, LIVE:] = sums.astype(bf16)


def pack(first, pieces):
    vmem = pl.BlockSpec(memory_space=pltpu.VMEM)
    return pl.pallas_call(
        pack_kernel,
        out_shape=(jax.ShapeDtypeStruct((32, LONG), bf16),) * 2
        + (jax.ShapeDtypeStruct((16, LONG), bf16),) * 4,
        in_specs=[pl.BlockSpec(memory_space=pltpu.SMEM), vmem],
        out_specs=(vmem,) * 6,
        scratch_shapes=[pltpu.VMEM((PIECE, LIVE + SLOTS + 128), f32)],
        compiler_params=params(10),
        name="pack",
    )(first, pieces)


def behind_kernel(in_ref, *refs):
    refs[-1][...] = in_ref[...]


def behind(value, after):
    vmem = pl.BlockSpec(memory_space=pltpu.VMEM)
    return pl.pallas_call(
        behind_kernel,
        out_shape=jax.ShapeDtypeStruct(value.shape, value.dtype),
        in_specs=[vmem] + [pl.BlockSpec(memory_space=pl.ANY)] * len(after),
        out_specs=vmem,
        compiler_params=params(4),
        name="behind",
    )(value, *after)


def gram_kernel(rows_ref, *refs):
    streams, (out_ref, cols_ref) = refs[:4], refs[4:]
    lane = lax.broadcasted_iota(jnp.int32, (16, 128), 1)
    terms = jnp.where(lane < 3, 1.0, 0.0).astype(bf16)
    for x in range(4):
        for z in range(4):
            for s in range(4):
                at = x * 256 + (z if s < 2 else z ^ 2) * PIECE + s * 16
                first = slot_of(s, x, z) * 16
                cols_ref[at : at + 16, :] = streams[s][first : first + 16, :]
        inside = slice(x * 256, (x + 1) * 256)
        out_ref[:256, inside] = lax.dot_general(
            rows_ref[:, :LIVE],
            cols_ref[inside, :LIVE],
            (((1,), (1,)), ((), ())),
            preferred_element_type=f32,
        )
        out_ref[256:, inside] = lax.dot_general(
            terms, cols_ref[inside, LIVE:], (((1,), (1,)), ((), ())), preferred_element_type=f32
        )[:8]


def gram(rows, streams):
    vmem = pl.BlockSpec(memory_space=pltpu.VMEM)
    return pl.pallas_call(
        gram_kernel,
        out_shape=jax.ShapeDtypeStruct((264, 1024), f32),
        in_specs=[vmem] * 5,
        out_specs=vmem,
        scratch_shapes=[pltpu.VMEM((1024, LONG), bf16)],
        compiler_params=params(14),
        cost_estimate=pl.CostEstimate(
            flops=2 * 256 * 1024 * LIVE, bytes_accessed=10 * 1024 * 1024, transcendentals=0
        ),
        name="gram",
    )(rows, *streams)


def put_blocks(info_ref, part_ref, core, ref, out_hbm, buffer, sem):
    row_block, col_block = info_ref[1], info_ref[2]
    part = part_ref[0]
    copies = []
    for x in range(4):
        inside = slice(x * 256, (x + 1) * 256)
        block = x * 2 + core

        @pl.when(col_block + block > row_block)
        def _():
            buffer[x] = ref[:256, inside] * part

        @pl.when(col_block + block == row_block)
        def _():
            row = lax.broadcasted_iota(jnp.int32, (256, 256), 0)
            col = lax.broadcasted_iota(jnp.int32, (256, 256), 1)
            buffer[x] = jnp.where(row <= col, ref[:256, inside] * part, 0.0)

        @pl.when(col_block + block < row_block)
        def _():
            buffer[x] = jnp.zeros((256, 256), f32)

        target = out_hbm.at[:, pl.ds(pl.multiple_of(block * 256, 256), 256)]
        copies.append(pltpu.make_async_copy(buffer.at[x], target, sem.at[x]))
        copies[-1].start()
    for copy in copies:
        copy.wait()


def own_kernel(info_ref, part_ref, own_ref, out_hbm, buffer, sem):
    put_blocks(info_ref, part_ref, info_ref[0], own_ref, out_hbm, buffer, sem)


def rest_kernel(info_ref, part_ref, own_ref, got_ref, in_hbm, mean_ref, out_hbm, buffer, sem):
    core = info_ref[0]
    for x in range(4):
        inside = slice(x * 256, (x + 1) * 256)
        for ref, which in ((own_ref, core), (got_ref, 1 - core)):
            at = pl.multiple_of(x * 512 + which * 256, 256)
            mean_ref[:, pl.ds(at, 256)] = ref[256:264, inside][:1] * part_ref[0]
    put_blocks(info_ref, part_ref, 1 - core, got_ref, out_hbm, buffer, sem)


def finish(info, part, own, got):
    vmem = pl.BlockSpec(memory_space=pltpu.VMEM)
    smem = pl.BlockSpec(memory_space=pltpu.SMEM)
    hbm = pl.BlockSpec(memory_space=pl.ANY)
    shape = jax.ShapeDtypeStruct((256, WIDTH), f32)
    scratch = [pltpu.VMEM((4, 256, 256), f32), pltpu.SemaphoreType.DMA((4,))]
    half = pl.pallas_call(
        own_kernel,
        out_shape=shape,
        in_specs=[smem, smem, vmem],
        out_specs=hbm,
        scratch_shapes=scratch,
        compiler_params=params(6),
        name="own_blocks",
    )(info, part, own)
    return pl.pallas_call(
        rest_kernel,
        out_shape=(jax.ShapeDtypeStruct((1, WIDTH), f32), shape),
        in_specs=[smem, smem, vmem, vmem, hbm],
        out_specs=(vmem, hbm),
        scratch_shapes=scratch,
        input_output_aliases={4: 1},
        compiler_params=params(6),
        name="other_blocks",
    )(info, part, own, got, half)


def swap(value):
    return lax.ppermute(value, "c", [(0, 1), (1, 0)])


def trade(value, axis, flip):
    return lax.ppermute(value, axis, [(i, i ^ flip) for i in range(4)])


def join(*values):
    return jnp.concatenate(values, axis=0)


def meet(value, axis, flip, which):
    got = trade(value, axis, flip)
    return join(jnp.where(which == 0, value, got), jnp.where(which == 0, got, value))


def per_device(resid, norm_gain, keep_index, counts):
    z, x, c, y = (lax.axis_index(a) for a in ("z", "x", "c", "y"))
    kept = jnp.concatenate([keep_index, counts, jnp.zeros((126,), jnp.int32)])[None, :]
    picked, sums = pick(resid, kept)
    all_sums = [sums] + [trade(sums, "y", flip) for flip in (1, 2, 3)]
    pieces = norm(kept, picked, norm_gain[:, None], all_sums)
    pieces = lax.all_to_all(pieces, TOK, 0, 0, tiled=True)

    loads = jnp.sum((pieces[:, 0, :] < jnp.inf).astype(jnp.int32), axis=1)
    first = jnp.cumsum(loads) - loads
    part = 1.0 / jnp.sum(loads).astype(f32)
    *halves, s0, s1, s2, s3 = pack(first, pieces)
    streams = [s0, s1, s2, s3]

    def send(half, turn):
        places = [(q, u) for q in range(4) for u in range(4)]
        return lax.ppermute(half, ("z", "y"), [(q * 4 + u, u * 4 + (q ^ u ^ turn)) for q, u in places])

    for step in range(4):
        for s in range(4):
            axis, flip = PARTNERS[(s + step) % 4]
            seen = [PARTNERS[(s + k) % 4][0] for k in range(step)]
            which = side(x if axis == "x" else z, flip, axis not in seen)
            streams[s] = meet(streams[s], axis, flip, which)
        if step == 0:
            low_t = send(behind(halves[0], streams[:1]), 0)
        if step == 0:
            high_t = send(behind(halves[1], streams), 2)
        if step == 1:
            rows = meet(behind(join(low_t, high_t), streams), "y", 1, side(y ^ z, 1, True))
        if step == 2:
            rows = meet(behind(rows, streams[:1]), "y", 3, side(y ^ z, 3, False))

    got = swap(gram(swap(rows), streams))
    own = gram(rows, streams)
    info = jnp.stack([c, z * 8 + x * 2 + c, y * 8]).astype(jnp.int32)
    mean, gram_factor = finish(info, part[None], own, got)
    return (mean[0], gram_factor)


def solution(mesh):
    fine = Mesh(mesh.devices.reshape(4, 4, 2, 4), ("z", "x", "c", "y"))
    return jax.shard_map(
        per_device,
        mesh=fine,
        in_specs=(P(TOK, "y"), P("y"), P(TOK), P(TOK)),
        out_specs=(P("y"), P(TOK, "y")),
        check_vma=False,
    )
```

```python
import jax
import jax.numpy as jnp
from jax import lax
from jax.experimental import pallas as pl
from jax.experimental.pallas import tpu as pltpu
from jax.sharding import Mesh, PartitionSpec as P

epsilon = 1e-05
TOK = ("z", "x", "c")
SLOTS = 256
LIVE = 4096
WIDTH = 2048
PIECE = 64
LONG = LIVE + 128
MIB = 1024 * 1024
bf16 = jnp.bfloat16
f32 = jnp.float32


def params(mib):
    return pltpu.CompilerParams(vmem_limit_bytes=mib * MIB)


def spread(value, place):
    high = value.astype(bf16).astype(f32)
    middle = (value - high).astype(bf16).astype(f32)
    low = value - high - middle
    rest = jnp.where(place == 2, low, 0.0)
    return jnp.where(place == 0, high, jnp.where(place == 1, middle, rest))


PARTNERS = (("x", 1), ("z", 1), ("x", 3), ("z", 3))


def side(place, flip, first):
    if flip == 1 and not first:
        return (place ^ (place >> 1)) & 1
    return place & 1 if flip == 1 else place >> 1


def slot_of(s, x, z):
    at, seen = 0, []
    for step in range(4):
        axis, flip = PARTNERS[(s + step) % 4]
        at += side(x if axis == "x" else z, flip, axis not in seen) << step
        seen.append(axis)
    return at


def live_slots(kept_ref):
    slot = lax.broadcasted_iota(jnp.int32, (1, SLOTS), 1)
    half = SLOTS // 2
    counts = kept_ref[:, SLOTS : SLOTS + 128]
    return slot < jnp.where(slot < half, counts[:, 0:1], half + counts[:, 1:2])


def pick_kernel(kept_ref, resid_ref, picked_ref, sums_ref):
    tokens = resid_ref.shape[0]
    token = lax.broadcasted_iota(jnp.int32, (tokens, SLOTS), 0)
    kept = jnp.where(live_slots(kept_ref), kept_ref[:, :SLOTS], -1)
    one_hot = jnp.where(token == kept, 1.0, 0.0).astype(bf16)
    total = jnp.zeros((1, SLOTS), f32)
    step = 512
    for k in range(WIDTH // step):
        part = lax.dot_general(
            resid_ref[:, k * step : (k + 1) * step],
            one_hot,
            (((0,), (0,)), ((), ())),
            preferred_element_type=f32,
        )
        total += jnp.sum(part * part, axis=0, keepdims=True)
        picked_ref[k * step : (k + 1) * step, :] = part.astype(bf16)
    sums_ref[...] = jnp.broadcast_to(total, sums_ref.shape)


def pick(resid, kept):
    vmem = pl.BlockSpec(memory_space=pltpu.VMEM)
    return pl.pallas_call(
        pick_kernel,
        out_shape=(
            jax.ShapeDtypeStruct((WIDTH, SLOTS), bf16),
            jax.ShapeDtypeStruct((8, SLOTS), f32),
        ),
        in_specs=[vmem] * 2,
        out_specs=(vmem,) * 2,
        compiler_params=params(16),
        name="pick",
    )(kept, resid)


def norm_kernel(kept_ref, picked_ref, gain_ref, s0, s1, s2, s3, out_ref):
    squares = (s0[:1, :] + s2[:1, :]) + (s1[:1, :] + s3[:1, :])
    scale = lax.rsqrt(squares / 8192 + epsilon)
    row = lax.broadcasted_iota(jnp.int32, (32, 1), 0)
    mark = jnp.where(row == 0, jnp.where(live_slots(kept_ref), 0.0, jnp.inf), 0.0).astype(bf16)
    for x in range(4):
        for c in range(2):
            first = (x * 2 + c) * 256
            rows = picked_ref[first : first + 256, :].astype(f32)
            short = (rows * scale * gain_ref[first : first + 256, :]).astype(bf16)
            for z in range(4):
                low, high = z * PIECE, (z ^ 2) * PIECE + 32
                out_ref[z * 8 + x * 2 + c, :32, :] = short[low : low + 32, :] + mark
                out_ref[z * 8 + x * 2 + c, 32:, :] = short[high : high + 32, :]


def norm(kept, picked, gain, sums):
    return pl.pallas_call(
        norm_kernel,
        out_shape=jax.ShapeDtypeStruct((32, PIECE, SLOTS), bf16),
        in_specs=[pl.BlockSpec(memory_space=pltpu.VMEM)] * 7,
        out_specs=pl.BlockSpec(memory_space=pltpu.VMEM),
        compiler_params=params(10),
        name="norm",
    )(kept, picked, gain, *sums)


def pack_kernel(first_ref, in_ref, *refs):
    out_refs, acc_ref = refs[:-1], refs[-1]
    acc_ref[...] = jnp.zeros_like(acc_ref)
    group = 4

    def body(g, _):
        moved = []
        for k in range(group):
            t = g * group + k
            rows = in_ref[t].astype(f32)
            rows = jnp.where(rows < jnp.inf, rows, 0.0)
            first = first_ref[t]
            base = pl.multiple_of((first // 128) * 128, 128)
            wide = jnp.concatenate([rows, jnp.zeros((PIECE, 128), f32)], axis=1)
            moved.append((base, pltpu.roll(wide, first - base, 1)))
        for base, rows in moved:
            acc_ref[:, pl.ds(base, SLOTS + 128)] += rows
        return 0

    lax.fori_loop(0, 32 // group, body, 0)
    for k, ref in enumerate(out_refs[2:]):
        rows = acc_ref[k * 16 : (k + 1) * 16, :LIVE]
        lane = lax.broadcasted_iota(jnp.int32, (16, 128), 1)
        sums = spread(jnp.sum(rows, axis=1, keepdims=True), lane)
        for into in (ref, out_refs[k // 2].at[pl.ds(k % 2 * 16, 16)]):
            into[:, :LIVE] = rows.astype(bf16)
            into[:, LIVE:] = sums.astype(bf16)


def pack(first, pieces):
    vmem = pl.BlockSpec(memory_space=pltpu.VMEM)
    return pl.pallas_call(
        pack_kernel,
        out_shape=(jax.ShapeDtypeStruct((32, LONG), bf16),) * 2
        + (jax.ShapeDtypeStruct((16, LONG), bf16),) * 4,
        in_specs=[pl.BlockSpec(memory_space=pltpu.SMEM), vmem],
        out_specs=(vmem,) * 6,
        scratch_shapes=[pltpu.VMEM((PIECE, LIVE + SLOTS + 128), f32)],
        compiler_params=params(10),
        name="pack",
    )(first, pieces)


def behind_kernel(in_ref, *refs):
    refs[-1][...] = in_ref[...]


def behind(value, after):
    vmem = pl.BlockSpec(memory_space=pltpu.VMEM)
    return pl.pallas_call(
        behind_kernel,
        out_shape=jax.ShapeDtypeStruct(value.shape, value.dtype),
        in_specs=[vmem] + [pl.BlockSpec(memory_space=pl.ANY)] * len(after),
        out_specs=vmem,
        compiler_params=params(4),
        name="behind",
    )(value, *after)


def gram_kernel(rows_ref, *refs):
    streams, (out_ref, cols_ref) = refs[:4], refs[4:]
    lane = lax.broadcasted_iota(jnp.int32, (16, 128), 1)
    terms = jnp.where(lane < 3, 1.0, 0.0).astype(bf16)
    for x in range(4):
        for z in range(4):
            for s in range(4):
                at = (z if s < 2 else z ^ 2) * PIECE + s * 16
                first = slot_of(s, x, z) * 16
                cols_ref[x % 2, at : at + 16, :] = streams[s][first : first + 16, :]
        inside = slice(x * 256, (x + 1) * 256)
        out_ref[:256, inside] = lax.dot_general(
            rows_ref[:, :LIVE],
            cols_ref[x % 2, :, :LIVE],
            (((1,), (1,)), ((), ())),
            preferred_element_type=f32,
        )
        out_ref[256:, inside] = lax.dot_general(
            terms, cols_ref[x % 2, :, LIVE:], (((1,), (1,)), ((), ())), preferred_element_type=f32
        )[:8]


def gram(rows, streams):
    vmem = pl.BlockSpec(memory_space=pltpu.VMEM)
    return pl.pallas_call(
        gram_kernel,
        out_shape=jax.ShapeDtypeStruct((264, 1024), f32),
        in_specs=[vmem] * 5,
        out_specs=vmem,
        scratch_shapes=[pltpu.VMEM((2, 256, LONG), bf16)],
        compiler_params=params(8),
        cost_estimate=pl.CostEstimate(
            flops=2 * 256 * 1024 * LIVE, bytes_accessed=10 * 1024 * 1024, transcendentals=0
        ),
        name="gram",
    )(rows, *streams)


def finish_kernel(info_ref, part_ref, *refs):
    own_ref, got_ref, mean_ref, out_ref = refs
    core, row_block, col_block = info_ref[0], info_ref[1], info_ref[2]
    part = part_ref[0]

    def put(ref, inside, block):
        at = pl.multiple_of(block * 256, 256)
        mean_ref[:, pl.ds(at, 256)] = ref[256:264, inside][:1] * part

        @pl.when(col_block + block > row_block)
        def _():
            out_ref[:, pl.ds(at, 256)] = ref[:256, inside] * part

        @pl.when(col_block + block == row_block)
        def _():
            row = lax.broadcasted_iota(jnp.int32, (256, 256), 0)
            col = lax.broadcasted_iota(jnp.int32, (256, 256), 1)
            out_ref[:, pl.ds(at, 256)] = jnp.where(row <= col, ref[:256, inside] * part, 0.0)

        @pl.when(col_block + block < row_block)
        def _():
            out_ref[:, pl.ds(at, 256)] = jnp.zeros((256, 256), f32)

    for x in range(4):
        inside = slice(x * 256, (x + 1) * 256)
        put(own_ref, inside, x * 2 + core)
        put(got_ref, inside, x * 2 + 1 - core)


def finish(info, part, own, got):
    vmem = pl.BlockSpec(memory_space=pltpu.VMEM)
    return pl.pallas_call(
        finish_kernel,
        out_shape=(
            jax.ShapeDtypeStruct((1, WIDTH), f32),
            jax.ShapeDtypeStruct((256, WIDTH), f32),
        ),
        in_specs=[pl.BlockSpec(memory_space=pltpu.SMEM)] * 2 + [vmem] * 2,
        out_specs=(vmem,) * 2,
        compiler_params=params(10),
        name="finish",
    )(info, part, own, got)


def swap(value):
    return lax.ppermute(value, "c", [(0, 1), (1, 0)])


def trade(value, axis, flip):
    return lax.ppermute(value, axis, [(i, i ^ flip) for i in range(4)])


def join(*values):
    return jnp.concatenate(values, axis=0)


def meet(value, axis, flip, which):
    got = trade(value, axis, flip)
    return join(jnp.where(which == 0, value, got), jnp.where(which == 0, got, value))


def per_device(resid, norm_gain, keep_index, counts):
    z, x, c, y = (lax.axis_index(a) for a in ("z", "x", "c", "y"))
    kept = jnp.concatenate([keep_index, counts, jnp.zeros((126,), jnp.int32)])[None, :]
    picked, sums = pick(resid, kept)
    all_sums = [sums] + [trade(sums, "y", flip) for flip in (1, 2, 3)]
    pieces = norm(kept, picked, norm_gain[:, None], all_sums)
    pieces = lax.all_to_all(pieces, TOK, 0, 0, tiled=True)

    loads = jnp.sum((pieces[:, 0, :] < jnp.inf).astype(jnp.int32), axis=1)
    first = jnp.cumsum(loads) - loads
    part = 1.0 / jnp.sum(loads).astype(f32)
    *halves, s0, s1, s2, s3 = pack(first, pieces)
    streams = [s0, s1, s2, s3]

    def send(half, turn):
        places = [(q, u) for q in range(4) for u in range(4)]
        return lax.ppermute(half, ("z", "y"), [(q * 4 + u, u * 4 + (q ^ u ^ turn)) for q, u in places])

    for step in range(4):
        for s in range(4):
            axis, flip = PARTNERS[(s + step) % 4]
            seen = [PARTNERS[(s + k) % 4][0] for k in range(step)]
            which = side(x if axis == "x" else z, flip, axis not in seen)
            streams[s] = meet(streams[s], axis, flip, which)
        if step == 0:
            low_t = send(behind(halves[0], streams[:1]), 0)
        if step == 0:
            high_t = send(behind(halves[1], streams), 2)
        if step == 1:
            rows = meet(behind(join(low_t, high_t), streams), "y", 1, side(y ^ z, 1, True))
        if step == 2:
            rows = meet(behind(rows, streams[:1]), "y", 3, side(y ^ z, 3, False))

    got = swap(gram(swap(rows), streams))
    own = gram(rows, streams)
    info = jnp.stack([c, z * 8 + x * 2 + c, y * 8]).astype(jnp.int32)
    mean, gram_factor = finish(info, part[None], own, got)
    return (mean[0], gram_factor)


def solution(mesh):
    fine = Mesh(mesh.devices.reshape(4, 4, 2, 4), ("z", "x", "c", "y"))
    return jax.shard_map(
        per_device,
        mesh=fine,
        in_specs=(P(TOK, "y"), P("y"), P(TOK), P(TOK)),
        out_specs=(P("y"), P(TOK, "y")),
        check_vma=False,
    )
```

```python
import jax
import jax.numpy as jnp
from jax import lax
from jax.experimental import pallas as pl
from jax.experimental.pallas import tpu as pltpu
from jax.sharding import Mesh, PartitionSpec as P

epsilon = 1e-05
TOK = ("z", "x", "c")
SLOTS = 256
LIVE = 4096
WIDTH = 2048
PIECE = 64
LONG = LIVE + 128
MIB = 1024 * 1024
bf16 = jnp.bfloat16
f32 = jnp.float32


def params(mib):
    return pltpu.CompilerParams(vmem_limit_bytes=mib * MIB)


def spread(value, place):
    high = value.astype(bf16).astype(f32)
    middle = (value - high).astype(bf16).astype(f32)
    low = value - high - middle
    rest = jnp.where(place == 2, low, 0.0)
    return jnp.where(place == 0, high, jnp.where(place == 1, middle, rest))


PARTNERS = (("x", 1), ("z", 1), ("x", 3), ("z", 3))


def side(place, flip, first):
    if flip == 1 and not first:
        return (place ^ (place >> 1)) & 1
    return place & 1 if flip == 1 else place >> 1


def slot_of(s, x, z):
    at, seen = 0, []
    for step in range(4):
        axis, flip = PARTNERS[(s + step) % 4]
        at += side(x if axis == "x" else z, flip, axis not in seen) << step
        seen.append(axis)
    return at


def live_slots(kept_ref):
    slot = lax.broadcasted_iota(jnp.int32, (1, SLOTS), 1)
    half = SLOTS // 2
    counts = kept_ref[:, SLOTS : SLOTS + 128]
    return slot < jnp.where(slot < half, counts[:, 0:1], half + counts[:, 1:2])


def pick_kernel(kept_ref, resid_ref, picked_ref, sums_ref):
    tokens = resid_ref.shape[0]
    token = lax.broadcasted_iota(jnp.int32, (tokens, SLOTS), 0)
    kept = jnp.where(live_slots(kept_ref), kept_ref[:, :SLOTS], -1)
    one_hot = jnp.where(token == kept, 1.0, 0.0).astype(bf16)
    total = jnp.zeros((1, SLOTS), f32)
    step = 512
    for k in range(WIDTH // step):
        part = lax.dot_general(
            resid_ref[:, k * step : (k + 1) * step],
            one_hot,
            (((0,), (0,)), ((), ())),
            preferred_element_type=f32,
        )
        total += jnp.sum(part * part, axis=0, keepdims=True)
        picked_ref[k * step : (k + 1) * step, :] = part.astype(bf16)
    sums_ref[...] = jnp.broadcast_to(total, sums_ref.shape)


def pick(resid, kept):
    vmem = pl.BlockSpec(memory_space=pltpu.VMEM)
    return pl.pallas_call(
        pick_kernel,
        out_shape=(
            jax.ShapeDtypeStruct((WIDTH, SLOTS), bf16),
            jax.ShapeDtypeStruct((8, SLOTS), f32),
        ),
        in_specs=[vmem] * 2,
        out_specs=(vmem,) * 2,
        compiler_params=params(16),
        name="pick",
    )(kept, resid)


def norm_kernel(kept_ref, picked_ref, gain_ref, s0, s1, s2, s3, out_ref):
    squares = (s0[:1, :] + s2[:1, :]) + (s1[:1, :] + s3[:1, :])
    scale = lax.rsqrt(squares / 8192 + epsilon)
    row = lax.broadcasted_iota(jnp.int32, (32, 1), 0)
    mark = jnp.where(row == 0, jnp.where(live_slots(kept_ref), 0.0, jnp.inf), 0.0).astype(bf16)
    for x in range(4):
        for c in range(2):
            first = (x * 2 + c) * 256
            rows = picked_ref[first : first + 256, :].astype(f32)
            short = (rows * scale * gain_ref[first : first + 256, :]).astype(bf16)
            for z in range(4):
                low, high = z * PIECE, (z ^ 2) * PIECE + 32
                out_ref[z * 8 + x * 2 + c, :32, :] = short[low : low + 32, :] + mark
                out_ref[z * 8 + x * 2 + c, 32:, :] = short[high : high + 32, :]


def norm(kept, picked, gain, sums):
    return pl.pallas_call(
        norm_kernel,
        out_shape=jax.ShapeDtypeStruct((32, PIECE, SLOTS), bf16),
        in_specs=[pl.BlockSpec(memory_space=pltpu.VMEM)] * 7,
        out_specs=pl.BlockSpec(memory_space=pltpu.VMEM),
        compiler_params=params(10),
        name="norm",
    )(kept, picked, gain, *sums)


def pack_kernel(first_ref, in_ref, *refs):
    out_refs, acc_ref = refs[:-1], refs[-1]
    acc_ref[...] = jnp.zeros_like(acc_ref)
    group = 4

    def body(g, _):
        moved = []
        for k in range(group):
            t = g * group + k
            rows = in_ref[t].astype(f32)
            rows = jnp.where(rows < jnp.inf, rows, 0.0)
            first = first_ref[t]
            base = pl.multiple_of((first // 128) * 128, 128)
            wide = jnp.concatenate([rows, jnp.zeros((PIECE, 128), f32)], axis=1)
            moved.append((base, pltpu.roll(wide, first - base, 1)))
        for base, rows in moved:
            acc_ref[:, pl.ds(base, SLOTS + 128)] += rows
        return 0

    lax.fori_loop(0, 32 // group, body, 0)
    for k, ref in enumerate(out_refs[2:]):
        rows = acc_ref[k * 16 : (k + 1) * 16, :LIVE]
        lane = lax.broadcasted_iota(jnp.int32, (16, 128), 1)
        sums = spread(jnp.sum(rows, axis=1, keepdims=True), lane)
        for into in (ref, out_refs[k // 2].at[pl.ds(k % 2 * 16, 16)]):
            into[:, :LIVE] = rows.astype(bf16)
            into[:, LIVE:] = sums.astype(bf16)


def pack(first, pieces):
    vmem = pl.BlockSpec(memory_space=pltpu.VMEM)
    return pl.pallas_call(
        pack_kernel,
        out_shape=(jax.ShapeDtypeStruct((32, LONG), bf16),) * 2
        + (jax.ShapeDtypeStruct((16, LONG), bf16),) * 4,
        in_specs=[pl.BlockSpec(memory_space=pltpu.SMEM), vmem],
        out_specs=(vmem,) * 6,
        scratch_shapes=[pltpu.VMEM((PIECE, LIVE + SLOTS + 128), f32)],
        compiler_params=params(10),
        name="pack",
    )(first, pieces)


def behind_kernel(in_ref, *refs):
    refs[-1][...] = in_ref[...]


def behind(value, after):
    vmem = pl.BlockSpec(memory_space=pltpu.VMEM)
    return pl.pallas_call(
        behind_kernel,
        out_shape=jax.ShapeDtypeStruct(value.shape, value.dtype),
        in_specs=[vmem] + [pl.BlockSpec(memory_space=pl.ANY)] * len(after),
        out_specs=vmem,
        compiler_params=params(4),
        name="behind",
    )(value, *after)


def gram_kernel(blocks, rows_ref, other_ref, *refs):
    streams, (own_ref, given_ref, cols_ref) = refs[:4], refs[4:]
    lane = lax.broadcasted_iota(jnp.int32, (16, 128), 1)
    terms = jnp.where(lane < 3, 1.0, 0.0).astype(bf16)
    for n, x in enumerate(blocks):
        for z in range(4):
            for s in range(4):
                at = (z if s < 2 else z ^ 2) * PIECE + s * 16
                first = slot_of(s, x, z) * 16
                cols_ref[n * 256 + at : n * 256 + at + 16, :] = streams[s][first : first + 16, :]
        inside = slice(n * 256, (n + 1) * 256)
        for left_ref, into_ref in ((rows_ref, own_ref), (other_ref, given_ref)):
            into_ref[:256, inside] = lax.dot_general(
                left_ref[:, :LIVE],
                cols_ref[inside, :LIVE],
                (((1,), (1,)), ((), ())),
                preferred_element_type=f32,
            )
        sums = lax.dot_general(
            terms, cols_ref[inside, LIVE:], (((1,), (1,)), ((), ())), preferred_element_type=f32
        )
        own_ref[256:, inside] = sums[:8]
        given_ref[256:, inside] = sums[:8]


def gram(blocks, rows, other, streams):
    vmem = pl.BlockSpec(memory_space=pltpu.VMEM)
    width = 256 * len(blocks)
    return pl.pallas_call(
        lambda *refs: gram_kernel(blocks, *refs),
        out_shape=(jax.ShapeDtypeStruct((264, width), f32),) * 2,
        in_specs=[vmem] * 6,
        out_specs=(vmem,) * 2,
        scratch_shapes=[pltpu.VMEM((width, LONG), bf16)],
        compiler_params=params(10),
        cost_estimate=pl.CostEstimate(
            flops=2 * 512 * width * LIVE, bytes_accessed=6 * 1024 * 1024, transcendentals=0
        ),
        name="gram",
    )(rows, other, *streams)


def finish_kernel(info_ref, part_ref, *refs):
    own, got, (mean_ref, out_ref) = refs[:2], refs[2:4], refs[4:]
    core, row_block, col_block = info_ref[0], info_ref[1], info_ref[2]
    part = part_ref[0]

    def put(ref, inside, block):
        at = pl.multiple_of(block * 256, 256)
        mean_ref[:, pl.ds(at, 256)] = ref[256:264, inside][:1] * part

        @pl.when(col_block + block > row_block)
        def _():
            out_ref[:, pl.ds(at, 256)] = ref[:256, inside] * part

        @pl.when(col_block + block == row_block)
        def _():
            row = lax.broadcasted_iota(jnp.int32, (256, 256), 0)
            col = lax.broadcasted_iota(jnp.int32, (256, 256), 1)
            out_ref[:, pl.ds(at, 256)] = jnp.where(row <= col, ref[:256, inside] * part, 0.0)

        @pl.when(col_block + block < row_block)
        def _():
            out_ref[:, pl.ds(at, 256)] = jnp.zeros((256, 256), f32)

    for x in range(4):
        inside = slice(x % 2 * 256, (x % 2 + 1) * 256)
        put(own[x // 2], inside, x * 2 + core)
        put(got[x // 2], inside, x * 2 + 1 - core)


def finish(info, part, own, got):
    vmem = pl.BlockSpec(memory_space=pltpu.VMEM)
    return pl.pallas_call(
        finish_kernel,
        out_shape=(
            jax.ShapeDtypeStruct((1, WIDTH), f32),
            jax.ShapeDtypeStruct((256, WIDTH), f32),
        ),
        in_specs=[pl.BlockSpec(memory_space=pltpu.SMEM)] * 2 + [vmem] * 4,
        out_specs=(vmem,) * 2,
        compiler_params=params(10),
        name="finish",
    )(info, part, *own, *got)


def swap(value):
    return lax.ppermute(value, "c", [(0, 1), (1, 0)])


def trade(value, axis, flip):
    return lax.ppermute(value, axis, [(i, i ^ flip) for i in range(4)])


def join(*values):
    return jnp.concatenate(values, axis=0)


def meet(value, axis, flip, which):
    got = trade(value, axis, flip)
    return join(jnp.where(which == 0, value, got), jnp.where(which == 0, got, value))


def per_device(resid, norm_gain, keep_index, counts):
    z, x, c, y = (lax.axis_index(a) for a in ("z", "x", "c", "y"))
    kept = jnp.concatenate([keep_index, counts, jnp.zeros((126,), jnp.int32)])[None, :]
    picked, sums = pick(resid, kept)
    all_sums = [sums] + [trade(sums, "y", flip) for flip in (1, 2, 3)]
    pieces = norm(kept, picked, norm_gain[:, None], all_sums)
    pieces = lax.all_to_all(pieces, TOK, 0, 0, tiled=True)

    loads = jnp.sum((pieces[:, 0, :] < jnp.inf).astype(jnp.int32), axis=1)
    first = jnp.cumsum(loads) - loads
    part = 1.0 / jnp.sum(loads).astype(f32)
    *halves, s0, s1, s2, s3 = pack(first, pieces)
    streams = [s0, s1, s2, s3]

    def send(half, turn):
        places = [(q, u) for q in range(4) for u in range(4)]
        return lax.ppermute(half, ("z", "y"), [(q * 4 + u, u * 4 + (q ^ u ^ turn)) for q, u in places])

    for step in range(4):
        for s in range(4):
            axis, flip = PARTNERS[(s + step) % 4]
            seen = [PARTNERS[(s + k) % 4][0] for k in range(step)]
            which = side(x if axis == "x" else z, flip, axis not in seen)
            streams[s] = meet(streams[s], axis, flip, which)
        if step == 0:
            low_t = send(behind(halves[0], streams[:1]), 0)
        if step == 0:
            high_t = send(behind(halves[1], streams), 2)
        if step == 1:
            rows = meet(behind(join(low_t, high_t), streams), "y", 1, side(y ^ z, 1, True))
        if step == 2:
            rows = meet(behind(rows, streams[:1]), "y", 3, side(y ^ z, 3, False))

    other = swap(rows)

    own, got = [], []
    for blocks in ((0, 1), (2, 3)):
        kept, given = gram(blocks, rows, other, streams)
        own.append(kept)
        got.append(swap(given))
    info = jnp.stack([c, z * 8 + x * 2 + c, y * 8]).astype(jnp.int32)
    mean, gram_factor = finish(info, part[None], own, got)
    return (mean[0], gram_factor)


def solution(mesh):
    fine = Mesh(mesh.devices.reshape(4, 4, 2, 4), ("z", "x", "c", "y"))
    return jax.shard_map(
        per_device,
        mesh=fine,
        in_specs=(P(TOK, "y"), P("y"), P(TOK), P(TOK)),
        out_specs=(P("y"), P(TOK, "y")),
        check_vma=False,
    )
```
